32 devices in a mesh: section: 2 (over x), dp: 16 (over z, y, core).
Axes of the slice: x: 2, y: 2, z: 4, core: 2. Of those that a mesh axis runs over, the one named last changes fastest.
Arguments:
- stream_in: bfloat16 [48, 150, 410], P('dp'), may hold values from -6 to 6
- memories: bfloat16 [2, 48, 640, 410], P('section', 'dp'), may hold values from -6 to 6
- cotangent: bfloat16 [48, 150, 410], P('dp'), may hold values from -6 to 6
- query_weight: bfloat16 [2, 410, 410], P('section'), may hold values from -0.3125 to 0.3125
- key_value_matrix: bfloat16 [2, 410, 820], P('section'), may hold values from -0.3125 to 0.3125
- position_weight: bfloat16 [2, 410, 410], P('section'), may hold values from -0.4375 to 0.4375
- output_weight: bfloat16 [2, 410, 410], P('section'), may hold values from -3 to 3
- bias_content: bfloat16 [2, 410], P('section'), may hold values from -3 to 3
- bias_position: bfloat16 [2, 410], P('section'), may hold values from -3 to 3
- attend_gain: bfloat16 [2, 410], P('section'), may hold values from 0.5 to 1.5
- attend_bias: bfloat16 [2, 410], P('section'), may hold values from -2 to 2
- inner_weight: bfloat16 [2, 410, 2100], P('section'), may hold values from -0.3125 to 0.3125
- inner_bias: bfloat16 [2, 2100], P('section'), may hold values from -3 to 3
- outer_weight: bfloat16 [2, 2100, 410], P('section'), may hold values from -0.125 to 0.125
- outer_bias: bfloat16 [2, 410], P('section'), may hold values from -3 to 3
- feed_gain: bfloat16 [2, 410], P('section'), may hold values from 0.5 to 1.5
- feed_bias: bfloat16 [2, 410], P('section'), may hold values from -2 to 2
Outputs:
- layer_out: bfloat16 [2, 48, 150, 410], P('section', 'dp')
- input_grad: bfloat16 [2, 48, 150, 410], P('section', 'dp')
- grad_query_weight: float32 [2, 410, 410], P('section')
- grad_key_value_weight: float32 [2, 410, 820], P('section')
- grad_position_weight: float32 [2, 410, 410], P('section')
- grad_output_weight: float32 [2, 410, 410], P('section')
- grad_bias_content: float32 [2, 410], P('section')
- grad_bias_position: float32 [2, 410], P('section')
- grad_attend_gain: float32 [2, 410], P('section')
- grad_attend_bias: float32 [2, 410], P('section')
- grad_inner_weight: float32 [2, 410, 2100], P('section')
- grad_inner_bias: float32 [2, 2100], P('section')
- grad_outer_weight: float32 [2, 2100, 410], P('section')
- outer_bias_gradient: float32 [2, 410], P('section')
- grad_feed_gain: float32 [2, 410], P('section')
- grad_feed_bias: float32 [2, 410], P('section')
The draws below stay inside these ranges and needn't reach their ends.
All inputs are finite; a program needn't handle non-finite values.
Results may differ from the reference program's by a relative error of at most 0.03.
Values may be sent and summed in bfloat16 or wider, within the bound.
No kernel may reach another device: no remote copies, remote signals or barrier semaphores. Data moves between devices by JAX's collectives and lax.ppermute only.
A program may use at most 256 MiB of HBM per device.

```python
import jax
import jax.numpy as jnp
from jax import lax

D = 410
HEADS = 10
FF = 2100
SEG = 150
MEM = 640
HD = 410
KEYS = 790
SEGS_DEV = 3
SEGS = 48


def block_scale(stream_key, shape, cuts, least, high):
    gain = 1.0
    for dim, parts in cuts:
        draws = jax.random.uniform(jax.random.fold_in(jax.random.fold_in(stream_key, 6), dim), (parts,), jnp.float32, least / len(cuts), high / len(cuts))
        gain = gain * jnp.repeat(jnp.exp(draws), shape[dim] // parts).reshape((-1,) + (1,) * (len(shape) - 1 - dim))
    return gain


def centred(stream_key, dims, width, limit, split=(), held_as=jnp.bfloat16):
    values = width * jax.random.normal(stream_key, dims, jnp.float32)
    if split:
        values = values * block_scale(stream_key, dims, split, -0.22, 0.18)
    return jnp.clip(values, -limit, limit).astype(held_as)


def setup_inputs(seed: int = 0) -> dict:
    seeds = jax.random.split(jax.random.key(seed), 18)
    return {
        "stream_in": centred(seeds[0], (SEGS, SEG, D), 1.0, 6.0, ((0, 16),)),
        "memories": centred(seeds[1], (2, SEGS, MEM, D), 1.0, 6.0, ((0, 2), (1, 16))),
        "cotangent": centred(seeds[2], (SEGS, SEG, D), 1.0, 6.0, ((0, 16),)),
        "query_weight": centred(seeds[3], (2, D, HD), D ** -0.5, 0.3125, ((0, 2),)),
        "key_value_matrix": centred(seeds[4], (2, D, 2 * HD), D ** -0.5, 0.3125, ((0, 2),)),
        "position_weight": centred(seeds[5], (2, D, HD), (D // 2) ** -0.5, 0.4375, ((0, 2),)),
        "output_weight": centred(seeds[6], (2, HD, D), (max(1, HD * 8 // KEYS)) ** -0.5, 3.0, ((0, 2),)),
        "bias_content": centred(seeds[7], (2, HD), 0.5, 3.0, ((0, 2),)),
        "bias_position": centred(seeds[8], (2, HD), 0.5, 3.0, ((0, 2),)),
        "attend_gain": jnp.clip(1.0 + 0.1 * jax.random.normal(seeds[9], (2, D), jnp.float32), 0.5, 1.5).astype(jnp.bfloat16),
        "attend_bias": centred(seeds[10], (2, D), 0.3, 2.0, ((0, 2),)),
        "inner_weight": centred(seeds[11], (2, D, FF), D ** -0.5, 0.3125, ((0, 2),)),
        "inner_bias": centred(seeds[12], (2, FF), 0.5, 3.0, ((0, 2),)),
        "outer_weight": centred(seeds[13], (2, FF, D), FF ** -0.5, 0.125, ((0, 2),)),
        "outer_bias": centred(seeds[14], (2, D), 0.5, 3.0, ((0, 2),)),
        "feed_gain": jnp.clip(1.0 + 0.1 * jax.random.normal(seeds[15], (2, D), jnp.float32), 0.5, 1.5).astype(jnp.bfloat16),
        "feed_bias": centred(seeds[16], (2, D), 0.3, 2.0, ((0, 2),)),
    }


@jax.custom_vjp
def low(v):
    return lax.optimization_barrier(v.astype(jnp.bfloat16)).astype(jnp.float32)

@jax.custom_vjp
def low_back(v):
    return v

def low_keep(v):
    return (low(v), None)

def low_pass(kept, grad):
    return (grad,)

def back_keep(v):
    return (v, None)

def back_low(kept, grad):
    return (low(grad),)
low.defvjp(low_keep, low_pass)
low_back.defvjp(back_keep, back_low)
NORM_EPS = 1e-05
GELU_SLOPE = 0.7978845608028654
GELU_CUBIC = 0.044715
MASK_FILL = -1e+30
EXACT = lax.Precision.HIGHEST

def tanh_gelu_approx(values):
    return 0.5 * values * (1.0 + jnp.tanh(GELU_SLOPE * (values + GELU_CUBIC * values * values * values)))

def position_table(key_count, model_width):
    distance = (key_count - 1 - jnp.arange(key_count)).astype(jnp.float32)
    exponent = jnp.arange(0, model_width, 2).astype(jnp.float32) / model_width
    angles = distance[:, None] * (10000.0 ** (-exponent))[None, :]
    return jnp.concatenate([jnp.sin(angles), jnp.cos(angles)], axis=1)

def shift_rows(scores_in):
    leading = scores_in.shape[:-2]
    row_count = scores_in.shape[-2]
    col_count = scores_in.shape[-1]
    padded = jnp.pad(scores_in, [(0, 0)] * len(leading) + [(0, 0), (1, 0)])
    folded = padded.reshape(leading + (col_count + 1, row_count))
    return folded[..., 1:, :].reshape(leading + (row_count, col_count))

def normalize(values, gain_row, shift_row):
    centered = values - lax.optimization_barrier(jnp.mean(values, axis=-1, keepdims=True))
    variance = lax.optimization_barrier(jnp.mean(centered * centered, axis=-1, keepdims=True))
    return centered * lax.rsqrt(variance + NORM_EPS) * gain_row + shift_row

def segment_block(hidden_in, memory, rel_keys, params):
    query_weight, key_value_matrix, output_weight, bias_content, bias_position, attend_gain, attend_bias, inner_weight, inner_bias, outer_weight, outer_bias, feed_gain, feed_bias = params
    groups_count, seg_len, model_width = hidden_in.shape
    mem_len = memory.shape[1]
    key_len = mem_len + seg_len
    proj_width = query_weight.shape[1]
    head_size = proj_width // HEADS
    hidden_in = low_back(hidden_in)
    combined_parts = jnp.concatenate([memory, hidden_in], axis=1)
    query_raw = low_back(jnp.einsum('gld,de->gle', hidden_in, query_weight, precision=EXACT))
    query_content = low(query_raw + bias_content).reshape(groups_count, seg_len, HEADS, head_size)
    query_position = low(query_raw + bias_position).reshape(groups_count, seg_len, HEADS, head_size)
    key_value = jnp.einsum('gkd,de->gke', combined_parts, key_value_matrix, precision=EXACT)
    key_heads = low(low_back(key_value[..., :proj_width])).reshape(groups_count, key_len, HEADS, head_size)
    value_heads = low(low_back(key_value[..., proj_width:])).reshape(groups_count, key_len, HEADS, head_size)
    content = jnp.einsum('glhe,gkhe->ghlk', query_content, key_heads, precision=EXACT)
    position = jnp.einsum('glhe,khe->ghlk', query_position, rel_keys, precision=EXACT)
    raw_scores = low_back(content + shift_rows(position))
    allowed = jnp.arange(key_len)[None, :] <= jnp.arange(seg_len)[:, None] + mem_len
    scores = jnp.where(allowed, raw_scores * head_size ** (-0.5), MASK_FILL)
    largest = lax.optimization_barrier(jnp.max(scores, axis=-1, keepdims=True))
    exponent_terms = jnp.exp(scores - largest)
    attention_map = exponent_terms / lax.optimization_barrier(jnp.sum(exponent_terms, axis=-1, keepdims=True))
    mixed = jnp.einsum('ghlk,gkhe->glhe', low(attention_map), value_heads, precision=EXACT)
    mixed = low(low_back(mixed.reshape(groups_count, seg_len, proj_width)))
    attend_out = low_back(jnp.einsum('gle,ed->gld', mixed, output_weight, precision=EXACT))
    middle = low(normalize(hidden_in + attend_out, attend_gain, attend_bias))
    pre_active = low_back(jnp.einsum('gld,df->glf', middle, inner_weight, precision=EXACT) + inner_bias)
    active = low(tanh_gelu_approx(pre_active))
    feed_out = low_back(jnp.einsum('glf,fd->gld', active, outer_weight, precision=EXACT) + outer_bias)
    return low(normalize(middle + feed_out, feed_gain, feed_bias))

def run_layer(hidden_in, memory, params, position_weight, sinusoid):
    rel_keys = low(low_back(jnp.dot(sinusoid, position_weight, precision=EXACT)))
    rel_keys = rel_keys.reshape(sinusoid.shape[0], HEADS, rel_keys.shape[1] // HEADS)
    checked_block = jax.checkpoint(segment_block)
    group_total = hidden_in.shape[0] // SEGS_DEV
    hidden_groups = hidden_in.reshape((group_total, SEGS_DEV) + hidden_in.shape[1:])
    memory_groups = memory.reshape((group_total, SEGS_DEV) + memory.shape[1:])

    def scan_step(carried, pieces):
        return (carried, checked_block(pieces[0], pieces[1], rel_keys, params))
    carried, outputs = lax.scan(scan_step, jnp.zeros((), jnp.float32), (hidden_groups, memory_groups))
    return outputs.reshape(hidden_in.shape)

def reference(stream_in, memories, cotangent, query_weight, key_value_matrix, position_weight, output_weight, bias_content, bias_position, attend_gain, attend_bias, inner_weight, inner_bias, outer_weight, outer_bias, feed_gain, feed_bias):
    stacked = tuple((member.astype(jnp.float32) for member in (query_weight, key_value_matrix, position_weight, output_weight, bias_content, bias_position, attend_gain, attend_bias, inner_weight, inner_bias, outer_weight, outer_bias, feed_gain, feed_bias)))
    stream = stream_in.astype(jnp.float32)
    memory_all = memories.astype(jnp.float32)
    sinusoid = low(position_table(KEYS, D))
    junction = jnp.zeros(stream.shape, jnp.float32)

    def layer_of(hidden_in, memory, params):
        return run_layer(hidden_in, memory, params[:2] + params[3:], params[2], sinusoid)

    def forward(stream, junction, stacked):
        first_out = layer_of(stream, memory_all[0], tuple((member[0] for member in stacked)))
        second_out = layer_of(first_out + junction, memory_all[1], tuple((member[1] for member in stacked)))
        return (first_out, second_out)
    (first_out, second_out), pullback = jax.vjp(forward, stream, junction, stacked)
    back_stream, back_junction, back_weights = pullback((jnp.zeros_like(first_out), cotangent.astype(jnp.float32)))
    layer_out = jnp.stack([first_out, second_out]).astype(jnp.bfloat16)
    input_grad = jnp.stack([back_stream, back_junction]).astype(jnp.bfloat16)
    return (layer_out, input_grad, back_weights[0], back_weights[1], back_weights[2], back_weights[3], back_weights[4], back_weights[5], back_weights[6], back_weights[7], back_weights[8], back_weights[9], back_weights[10], back_weights[11], back_weights[12], back_weights[13])
```

```python
from functools import partial
from typing import Any, NamedTuple

import jax
import jax.numpy as jnp
import numpy as np
from jax import lax
from jax.experimental import pallas as pl
from jax.experimental.pallas import tpu as pltpu
from jax.sharding import PartitionSpec as P

HEADS = 10
HALVES = 2
GROUP = HEADS // HALVES
LANES = 128
UNIT = 32
NORM_EPS = 1e-05
GELU_SLOPE = 0.7978845608028654
GELU_CUBIC = 0.044715
MASK_FILL = -1e30
LOG2_E = 1.4426950408889634
F32 = jnp.float32
BF16 = jnp.bfloat16
VMEM_BYTES = 60 * 1024 * 1024


def round_up(value, unit):
    return -(-value // unit) * unit


class Sizes:
    def __init__(self, seg_len, mem_len, model, proj, hidden):
        self.seg, self.mem, self.model, self.proj, self.hidden = seg_len, mem_len, model, proj, hidden
        self.keys = mem_len + seg_len
        self.head = proj // HEADS
        self.rows = round_up(seg_len, 16)
        self.body = seg_len // 16 * 16
        self.tail = self.body + 8
        self.used = GROUP * self.head
        self.width = round_up(self.used, 256)
        self.cols = round_up(self.keys, LANES)
        self.recent = self.cols - mem_len
        self.stack = round_up(GROUP * self.tail, 256)
        self.tail_at = GROUP * self.body
        self.tail_rows = self.stack - self.tail_at
        self.tiles = self.cols // LANES
        self.shift = round_up(seg_len - 1, 8)
        self.scale = self.head ** (-0.5)
        assert self.seg - self.body <= 8 and self.tail_rows % 16 == 0
        assert self.shift == self.tail and self.mem % LANES == 0 and self.shift <= LANES * 2


class Weights(NamedTuple):
    query: Any
    key_value: Any
    output: Any
    rel: Any
    inner: Any
    outer: Any
    lines: Any


class Line:
    bias_content, bias_position = 0, HALVES
    attend_gain, attend_bias, inner_bias, outer_bias, feed_gain, feed_bias = range(
        2 * HALVES, 2 * HALVES + 6
    )
    count = 16


class Kept(NamedTuple):
    attention: Any
    content_stack: Any
    position_stack: Any
    keys: Any
    values: Any
    mixed: Any


class KeptFeed(NamedTuple):
    first_normed: Any
    first_inverse: Any
    second_normed: Any
    second_inverse: Any
    slope: Any


class Fed(NamedTuple):
    mixed_low: Any
    middle: Any
    active: Any


class BackFeed(NamedTuple):
    pre: Any
    outer: Any
    attend: Any
    sums: Any


class BackAttend(NamedTuple):
    query: Any
    key_value: Any
    rel: Any
    sums: Any


def layouts(z):
    halves = lambda rows, cols, kind: ((HALVES, rows, cols), kind)
    kept = Kept(
        halves(z.stack, z.cols, BF16),
        halves(z.stack, z.width, BF16),
        halves(z.stack, z.width, BF16),
        halves(z.width, z.cols, BF16),
        halves(z.width, z.cols, BF16),
        halves(z.rows, z.width, F32),
    )
    wide, narrow = ((z.rows, z.model), F32), ((z.rows, 1), F32)
    kept_feed = KeptFeed(wide, narrow, wide, narrow, ((z.rows, z.hidden), BF16))
    low = ((z.rows, z.model), BF16)
    fed = Fed(halves(z.rows, z.width, BF16), low, ((z.rows, z.hidden), BF16))
    back_feed = BackFeed(((z.rows, z.hidden), BF16), low, low, ((8, z.model), F32))
    back_attend = BackAttend(
        halves(z.rows, z.width, BF16),
        ((2 * HALVES, z.width, z.cols), BF16),
        halves(z.width, z.cols, BF16),
        halves(8, z.width, F32),
    )
    return kept, kept_feed, fed, back_feed, back_attend


def dot(left, right):
    return lax.dot_general(left, right, (((1,), (0,)), ((), ())), preferred_element_type=F32)


def dot_nt(left, right):
    return lax.dot_general(left, right, (((1,), (1,)), ((), ())), preferred_element_type=F32)


def dot_tn(left, right):
    return lax.dot_general(left, right, (((0,), (0,)), ((), ())), preferred_element_type=F32)


def iota(shape, dim):
    return lax.broadcasted_iota(jnp.int32, shape, dim)


class Item:
    def __init__(self, ref, copy=None, once=None):
        self.ref, self.copy, self.once = ref, copy, once

    def __call__(self):
        if self.copy is not None:
            self.once(self.copy.wait)
            self.copy = None
        return self.ref


class Out:
    def __init__(self, ref, target, sems):
        self.ref, self.target, self.sems = ref, target, sems
        self.copies = []

    def part(self, index, slot):
        copy = pltpu.make_async_copy(self.ref.at[index], self.target.at[index], self.sems.at[slot])
        copy.start()
        return copy

    def send(self):
        copy = pltpu.make_async_copy(self.ref, self.target, self.sems.at[0])
        copy.start()
        self.copies.append(copy)


def kernel_call(name, body, direct, fetched, made, scratch, count=1, flops=0):
    made = list(made)
    parts = 4
    slots = jnp.stack([jnp.int32(0 if slot is None else slot) for _, slot in fetched])

    def kernel(slots, *refs):
        refs = list(refs)

        def take(number):
            taken = refs[:number]
            del refs[:number]
            return taken

        ins, sources, targets = take(len(direct)), take(len(fetched)), take(len(made))
        landed, built = take(len(fetched)), take(len(made))
        in_sems, out_sems = take(2)
        first = pl.program_id(0) == 0
        once = (lambda act: act()) if count == 1 else (lambda act: pl.when(first)(act))
        items = []
        for k, (ref, (_, slot)) in enumerate(zip(sources, fetched)):
            source = ref if slot is None else ref.at[slots[k]]
            copy = pltpu.make_async_copy(source, landed[k], in_sems.at[k])
            once(copy.start)
            items.append(Item(landed[k], copy, once))
        outs = [
            Out(ref, target.at[pl.program_id(0)], out_sems.at[k])
            for k, (ref, target) in enumerate(zip(built, targets))
        ]
        body(ins, items, outs, *refs)
        for item in items:
            item()
        for out in outs:
            for copy in out.copies:
                copy.wait()

    landing = [
        pltpu.VMEM(array.shape if slot is None else array.shape[1:], array.dtype)
        for array, slot in fetched
    ]
    results = pl.pallas_call(
        kernel,
        grid=(count,),
        in_specs=[pl.BlockSpec(memory_space=pltpu.SMEM)]
        + [spec for _, spec in direct]
        + [pl.BlockSpec(memory_space=pl.ANY)] * len(fetched),
        out_specs=[pl.BlockSpec(memory_space=pl.ANY)] * len(made),
        out_shape=[jax.ShapeDtypeStruct((count,) + tuple(s), t) for s, t in made],
        scratch_shapes=landing
        + [pltpu.VMEM(s, t) for s, t in made]
        + [
            pltpu.SemaphoreType.DMA((max(len(fetched), 1),)),
            pltpu.SemaphoreType.DMA((max(len(made), 1), parts)),
        ]
        + scratch,
        compiler_params=pltpu.CompilerParams(vmem_limit_bytes=VMEM_BYTES),
        cost_estimate=pl.CostEstimate(flops=flops, bytes_accessed=1 << 23, transcendentals=0),
        name=name,
    )(slots, *[array for array, _ in direct], *[array for array, _ in fetched])
    return list(results)


def whole(array):
    zeros = (0,) * array.ndim
    return (array, pl.BlockSpec(array.shape, lambda i: zeros, pipeline_mode=pl.Buffered(1)))


def segment(array, slot):
    zeros = (0,) * (array.ndim - 1)
    return (array, pl.BlockSpec((None,) + array.shape[1:], lambda i: (i + slot,) + zeros))


def head_lanes(z, rows, head):
    lane = iota((rows, z.width), 1)
    return (lane >= z.head * head) & (lane < z.head * (head + 1))


def stack_heads(z, target, source):
    tails = []
    for head in range(GROUP):
        own = jnp.where(head_lanes(z, z.tail, head), source[: z.tail], 0.0)
        target[z.body * head : z.body * (head + 1), :] = own[: z.body].astype(BF16)
        tails.append(own[z.body :])
    tails.append(jnp.zeros((z.tail_rows - 8 * GROUP, z.width), F32))
    target[z.tail_at :, :] = jnp.concatenate(tails, axis=0).astype(BF16)


def unstack_heads(z, source):
    total = None
    for head in range(GROUP):
        rows = jnp.concatenate(
            [
                source[z.body * head : z.body * (head + 1)],
                source[z.tail_at + 8 * head : z.tail_at + 8 * (head + 1)],
            ],
            axis=0,
        )
        own = jnp.where(head_lanes(z, z.tail, head), rows, 0.0)
        total = own if total is None else total + own
    return total


def normalize(values):
    centered = values - jnp.mean(values, axis=-1, keepdims=True)
    variance = jnp.mean(centered * centered, axis=-1, keepdims=True)
    inverse = lax.rsqrt(variance + NORM_EPS)
    return (centered * inverse, inverse)


def normalize_back(grad_normed, normed, inverse):
    return inverse * (
        grad_normed
        - jnp.mean(grad_normed, axis=-1, keepdims=True)
        - normed * jnp.mean(grad_normed * normed, axis=-1, keepdims=True)
    )


def shifted_tiles(z, tiles, first_row):
    base = (first_row - z.shift) % LANES
    turns = (first_row - z.shift - base) // LANES
    lane, row = iota((8, LANES), 1), iota((8, LANES), 0)
    turned = [pltpu.roll(tile, base, 1, stride=1, stride_axis=0) for tile in tiles]
    kept = lane >= base + row
    return [
        jnp.where(kept, turned[(t - turns) % z.tiles], turned[(t - turns - 1) % z.tiles])
        for t in range(z.tiles)
    ]


def restored_tiles(z, tiles, first_row):
    lane, row = iota((8, LANES), 1), iota((8, LANES), 0)
    amount = z.shift - first_row
    place = (lane - amount + row) % LANES
    turned = [jnp.take_along_axis(tile, place, axis=1) for tile in tiles]
    base, turns = amount % LANES, amount // LANES
    if base >= 8:
        kept, other = lane >= base - row, -1
    else:
        assert base == 0
        kept, other = lane < LANES - row, 1
    return [
        jnp.where(kept, turned[(t - turns) % z.tiles], turned[(t - turns + other) % z.tiles])
        for t in range(z.tiles)
    ]


def split_tiles(z, block):
    return [block[:, LANES * t : LANES * (t + 1)] for t in range(z.tiles)]


def over_rows(z, chunk):
    for head in range(GROUP):
        for part in range(z.body // 16):
            chunk(head * z.body + 16 * part, 16 * part, 16 * part + 8)
    for part in range(z.tail_rows // 16):
        chunk(z.tail_at + 16 * part, z.body, z.body)


def attention_rows(z, content, position, attention):
    def chunk(row, first, second):
        for at, query in ((row, first), (row + 8, second)):
            rows = slice(at, at + 8)
            moved = shifted_tiles(z, split_tiles(z, position[rows, :]), query)
            for t in range(z.tiles):
                lanes = slice(LANES * t, LANES * (t + 1))
                scores = content[rows, lanes] + moved[t]
                if t >= z.mem // LANES:
                    ahead = iota((8, LANES), 1) - iota((8, LANES), 0)
                    allowed = ahead <= z.mem + query - LANES * t
                    scores = jnp.where(allowed, scores, MASK_FILL)
                content[rows, lanes] = scores

    over_rows(z, chunk)
    scores = content[...]
    largest = jnp.max(scores, axis=-1, keepdims=True)
    powers = jnp.exp2((scores - largest) * (z.scale * LOG2_E))
    inverse = 1.0 / jnp.sum(powers, axis=-1, keepdims=True)
    attention[...] = (powers * inverse).astype(BF16)


def attention_rows_back(z, attention, back_map, weighted, back_raw, back_table):
    def chunk(row, first, second):
        rows = slice(row, row + 16)
        inner = weighted[rows, :]
        tops, lows = [], []
        for t in range(z.tiles):
            lanes = slice(LANES * t, LANES * (t + 1))
            raw = attention[rows, lanes].astype(F32) * ((back_map[rows, lanes] - inner) * z.scale)
            back_raw[rows, lanes] = raw.astype(BF16)
            tops.append(raw[:8])
            lows.append(raw[8:])
        tops, lows = restored_tiles(z, tops, first), restored_tiles(z, lows, second)
        for t in range(z.tiles):
            pair = jnp.concatenate([tops[t], lows[t]], axis=0).astype(BF16)
            back_table[rows, LANES * t : LANES * (t + 1)] = pair

    over_rows(z, chunk)


def gelu_and_slope(values):
    squared = values * values
    tangent = jnp.tanh(GELU_SLOPE * (values + GELU_CUBIC * squared * values))
    half = 0.5 * (1.0 + tangent)
    slope = half + 0.5 * values * (1.0 - tangent * tangent) * GELU_SLOPE * (
        1.0 + 3.0 * GELU_CUBIC * squared
    )
    return (values * half, slope)


def forward_body(
    z, w, source, memory, kept, kept_feed, fed, result, hidden, content, position, attention_done
):
    hidden[...] = jnp.zeros(hidden.shape, BF16)
    hidden[: z.seg, :] = source[...]
    for j in range(2 * HALVES):
        target = (kept.keys if j < HALVES else kept.values).at[j % HALVES]
        target[:, : z.mem] = dot(w.key_value()[j], memory[...]).astype(BF16)
        target[:, z.mem :] = dot_nt(w.key_value()[j], hidden[...]).astype(BF16)
    rows_in = hidden[: z.rows, :]
    real = iota((z.rows, 1), 0) < z.seg
    lines = w.lines()
    line = lambda number: lines[number : number + 1, : z.model]
    for half in range(HALVES):
        raw = dot(rows_in, w.query()[half])
        for stack, number in (
            (kept.content_stack, Line.bias_content), (kept.position_stack, Line.bias_position)
        ):
            bias = lines[number + half : number + half + 1, : z.width]
            stack_heads(z, stack.at[half], jnp.where(real, raw + bias, 0.0))
    rel = w.rel()

    def one_half(half, carry):
        content[...] = dot(kept.content_stack[half], kept.keys[half])
        position[...] = dot(kept.position_stack[half], rel[half])
        attention_rows(z, content, position, kept.attention.at[half])
        mixed = unstack_heads(z, dot_nt(kept.attention[half], kept.values[half]))
        kept.mixed[half, : z.tail, :] = mixed
        kept.mixed[half, z.tail :, :] = jnp.zeros((z.rows - z.tail, z.width), F32)
        return carry

    lax.fori_loop(0, HALVES, one_half, 0)
    attention_done()
    total = rows_in.astype(F32)
    for half in range(HALVES):
        mixed = kept.mixed[half].astype(BF16)
        fed.mixed_low[half] = mixed
        total = total + dot(mixed, w.output()[half])
    normed, inverse = normalize(total)
    kept_feed.first_normed[...] = normed
    kept_feed.first_inverse[...] = inverse
    middle = (normed * line(Line.attend_gain) + line(Line.attend_bias)).astype(BF16)
    fed.middle[...] = middle
    active, slope = gelu_and_slope(
        dot(middle, w.inner()[...]) + lines[Line.inner_bias : Line.inner_bias + 1, :]
    )
    kept_feed.slope[...] = slope.astype(BF16)
    active = active.astype(BF16)
    fed.active[...] = active
    feed = dot_nt(active, w.outer()[...]) + line(Line.outer_bias)
    normed, inverse = normalize(middle.astype(F32) + feed)
    kept_feed.second_normed[...] = normed
    kept_feed.second_inverse[...] = inverse
    out = (normed * line(Line.feed_gain) + line(Line.feed_bias)).astype(BF16)
    result[...] = out[: z.seg]


def feed_back_body(z, w, grad_in, kept, back, back_first, top):
    top[...] = jnp.zeros(top.shape, BF16)
    top[: z.seg, :] = grad_in[...]
    grad_top = top[...].astype(F32)
    lines = w.lines()
    line = lambda number: lines[number : number + 1, : z.model]
    normed = kept.second_normed()[...]
    second = normalize_back(
        grad_top * line(Line.feed_gain), normed, kept.second_inverse()[...]
    )
    outer = second.astype(BF16)
    back.outer[...] = outer
    pre = (dot(outer, w.outer()[...]) * kept.slope()[...].astype(F32)).astype(BF16)
    back.pre[...] = pre
    middle = second + dot_nt(pre, w.inner()[...])
    first_normed = kept.first_normed()[...]
    first = normalize_back(
        middle * line(Line.attend_gain), first_normed, kept.first_inverse()[...]
    )
    back_first[...] = first
    back.attend[...] = first.astype(BF16)
    sums = back.sums
    sums[...] = jnp.zeros(sums.shape, F32)
    rows = (middle * first_normed, middle, outer.astype(F32), grad_top * normed, grad_top)
    for k, values in enumerate(rows):
        sums[k : k + 1, :] = jnp.sum(values, axis=0, keepdims=True)


def attend_back_body(
    z, w, kept, back_first, back_attend, back, send, input_grad, stack, back_map, weighted, raw, table
):
    refs = Kept(*[item() for item in kept])
    output, rel = w.output(), w.rel()

    def one_half(half, carry):
        own = dot_nt(back_attend[...], output[half]).astype(BF16).astype(F32)
        stack_heads(z, stack, own)
        product = own[: z.tail] * refs.mixed[half, : z.tail, :]
        weighted[z.tail_at :, :] = jnp.zeros((z.tail_rows, 1), F32)
        for head in range(GROUP):
            inner = jnp.where(head_lanes(z, z.tail, head), product, 0.0)
            inner = jnp.sum(inner, axis=1, keepdims=True)
            weighted[z.body * head : z.body * (head + 1), :] = inner[: z.body]
            at = z.tail_at + 8 * head
            weighted[at : at + 8, :] = inner[z.body :]
        back_map[...] = dot(stack[...], refs.values[half])
        attention_rows_back(z, refs.attention.at[half], back_map, weighted, raw, table)
        back.key_value[half] = dot_tn(refs.content_stack[half], raw[...]).astype(BF16)
        back.key_value[HALVES + half] = dot_tn(stack[...], refs.attention[half]).astype(BF16)
        back.rel[half] = dot_tn(refs.position_stack[half], table[...]).astype(BF16)
        send(half)
        from_content = unstack_heads(z, dot_nt(raw[...], refs.keys[half]))
        from_position = unstack_heads(z, dot_nt(table[...], rel[half]))
        back.query[half, : z.tail, :] = (from_content + from_position).astype(BF16)
        back.query[half, z.tail :, :] = jnp.zeros((z.rows - z.tail, z.width), BF16)
        back.sums[half] = jnp.concatenate(
            [
                jnp.sum(from_content, axis=0, keepdims=True),
                jnp.sum(from_position, axis=0, keepdims=True),
                jnp.zeros((6, z.width), F32),
            ],
            axis=0,
        )
        return carry

    lax.fori_loop(0, HALVES, one_half, 0)
    total = back_first[...]
    for half in range(HALVES):
        total = total + dot_nt(back.query[half], w.query()[half])
    for j in range(2 * HALVES):
        recent = dot_tn(back.key_value[j, :, z.mem :], w.key_value()[j])
        total = total + recent[: z.rows]
    input_grad[...] = total[: z.seg].astype(BF16)


def back_scratch(z):
    return [
        pltpu.VMEM((z.stack, z.width), BF16),
        pltpu.VMEM((z.stack, z.cols), F32),
        pltpu.VMEM((z.stack, 1), F32),
        pltpu.VMEM((z.stack, z.cols), BF16),
        pltpu.VMEM((z.stack, z.cols), BF16),
    ]


def vmem(entries):
    return [pltpu.VMEM(s, t) for s, t in entries]


def tally(z, passes):
    return int(passes * 2e10)


ARRIVAL = (1, 6, 0, 3, 2, 4, 5)


def arriving(weights):
    return [(weights[k], None) for k in ARRIVAL]


def arrived_weights(items):
    own = dict(zip(ARRIVAL, items))
    return Weights(*[own[k] for k in range(len(ARRIVAL))])


def refs_of(kind, outs):
    return kind(*[out.ref for out in outs])


def send_all(outs):
    for out in outs:
        out.send()


def attend_sender(outs):
    query, key_value, rel, sums = outs

    def parts(half):
        yield key_value, half, half
        yield key_value, HALVES + half, HALVES + half
        yield rel, half, half

    def send(half):
        for out, index, slot in parts(half):
            out.part(index, slot)

    def finish():
        for half in range(HALVES):
            for out, index, slot in parts(half):
                pltpu.make_async_copy(
                    out.ref.at[index], out.target.at[index], out.sems.at[slot]
                ).wait()

    return send, finish


@partial(jax.jit, static_argnums=(0, 4, 5))
def forward_call(z, weights, source, memory, slot, count):
    kept, kept_feed, fed = layouts(z)[:3]
    direct = [segment(source, slot), segment(memory, slot)]

    def body(ins, items, outs, hidden, content, position):
        result, outs = outs[0], outs[1:]
        forward_body(
            z, arrived_weights(items), ins[0], ins[1], refs_of(Kept, outs[:6]),
            refs_of(KeptFeed, outs[6:11]), refs_of(Fed, outs[11:]), result.ref, hidden, content,
            position, lambda: send_all(outs[:6]),
        )
        send_all([result] + outs[6:])

    made = [((z.seg, z.model), BF16), *kept, *kept_feed, *fed]
    results = kernel_call(
        "forward", body, direct, arriving(weights), made,
        [
            pltpu.VMEM((z.recent, z.model), BF16),
            pltpu.VMEM((z.stack, z.cols), F32),
            pltpu.VMEM((z.stack, z.cols), F32),
        ],
        count, tally(z, count),
    )
    return results[0], Kept(*results[1:7]), KeptFeed(*results[7:12]), Fed(*results[12:])


@partial(jax.jit, static_argnums=0)
def both_call(z, weights, source, source_slot, memory, grad_in, slot):
    kept, kept_feed, fed, back_feed, back_attend = layouts(z)
    fetched = [(source, source_slot), (memory, slot)] + arriving(weights) + [(grad_in, slot)]

    def body(ins, items, outs, hidden, content, position, *scratch):
        w = arrived_weights(items[2:-1])
        result, input_grad = outs[:2]
        fed_outs, feed_outs, attend_outs = outs[2:5], outs[5:9], outs[9:13]
        held, held_feed = Kept(*scratch[:6]), KeptFeed(*scratch[6:11])
        first, top, stack, weighted, raw, table = scratch[11:]
        forward_body(
            z, w, items[0](), items[1](), held, held_feed, refs_of(Fed, fed_outs), result.ref,
            hidden, content, position, lambda: None,
        )
        send_all([result] + fed_outs)
        feed_refs = refs_of(BackFeed, feed_outs)
        feed_back_body(
            z, w, items[-1](), KeptFeed(*[Item(ref) for ref in held_feed]), feed_refs, first, top
        )
        send_all(feed_outs)
        send, finish = attend_sender(attend_outs)
        attend_back_body(
            z, w, Kept(*[Item(ref) for ref in held]), first, feed_refs.attend,
            refs_of(BackAttend, attend_outs), send, input_grad.ref, stack, content, weighted,
            raw, table,
        )
        send_all([input_grad, attend_outs[0], attend_outs[3]])
        finish()

    row = ((z.seg, z.model), BF16)
    scratch = back_scratch(z)
    del scratch[1]
    results = kernel_call(
        "forward_backward", body, [], fetched, [row, row, *fed, *back_feed, *back_attend],
        [
            pltpu.VMEM((z.recent, z.model), BF16),
            pltpu.VMEM((z.stack, z.cols), F32),
            pltpu.VMEM((z.stack, z.cols), F32),
        ]
        + vmem(kept)
        + vmem(kept_feed)
        + [pltpu.VMEM((z.rows, z.model), F32), pltpu.VMEM((z.rows, z.model), BF16)]
        + scratch,
        1, tally(z, 2),
    )
    return (
        results[0], results[1], Fed(*results[2:5]), BackFeed(*results[5:9]),
        BackAttend(*results[9:13]),
    )


@partial(jax.jit, static_argnums=0)
def feed_back_call(z, weights, grad_in, kept, slot):
    back_feed = layouts(z)[3]
    fetched = [(weights.lines, None)]
    fetched += [(a, slot) for a in (kept.second_normed, kept.second_inverse)]
    fetched += [(weights.outer, None), (kept.slope, slot), (weights.inner, None)]
    fetched += [(a, slot) for a in (kept.first_normed, kept.first_inverse)]

    def body(ins, items, outs, top):
        lines, second_normed, second_inverse, outer, slope, inner, first_normed, first_inverse = items
        w = Weights(*[None] * 4, inner, outer, lines)
        held = KeptFeed(first_normed, first_inverse, second_normed, second_inverse, slope)
        feed_back_body(z, w, ins[0], held, refs_of(BackFeed, outs[1:]), outs[0].ref, top)
        send_all(outs)

    results = kernel_call(
        "feed_backward", body, [segment(grad_in, 0)], fetched,
        [((z.rows, z.model), F32), *back_feed], [pltpu.VMEM((z.rows, z.model), BF16)],
        1, tally(z, 0.3),
    )
    return results[0], BackFeed(*results[1:])


@partial(jax.jit, static_argnums=0)
def attend_back_call(z, weights, back_first, back_attend, kept, slot):
    fetched = [(back_first, 0), (back_attend, 0), (weights.output, None)]
    fetched += [(array, slot) for array in kept]
    fetched += [(a, None) for a in (weights.rel, weights.query, weights.key_value)]

    def body(ins, items, outs, *scratch):
        first, attend, output = items[:3]
        rel, query, key_value = items[9:]
        w = Weights(query, key_value, output, rel, *[None] * 3)
        send, finish = attend_sender(outs[1:])
        attend_back_body(
            z, w, Kept(*items[3:9]), first(), attend(), refs_of(BackAttend, outs[1:]), send,
            outs[0].ref, *scratch,
        )
        send_all([outs[0], outs[1], outs[4]])
        finish()

    results = kernel_call(
        "attend_backward", body, [], fetched, [((z.seg, z.model), BF16), *layouts(z)[4]],
        back_scratch(z), 1, tally(z, 0.7),
    )
    return results[0], BackAttend(*results[1:])


class Part:
    def __init__(self, z, widths, extra, devices):
        self.rows = round_up(z.model, UNIT)
        self.per_tile = self.rows // UNIT
        self.first, at = [], 0
        for width in widths:
            self.first.append(at)
            at += round_up(width, LANES) // LANES
        self.extra_at = at * self.per_tile
        self.used = self.extra_at + extra
        bits = devices.bit_length() - 1
        assert devices == 1 << bits and bits >= 3
        order = list(range(1, bits))
        self.orders = (order, [order[1], order[0]] + order[2:])
        self.pieces = devices // 2
        per_piece = -(-self.used // devices)
        self.sizes = (-(-per_piece // 2), per_piece // 2)
        self.starts = (0, self.pieces * self.sizes[0])
        self.half = self.pieces * per_piece
        self.units = 2 * self.half

    def paths(self):
        return list(zip(self.orders, self.sizes, self.starts))

    def ports(self):
        return [self.pieces // 2 * size for size in self.sizes for _ in range(2)]


def rearranged(index, order):
    total = 0
    for place, bit in enumerate(reversed(order)):
        total = total + (((index >> bit) & 1) << place)
    return total


def exchanged(array, bit):
    count = lax.axis_size("dp")
    return lax.ppermute(array, "dp", [(i, i ^ (1 << bit)) for i in range(count)])


class Chain:
    def __init__(self, order, mine, came):
        self.order, self.reduced, self.spread = order, 1, len(order) - 1
        self.keep = mine[0] + came[0]
        self.flying = exchanged(mine[1] + came[1], order[0])

    def order_after(self, other):
        self.flying, other.keep = lax.optimization_barrier((self.flying, other.keep))

    def advance(self):
        came, keep = self.flying, self.keep
        if self.reduced < len(self.order):
            half = keep.shape[0] // 2
            self.keep = keep[:half] + came[:half]
            self.flying = exchanged(keep[half:] + came[half:], self.order[self.reduced])
            self.reduced += 1
            return
        if self.spread == len(self.order) - 1:
            self.keep = keep + came
        else:
            self.keep = jnp.concatenate([keep, came], axis=0)
        self.flying = exchanged(self.keep, self.order[self.spread])
        self.spread -= 1


def swapped_cores(arrays):
    return [exchanged(array, 0) for array in arrays]


def chains_of(part, mine, came):
    return [
        Chain(order, mine[2 * k : 2 * k + 2], came[2 * k : 2 * k + 2])
        for k, order in enumerate(part.orders)
    ]


def step_all(chains, last):
    for chain in chains:
        chain.order_after(last)
        chain.advance()
        last = chain
    return last


def finished(chains):
    own = sum([[chain.keep, chain.flying] for chain in chains], [])
    return own + swapped_cores(own)


def piece_places(part, device, core):
    places = []
    for rel_core in range(2):
        base = (core ^ rel_core) * part.half
        for k, (order, size, start) in enumerate(part.paths()):
            own = rearranged(device, order)
            for piece in range(part.pieces):
                number = rel_core * 2 * len(part.orders) + 2 * k + piece // (part.pieces // 2)
                within = piece % (part.pieces // 2) * size
                places.append((number, within, base + start + (piece ^ own) * size, size))
    return places


def put_block(part, packed, number, value, tile=0):
    for t in range(value.shape[1] // LANES):
        block = value[:, LANES * t : LANES * (t + 1)]
        if block.shape[0] < part.rows:
            fill = jnp.zeros((part.rows - block.shape[0], LANES), block.dtype)
            block = jnp.concatenate([block, fill], axis=0)
        at = (part.first[number] + tile + t) * part.per_tile
        packed[at : at + part.per_tile] = block.astype(BF16).reshape(part.per_tile, UNIT, LANES)


def packed_call(
    name, z, part, section, device, choices, direct, body, scratch, flops, lists=(), grouped=0,
    per_group=1,
):
    count, ports = len(choices), len(part.ports())
    buffers, place_of = [], []
    for k, ((array, _), _) in enumerate(choices + sum(lists, [])):
        shape = array.shape[1:]
        member = k % per_group
        if k < grouped and member:
            place_of.append((len(buffers) - 1, member))
            continue
        place_of.append((len(buffers), 0 if k < grouped else None))
        rows = shape[0] * (per_group if k < grouped else 1)
        buffers.append(pltpu.VMEM((rows,) + shape[1:], array.dtype))
    choices = choices + sum(lists, [])

    def kernel(place, *refs):
        ins, refs = refs[: len(direct)], refs[len(direct) :]
        sources, refs = refs[: 2 * len(choices)], refs[2 * len(choices) :]
        halves, refs = (refs[:ports], refs[ports : 2 * ports]), refs[2 * ports :]
        joined, refs = refs[: len(lists)], refs[len(lists) :]
        landed, refs = refs[: len(buffers)], refs[len(buffers) :]
        packed, in_sems, out_sems, joined_sems = refs[:4]
        items = []
        for k, pair in enumerate(choices):
            copies, target = [], landed[place_of[k][0]]
            if place_of[k][1] is not None:
                rows = pair[0][0].shape[1]
                target = target.at[pl.ds(place_of[k][1] * rows, rows)]
            for side, (_, slot) in enumerate(pair):
                copy = pltpu.make_async_copy(
                    sources[2 * k + side].at[slot], target, in_sems.at[k]
                )
                pl.when(place[0] == side)(copy.start)
                copies.append(copy)
            items.append(Item(landed[place_of[k][0]], copies[0], lambda act: act()))
        body(items[:count], ins, packed, *refs[4:])
        if part.units > part.used:
            packed[part.used :] = jnp.zeros((part.units - part.used, UNIT, LANES), BF16)
        copies = []
        core = place[1] & 1
        side = part.pieces // 2
        for rel_core, targets in enumerate(halves):
            base = (core ^ rel_core) * part.half
            for k, (order, size, start) in enumerate(part.paths()):
                own = rearranged(place[1], order)
                for piece in range(part.pieces):
                    copies.append(
                        pltpu.make_async_copy(
                            packed.at[pl.ds(base + start + (piece ^ own) * size, size)],
                            targets[2 * k + piece // side].at[pl.ds(piece % side * size, size)],
                            out_sems.at[len(copies)],
                        )
                    )
                    copies[-1].start()
        at = count
        for k, members in enumerate(lists):
            for i in range(len(members)):
                copies.append(
                    pltpu.make_async_copy(items[at](), joined[k].at[i], joined_sems.at[at - count])
                )
                copies[-1].start()
                at += 1
        for copy in copies:
            copy.wait()

    number = 2 * part.pieces * len(part.orders)
    shapes = [jax.ShapeDtypeStruct((units, UNIT, LANES), BF16) for units in part.ports()]
    anywhere = pl.BlockSpec(memory_space=pl.ANY)
    results = pl.pallas_call(
        kernel,
        in_specs=[pl.BlockSpec(memory_space=pltpu.SMEM)]
        + [pl.BlockSpec(memory_space=pltpu.VMEM)] * len(direct)
        + [anywhere] * (2 * len(choices)),
        out_specs=[anywhere] * (2 * ports + len(lists)),
        out_shape=shapes * 2
        + [
            jax.ShapeDtypeStruct((len(members),) + members[0][0][0].shape[1:], BF16)
            for members in lists
        ],
        scratch_shapes=buffers
        + [
            pltpu.VMEM((part.units, UNIT, LANES), BF16),
            pltpu.SemaphoreType.DMA((len(choices),)),
            pltpu.SemaphoreType.DMA((number,)),
            pltpu.SemaphoreType.DMA((max(len(choices) - count, 1),)),
        ]
        + scratch,
        compiler_params=pltpu.CompilerParams(vmem_limit_bytes=VMEM_BYTES),
        cost_estimate=pl.CostEstimate(flops=flops, bytes_accessed=1 << 23, transcendentals=0),
        name=name,
    )(
        jnp.stack([section, device]).astype(jnp.int32),
        *direct,
        *[array for pair in choices for array, _ in pair],
    )
    return results[:ports], results[ports : 2 * ports], *results[2 * ports :]


def feed_gradients(z, part, section, device, fed, back):
    count = len(fed[0])

    def both_sides(groups, field):
        return [
            tuple((getattr(groups[side][i][0], field), groups[side][i][1]) for side in range(2))
            for i in range(count)
        ]

    fields = (
        both_sides(fed, Fed._fields[1]), both_sides(back, BackFeed._fields[0]),
        both_sides(back, BackFeed._fields[1]), both_sides(fed, Fed._fields[2]),
    )

    def body(items, ins, packed):
        def rows_of(k):
            return [item() for item in items[k * count : (k + 1) * count]][0][...]

        def hidden_columns(number, left, right):
            left = jnp.transpose(left)
            for at in range(0, z.hidden, 512):
                stop = min(at + 512, z.hidden)
                value = dot(left, right[:, at:stop]).astype(BF16)
                short = round_up(stop - at, LANES) - (stop - at)
                if short:
                    fill = jnp.zeros((value.shape[0], short), BF16)
                    value = jnp.concatenate([value, fill], axis=1)
                put_block(part, packed, number, value, at // LANES)

        pre = rows_of(1)
        hidden_columns(0, rows_of(0), pre)
        hidden_columns(1, rows_of(2), rows_of(3))
        wide = round_up(z.hidden, LANES)
        line = jnp.sum(pre.astype(F32), axis=0, keepdims=True)
        line = jnp.concatenate([line, jnp.zeros((1, wide - z.hidden), F32)], axis=1)
        lines = [line[:, LANES * t : LANES * (t + 1)] for t in range(wide // LANES)]
        lines.append(jnp.zeros((UNIT - len(lines), LANES), F32))
        packed[part.extra_at] = jnp.concatenate(lines, axis=0).astype(BF16)

    return packed_call(
        "feed_gradients", z, part, section, device, sum(fields, []), [], body, [], tally(z, 0.4),
        (), 4 * count, count,
    )


def attend_gradients(
    z, part, section, device, table, memory, sources, fed, back_feed, back, lists
):
    count = len(fed[0])

    def both_sides(groups, field):
        return [
            tuple((getattr(groups[side][i][0], field), groups[side][i][1]) for side in range(2))
            for i in range(count)
        ]

    fields = (
        [tuple(sources[side][i] for side in range(2)) for i in range(count)],
        both_sides(back, BackAttend._fields[0]),
        both_sides(back_feed, BackFeed._fields[2]),
        both_sides(fed, Fed._fields[0]),
        [((memory, i), (memory, i)) for i in range(count)],
        both_sides(back, BackAttend._fields[1]),
        both_sides(back, BackAttend._fields[2]),
        both_sides(back, BackAttend._fields[3]),
        both_sides(back_feed, BackFeed._fields[3]),
    )

    def body(items, ins, packed, inputs):
        def refs(k):
            return [item() for item in items[k * count : (k + 1) * count]]

        inputs[...] = jnp.zeros(inputs.shape, BF16)
        for i, ref in enumerate(refs(0)):
            inputs[i, : z.seg, :] = ref[...]
        turned = [jnp.transpose(inputs[i]) for i in range(count)]
        rows_in = jnp.concatenate([inputs[i, : z.rows, :] for i in range(count)], axis=0)
        rows_in = jnp.transpose(rows_in)
        per_half = z.width // LANES
        query, mixed = refs(1), refs(3)
        attend = jnp.transpose(jnp.concatenate([ref[...] for ref in refs(2)], axis=0))
        for half in range(HALVES):
            value = dot(rows_in, jnp.concatenate([ref[half] for ref in query], axis=0))
            put_block(part, packed, 0, value, half * per_half)
            value = dot(attend, jnp.concatenate([ref[half] for ref in mixed], axis=0))
            put_block(part, packed, 3, value, half * per_half)
        memories, key_value = refs(4), refs(5)
        for j in range(2 * HALVES):
            value = None
            for i in range(count):
                grad = dot_nt(memories[i][...], key_value[i][j, :, : z.mem])
                grad = grad + dot_nt(turned[i], key_value[i][j, :, z.mem :])
                value = grad if value is None else value + grad
            put_block(part, packed, 1, value, j * per_half)
        rel = refs(6)
        for half in range(HALVES):
            total = rel[0][half].astype(F32)
            for ref in rel[1:]:
                total = total + ref[half].astype(F32)
            value = dot_nt(ins[0][...], total.astype(BF16))
            put_block(part, packed, 2, value, half * per_half)
        biases, feed = refs(7), refs(8)
        rows = []
        for half in range(HALVES):
            total = biases[0][half]
            for ref in biases[1:]:
                total = total + ref[half]
            rows += [total[:, LANES * t : LANES * (t + 1)] for t in range(per_half)]
        packed[part.extra_at] = jnp.concatenate(
            rows + [jnp.zeros((UNIT - 8 * len(rows), LANES), F32)] * (8 * len(rows) < UNIT), axis=0
        ).astype(BF16)
        total = feed[0][...]
        for ref in feed[1:]:
            total = total + ref[...]
        short = round_up(z.model, LANES) - z.model
        total = jnp.concatenate([total, jnp.zeros((8, short), F32)], axis=1)
        rows = [total[:, LANES * t : LANES * (t + 1)] for t in range(total.shape[1] // LANES)]
        packed[part.extra_at + 1] = jnp.concatenate(
            rows + [jnp.zeros((UNIT - 8 * len(rows), LANES), F32)] * (8 * len(rows) < UNIT), axis=0
        ).astype(BF16)

    return packed_call(
        "attend_gradients", z, part, section, device, sum(fields, []), [table], body,
        [pltpu.VMEM((count, z.recent, z.model), BF16)], tally(z, 0.4), lists,
    )


def half_selection(z):
    shape = (z.proj, HALVES * z.width)
    dense, split = iota(shape, 0), iota(shape, 1)
    within = split % z.width
    same = (split // z.width) * z.used + within == dense
    return jnp.where((within < z.used) & same, 1.0, 0.0).astype(BF16)


def unpack_call(name, z, part, device, arrays, shapes, body):
    number = len(arrays)
    places = 2 * part.pieces * len(part.orders)

    def kernel(place, *refs):
        sources, outs = refs[:number], refs[number:-2]
        buffer, sems = refs[-2:]
        copies = []
        for source, within, at, size in piece_places(part, place[0], place[0] & 1):
            copy = pltpu.make_async_copy(
                sources[source].at[pl.ds(within, size)], buffer.at[pl.ds(at, size)],
                sems.at[len(copies)],
            )
            copy.start()
            copies.append(copy)

        def block(matrix, tile, count):
            tiles = []
            for t in range(part.first[matrix] + tile, part.first[matrix] + tile + count):
                at = t * part.per_tile
                tiles.append(buffer[at : at + part.per_tile].reshape(part.rows, LANES))
            return jnp.concatenate(tiles, axis=1) if count > 1 else tiles[0]

        for copy in copies:
            copy.wait()
        body(block, buffer, *outs)

    return pl.pallas_call(
        kernel,
        in_specs=[pl.BlockSpec(memory_space=pltpu.SMEM)]
        + [pl.BlockSpec(memory_space=pl.ANY)] * number,
        out_shape=[jax.ShapeDtypeStruct(shape, F32) for shape in shapes],
        scratch_shapes=[
            pltpu.VMEM((part.units, UNIT, LANES), BF16), pltpu.SemaphoreType.DMA((places,))
        ],
        compiler_params=pltpu.CompilerParams(vmem_limit_bytes=VMEM_BYTES),
        cost_estimate=pl.CostEstimate(flops=tally(z, 0.2), bytes_accessed=1 << 23, transcendentals=0),
        name=name,
    )(device.reshape(1).astype(jnp.int32), *arrays)


def unpack_feed(z, part, device, arrays):
    def body(block, buffer, inner, outer, inner_bias):
        for number, out in ((0, inner), (1, outer)):
            for at in range(0, z.hidden, 512):
                stop = min(at + 512, z.hidden)
                value = block(number, at // LANES, -(-(stop - at) // LANES)).astype(F32)
                out[:, 0, at:stop] = value[: z.model, : stop - at]
        stacked = buffer[part.extra_at].astype(F32)
        tiles = round_up(z.hidden, LANES) // LANES
        line = jnp.concatenate([stacked[t : t + 1] for t in range(tiles)], axis=1)
        inner_bias[...] = line[:, : z.hidden]

    wide = (z.model, 1, z.hidden)
    inner, outer, inner_bias = unpack_call(
        "unpack_feed", z, part, device, arrays, (wide, wide, (1, z.hidden)), body
    )
    return jnp.transpose(inner, (1, 0, 2)), jnp.transpose(outer, (1, 2, 0)), inner_bias


def unpack_attend(z, part, device, arrays):
    def body(block, buffer, query, key_value, position, output, content_bias, position_bias, *rows):
        spread = half_selection(z)
        wide = HALVES * z.width // LANES
        query[:, 0, :] = dot_nt(block(0, 0, wide), spread)[: z.model]
        position[:, 0, :] = dot_nt(block(2, 0, wide), spread)[: z.model]
        output[:, 0, :] = dot_nt(spread, block(3, 0, wide))[:, : z.model]
        for side in range(2):
            value = dot_nt(block(1, side * wide, wide), spread)[: z.model]
            key_value[:, 0, side * z.proj : (side + 1) * z.proj] = value
        stacked = buffer[part.extra_at].astype(F32)
        sums = jnp.concatenate([stacked[8 * t : 8 * (t + 1)] for t in range(wide)], axis=1)
        sums = dot_nt(sums.astype(BF16), spread)
        content_bias[...] = sums[0:1]
        position_bias[...] = sums[1:2]
        stacked = buffer[part.extra_at + 1].astype(F32)
        tiles = round_up(z.model, LANES) // LANES
        sums = jnp.concatenate([stacked[8 * t : 8 * (t + 1)] for t in range(tiles)], axis=1)
        for k, out in enumerate(rows):
            out[...] = sums[k : k + 1, : z.model]

    square, row = (z.model, 1, z.proj), (1, z.model)
    shapes = (
        square, (z.model, 1, 2 * z.proj), square, (z.proj, 1, z.model), (1, z.proj), (1, z.proj),
        row, row, row, row, row,
    )
    results = unpack_call("unpack_attend", z, part, device, arrays, shapes, body)
    return [jnp.transpose(r, (1, 0, 2)) if r.ndim == 3 else r for r in results]


def frequencies(z):
    exponent = np.arange(0, z.model, 2).astype(np.float32) / np.float32(z.model)
    return np.power(np.float32(10000.0), -exponent).astype(np.float32)[:, None]


def prepare_call(z, query, key_value, position, output, biases, rows):
    farthest = z.keys - 1 + z.shift - z.seg + 1
    number = len(biases)

    def body(rate, query, key_value, position, output, *refs):
        ins, refs = refs[: number + len(rows)], refs[number + len(rows) :]
        query_out, key_value_out, output_out, rel_out, table, lines = refs
        lines[...] = jnp.zeros(lines.shape, F32)
        rest = iota((z.model // 2, LANES), 1).astype(F32)
        near = rate[...] * rest
        far = rate[...] * (farthest - LANES * rest)
        near_sin, near_cos = jnp.sin(near), jnp.cos(near)
        far_sin, far_cos = jnp.sin(far), jnp.cos(far)
        sines, cosines = [], []
        for t in range(z.tiles):
            a, b = far_sin[:, t : t + 1], far_cos[:, t : t + 1]
            sines.append(a * near_cos - b * near_sin)
            cosines.append(b * near_cos + a * near_sin)
        values = [jnp.concatenate(tiles, axis=1) for tiles in (sines, cosines)]
        table[...] = jnp.concatenate(values, axis=0).astype(BF16)
        spread = half_selection(z)
        for half in range(HALVES):
            part = spread[:, half * z.width : (half + 1) * z.width]
            query_out[half] = dot(query[...], part).astype(BF16)
            output_out[half] = dot_tn(part, output[...]).astype(BF16)
            wide = dot_tn(part, jnp.transpose(position[...])).astype(BF16)
            rel_out[half] = dot(wide, table[...]).astype(BF16)
            for side in range(2):
                own = key_value[:, side * z.proj : (side + 1) * z.proj]
                key_value_out[side * HALVES + half] = dot_tn(
                    part, jnp.transpose(own.astype(F32)).astype(BF16)
                ).astype(BF16)
            for k, source in enumerate(ins[:number]):
                at = k * HALVES + half
                lines[at : at + 1, : z.width] = dot(source[...], part)
        for k, source in enumerate(ins[number:]):
            at = number * HALVES + k
            lines[at : at + 1, : source.shape[1]] = source[...].astype(F32)

    shapes = [
        ((HALVES, z.model, z.width), BF16), ((2 * HALVES, z.width, z.model), BF16),
        ((HALVES, z.width, z.model), BF16), ((HALVES, z.width, z.cols), BF16),
        ((z.model, z.cols), BF16), ((Line.count, z.hidden), F32),
    ]
    return pl.pallas_call(
        body,
        out_shape=[jax.ShapeDtypeStruct(s, t) for s, t in shapes],
        compiler_params=pltpu.CompilerParams(vmem_limit_bytes=VMEM_BYTES),
        name="prepare",
    )(frequencies(z), query, key_value, position, output, *biases, *rows)


def unwritten(shapes):
    return pl.pallas_call(
        lambda *refs: None,
        out_shape=shapes,
        out_specs=jax.tree.map(lambda s: pl.BlockSpec(memory_space=pl.ANY), shapes),
        name="unwritten",
    )()


def moved_along(value, steps):
    count = lax.axis_size("section")
    first, last = max(0, -steps), min(count, count - steps)
    return lax.ppermute(value, "section", [(i, i + steps) for i in range(first, last)])


def shards(
    stream_in, memories, cotangent, query_weight, key_value_matrix, position_weight,
    output_weight, bias_content, bias_position, attend_gain, attend_bias, inner_weight,
    inner_bias, outer_weight, outer_bias, feed_gain, feed_bias,
):
    count, seg_len, model = stream_in.shape
    z = Sizes(seg_len, memories.shape[2], model, query_weight.shape[2], inner_weight.shape[2])
    devices = lax.axis_size("dp")
    section, device = lax.axis_index("section"), lax.axis_index("dp")
    first = section == 0
    memory = jnp.transpose(memories[0], (0, 2, 1))
    made = prepare_call(
        z, query_weight[0], key_value_matrix[0], position_weight[0], output_weight[0],
        [bias_content, bias_position],
        [attend_gain, attend_bias, inner_bias, outer_bias, feed_gain, feed_bias],
    )
    table = made[4]
    weights = Weights(
        made[0], made[1], made[2], made[3], inner_weight[0], jnp.transpose(outer_weight[0]), made[5],
    )
    rest = count - 1

    def shape_of(value):
        return jax.tree.map(lambda a: jax.ShapeDtypeStruct(a.shape, a.dtype), value)

    def pick(first_act, second_act):
        made = [jax.eval_shape(act) for act in (first_act, second_act)]

        def branch(side, act):
            def run():
                blank = shape_of(made[1 - side])
                blank = unwritten(blank) if jax.tree.leaves(blank) else blank
                return (act(), blank) if side == 0 else (blank, act())

            return run

        return lax.cond(jnp.logical_not(first), branch(1, second_act), branch(0, first_act))

    forward_zero = forward_call(z, weights, stream_in, memory, 0, 1)
    sent = moved_along(forward_zero[0], 1)

    def both(segment_number, source, slot):
        return both_call(z, weights, source, slot, memory, cotangent, segment_number)

    forward_rest, both_zero = pick(
        lambda: forward_call(z, weights, stream_in, memory, 1, rest),
        lambda: both(0, sent, 0),
    )
    arrived = moved_along(forward_rest[0], 1)
    grads = [moved_along(both_zero[1], -1)]

    def forwarded(number):
        return (forward_zero, 0) if number == 0 else (forward_rest, number - 1)

    def feed_back(number):
        stored, slot = forwarded(number)
        return feed_back_call(z, weights, grads[number], stored[2], slot)

    def attend_back(number, back_first, feed):
        stored, slot = forwarded(number)
        return attend_back_call(z, weights, back_first, feed.attend, stored[1], slot)

    both_made, feeds, attends = [both_zero], [], []
    for number in range(rest):

        def first_act(number=number):
            back_first, feed = feed_back(number)
            return feed, attend_back(number, back_first, feed)

        (feed, attend), second = pick(
            first_act, lambda number=number: both(number + 1, arrived, number)
        )
        feeds.append(feed)
        attends.append(attend)
        both_made.append(second)
        grads.append(moved_along(second[1], -1))

    feed_part = Part(z, (z.hidden, z.hidden), 1, devices)
    wide = HALVES * z.width
    attend_part = Part(z, (wide, 2 * wide, wide, wide), 2, devices)
    fed = (
        [(stored[3], slot) for stored, slot in map(forwarded, range(count))],
        [(member[2], 0) for member in both_made],
    )
    (back_first, feed), _ = pick(lambda: feed_back(rest), lambda: ())
    feeds.append(feed)
    back_feed = ([(member, 0) for member in feeds], [(member[3], 0) for member in both_made])
    feed_mine, feed_theirs = feed_gradients(z, feed_part, section, device, fed, back_feed)
    feed_chains = chains_of(feed_part, feed_mine, swapped_cores(feed_theirs))
    back_first, feed_chains[1].keep = lax.optimization_barrier((back_first, feed_chains[1].keep))
    attend, _ = pick(lambda: attend_back(rest, back_first, feed), lambda: ())
    attends.append(attend)
    last_grad, feed_chains[0].flying = lax.optimization_barrier(
        (attend[0], feed_chains[0].flying)
    )
    last = step_all(feed_chains, feed_chains[1])
    table, last.keep = lax.optimization_barrier((table, last.keep))
    sources = (
        [(stream_in, i) for i in range(count)],
        [(sent, 0)] + [(arrived, i) for i in range(rest)],
    )
    firsts = [forwarded(i) for i in range(count)]
    layer_out = [
        ((firsts[i][0][0], firsts[i][1]), (both_made[i][0], 0)) for i in range(count)
    ]
    gradients = [attend[0] for attend in attends[:-1]] + [last_grad]
    input_grad = [((gradients[i], 0), (both_made[i][1], 0)) for i in range(count)]
    mine, theirs, outputs, input_grads = attend_gradients(
        z, attend_part, section, device, table, memory, sources, fed, back_feed,
        ([(member[1], 0) for member in attends], [(member[4], 0) for member in both_made]),
        (layer_out, input_grad),
    )
    attend_chains = chains_of(attend_part, mine, swapped_cores(theirs))
    last = attend_chains[1]
    while feed_chains[0].spread >= 0:
        last = step_all(feed_chains, last)
        last = step_all(attend_chains, last)
    feed_arrays = finished(feed_chains)
    inner, outer, inner_bias_grad = unpack_feed(z, feed_part, device, feed_arrays)
    chain = attend_chains[0]
    chain.flying, inner_bias_grad = lax.optimization_barrier((chain.flying, inner_bias_grad))
    while chain.spread >= 0:
        last = step_all(attend_chains, last)
    attend_arrays = finished(attend_chains)
    (
        query, key_value, position, output, bias_c, bias_p, gain_a, bias_a, bias_o, gain_f, bias_f,
    ) = unpack_attend(z, attend_part, device, attend_arrays)
    return (
        outputs[None], input_grads[None], query, key_value, position, output, bias_c, bias_p,
        gain_a, bias_a, inner, inner_bias_grad, outer, bias_o, gain_f, bias_f,
    )


def solution(mesh):
    stacked, dp = P("section"), P("dp")
    both = P("section", "dp")
    return jax.shard_map(
        shards,
        mesh=mesh,
        in_specs=(dp, both, dp) + (stacked,) * 14,
        out_specs=(both, both) + (stacked,) * 14,
        check_vma=False,
    )
```

```python
from functools import partial
from typing import Any, NamedTuple

import jax
import jax.numpy as jnp
import numpy as np
from jax import lax
from jax.experimental import pallas as pl
from jax.experimental.pallas import tpu as pltpu
from jax.sharding import PartitionSpec as P

HEADS = 10
HALVES = 2
GROUP = HEADS // HALVES
LANES = 128
UNIT = 32
NORM_EPS = 1e-05
GELU_SLOPE = 0.7978845608028654
GELU_CUBIC = 0.044715
MASK_FILL = -1e30
LOG2_E = 1.4426950408889634
F32 = jnp.float32
BF16 = jnp.bfloat16
VMEM_BYTES = 60 * 1024 * 1024


def round_up(value, unit):
    return -(-value // unit) * unit


class Sizes:
    def __init__(self, seg_len, mem_len, model, proj, hidden):
        self.seg, self.mem, self.model, self.proj, self.hidden = seg_len, mem_len, model, proj, hidden
        self.keys = mem_len + seg_len
        self.head = proj // HEADS
        self.rows = round_up(seg_len, 16)
        self.body = seg_len // 16 * 16
        self.tail = self.body + 8
        self.used = GROUP * self.head
        self.width = round_up(self.used, 256)
        self.cols = round_up(self.keys, LANES)
        self.recent = self.cols - mem_len
        self.stack = round_up(GROUP * self.tail, 256)
        self.tail_at = GROUP * self.body
        self.tail_rows = self.stack - self.tail_at
        self.tiles = self.cols // LANES
        self.shift = round_up(seg_len - 1, 8)
        self.scale = self.head ** (-0.5)
        assert self.seg - self.body <= 8 and self.tail_rows % 16 == 0
        assert self.shift == self.tail and self.mem % LANES == 0 and self.shift <= LANES * 2


class Weights(NamedTuple):
    query: Any
    key_value: Any
    output: Any
    rel: Any
    inner: Any
    outer: Any
    lines: Any


class Line:
    bias_content, bias_position = 0, HALVES
    attend_gain, attend_bias, inner_bias, outer_bias, feed_gain, feed_bias = range(
        2 * HALVES, 2 * HALVES + 6
    )
    count = 16


class Kept(NamedTuple):
    attention: Any
    content_stack: Any
    position_stack: Any
    keys: Any
    values: Any
    mixed: Any


class KeptFeed(NamedTuple):
    first_normed: Any
    first_inverse: Any
    second_normed: Any
    second_inverse: Any
    slope: Any


class Fed(NamedTuple):
    mixed_low: Any
    middle: Any
    active: Any


class BackFeed(NamedTuple):
    pre: Any
    outer: Any
    attend: Any
    sums: Any


class BackAttend(NamedTuple):
    query: Any
    key_value: Any
    rel: Any
    sums: Any


def layouts(z):
    halves = lambda rows, cols, kind: ((HALVES, rows, cols), kind)
    kept = Kept(
        halves(z.stack, z.cols, BF16),
        halves(z.stack, z.width, BF16),
        halves(z.stack, z.width, BF16),
        halves(z.width, z.cols, BF16),
        halves(z.width, z.cols, BF16),
        halves(z.rows, z.width, F32),
    )
    wide, narrow = ((z.rows, z.model), F32), ((z.rows, 1), F32)
    kept_feed = KeptFeed(wide, narrow, wide, narrow, ((z.rows, z.hidden), BF16))
    low = ((z.rows, z.model), BF16)
    fed = Fed(halves(z.rows, z.width, BF16), low, ((z.rows, z.hidden), BF16))
    back_feed = BackFeed(((z.rows, z.hidden), BF16), low, low, ((8, z.model), F32))
    back_attend = BackAttend(
        halves(z.rows, z.width, BF16),
        ((2 * HALVES, z.width, z.cols), BF16),
        halves(z.width, z.cols, BF16),
        halves(8, z.width, F32),
    )
    return kept, kept_feed, fed, back_feed, back_attend


def dot(left, right):
    return lax.dot_general(left, right, (((1,), (0,)), ((), ())), preferred_element_type=F32)


def dot_nt(left, right):
    return lax.dot_general(left, right, (((1,), (1,)), ((), ())), preferred_element_type=F32)


def dot_tn(left, right):
    return lax.dot_general(left, right, (((0,), (0,)), ((), ())), preferred_element_type=F32)


def iota(shape, dim):
    return lax.broadcasted_iota(jnp.int32, shape, dim)


class Item:
    def __init__(self, ref, copy=None, once=None):
        self.ref, self.copy, self.once = ref, copy, once

    def __call__(self):
        if self.copy is not None:
            self.once(self.copy.wait)
            self.copy = None
        return self.ref


class Out:
    def __init__(self, ref, target, sems):
        self.ref, self.target, self.sems = ref, target, sems
        self.copies = []

    def part(self, index, slot):
        copy = pltpu.make_async_copy(self.ref.at[index], self.target.at[index], self.sems.at[slot])
        copy.start()
        return copy

    def send(self):
        copy = pltpu.make_async_copy(self.ref, self.target, self.sems.at[0])
        copy.start()
        self.copies.append(copy)


def kernel_call(name, body, direct, fetched, made, scratch, count=1, flops=0):
    made = list(made)
    parts = 4
    slots = jnp.stack([jnp.int32(0 if slot is None else slot) for _, slot in fetched])

    def kernel(slots, *refs):
        refs = list(refs)

        def take(number):
            taken = refs[:number]
            del refs[:number]
            return taken

        ins, sources, targets = take(len(direct)), take(len(fetched)), take(len(made))
        landed, built = take(len(fetched)), take(len(made))
        in_sems, out_sems = take(2)
        first = pl.program_id(0) == 0
        once = (lambda act: act()) if count == 1 else (lambda act: pl.when(first)(act))
        items = []
        for k, (ref, (_, slot)) in enumerate(zip(sources, fetched)):
            source = ref if slot is None else ref.at[slots[k]]
            copy = pltpu.make_async_copy(source, landed[k], in_sems.at[k])
            once(copy.start)
            items.append(Item(landed[k], copy, once))
        outs = [
            Out(ref, target.at[pl.program_id(0)], out_sems.at[k])
            for k, (ref, target) in enumerate(zip(built, targets))
        ]
        body(ins, items, outs, *refs)
        for item in items:
            item()
        for out in outs:
            for copy in out.copies:
                copy.wait()

    landing = [
        pltpu.VMEM(array.shape if slot is None else array.shape[1:], array.dtype)
        for array, slot in fetched
    ]
    results = pl.pallas_call(
        kernel,
        grid=(count,),
        in_specs=[pl.BlockSpec(memory_space=pltpu.SMEM)]
        + [spec for _, spec in direct]
        + [pl.BlockSpec(memory_space=pl.ANY)] * len(fetched),
        out_specs=[pl.BlockSpec(memory_space=pl.ANY)] * len(made),
        out_shape=[jax.ShapeDtypeStruct((count,) + tuple(s), t) for s, t in made],
        scratch_shapes=landing
        + [pltpu.VMEM(s, t) for s, t in made]
        + [
            pltpu.SemaphoreType.DMA((max(len(fetched), 1),)),
            pltpu.SemaphoreType.DMA((max(len(made), 1), parts)),
        ]
        + scratch,
        compiler_params=pltpu.CompilerParams(vmem_limit_bytes=VMEM_BYTES),
        cost_estimate=pl.CostEstimate(flops=flops, bytes_accessed=1 << 23, transcendentals=0),
        name=name,
    )(slots, *[array for array, _ in direct], *[array for array, _ in fetched])
    return list(results)


def whole(array):
    zeros = (0,) * array.ndim
    return (array, pl.BlockSpec(array.shape, lambda i: zeros, pipeline_mode=pl.Buffered(1)))


def segment(array, slot):
    zeros = (0,) * (array.ndim - 1)
    return (array, pl.BlockSpec((None,) + array.shape[1:], lambda i: (i + slot,) + zeros))


def head_lanes(z, rows, head):
    lane = iota((rows, z.width), 1)
    return (lane >= z.head * head) & (lane < z.head * (head + 1))


def stack_heads(z, target, source):
    tails = []
    for head in range(GROUP):
        own = jnp.where(head_lanes(z, z.tail, head), source[: z.tail], 0.0)
        target[z.body * head : z.body * (head + 1), :] = own[: z.body].astype(BF16)
        tails.append(own[z.body :])
    tails.append(jnp.zeros((z.tail_rows - 8 * GROUP, z.width), F32))
    target[z.tail_at :, :] = jnp.concatenate(tails, axis=0).astype(BF16)


def unstack_heads(z, source):
    total = None
    for head in range(GROUP):
        rows = jnp.concatenate(
            [
                source[z.body * head : z.body * (head + 1)],
                source[z.tail_at + 8 * head : z.tail_at + 8 * (head + 1)],
            ],
            axis=0,
        )
        own = jnp.where(head_lanes(z, z.tail, head), rows, 0.0)
        total = own if total is None else total + own
    return total


def normalize(values):
    centered = values - jnp.mean(values, axis=-1, keepdims=True)
    variance = jnp.mean(centered * centered, axis=-1, keepdims=True)
    inverse = lax.rsqrt(variance + NORM_EPS)
    return (centered * inverse, inverse)


def normalize_back(grad_normed, normed, inverse):
    return inverse * (
        grad_normed
        - jnp.mean(grad_normed, axis=-1, keepdims=True)
        - normed * jnp.mean(grad_normed * normed, axis=-1, keepdims=True)
    )


def shifted_tiles(z, tiles, first_row):
    base = (first_row - z.shift) % LANES
    turns = (first_row - z.shift - base) // LANES
    lane, row = iota((8, LANES), 1), iota((8, LANES), 0)
    turned = [pltpu.roll(tile, base, 1, stride=1, stride_axis=0) for tile in tiles]
    kept = lane >= base + row
    return [
        jnp.where(kept, turned[(t - turns) % z.tiles], turned[(t - turns - 1) % z.tiles])
        for t in range(z.tiles)
    ]


def restored_tiles(z, tiles, first_row):
    lane, row = iota((8, LANES), 1), iota((8, LANES), 0)
    amount = z.shift - first_row
    place = (lane - amount + row) % LANES
    turned = [jnp.take_along_axis(tile, place, axis=1) for tile in tiles]
    base, turns = amount % LANES, amount // LANES
    if base >= 8:
        kept, other = lane >= base - row, -1
    else:
        assert base == 0
        kept, other = lane < LANES - row, 1
    return [
        jnp.where(kept, turned[(t - turns) % z.tiles], turned[(t - turns + other) % z.tiles])
        for t in range(z.tiles)
    ]


def split_tiles(z, block):
    return [block[:, LANES * t : LANES * (t + 1)] for t in range(z.tiles)]


def over_rows(z, chunk):
    for head in range(GROUP):
        for part in range(z.body // 16):
            chunk(head * z.body + 16 * part, 16 * part, 16 * part + 8)
    for part in range(z.tail_rows // 16):
        chunk(z.tail_at + 16 * part, z.body, z.body)


def attention_rows(z, content, position, attention):
    def chunk(row, first, second):
        for at, query in ((row, first), (row + 8, second)):
            rows = slice(at, at + 8)
            moved = shifted_tiles(z, split_tiles(z, position[rows, :]), query)
            for t in range(z.tiles):
                lanes = slice(LANES * t, LANES * (t + 1))
                scores = content[rows, lanes] + moved[t]
                if t >= z.mem // LANES:
                    ahead = iota((8, LANES), 1) - iota((8, LANES), 0)
                    allowed = ahead <= z.mem + query - LANES * t
                    scores = jnp.where(allowed, scores, MASK_FILL)
                content[rows, lanes] = scores

    over_rows(z, chunk)
    scores = content[...]
    largest = jnp.max(scores, axis=-1, keepdims=True)
    powers = jnp.exp2((scores - largest) * (z.scale * LOG2_E))
    inverse = 1.0 / jnp.sum(powers, axis=-1, keepdims=True)
    attention[...] = (powers * inverse).astype(BF16)


def attention_rows_back(z, attention, back_map, weighted, back_raw, back_table):
    def chunk(row, first, second):
        rows = slice(row, row + 16)
        inner = weighted[rows, :]
        tops, lows = [], []
        for t in range(z.tiles):
            lanes = slice(LANES * t, LANES * (t + 1))
            raw = attention[rows, lanes].astype(F32) * ((back_map[rows, lanes] - inner) * z.scale)
            back_raw[rows, lanes] = raw.astype(BF16)
            tops.append(raw[:8])
            lows.append(raw[8:])
        tops, lows = restored_tiles(z, tops, first), restored_tiles(z, lows, second)
        for t in range(z.tiles):
            pair = jnp.concatenate([tops[t], lows[t]], axis=0).astype(BF16)
            back_table[rows, LANES * t : LANES * (t + 1)] = pair

    over_rows(z, chunk)


def gelu_and_slope(values):
    squared = values * values
    tangent = jnp.tanh(GELU_SLOPE * (values + GELU_CUBIC * squared * values))
    half = 0.5 * (1.0 + tangent)
    slope = half + 0.5 * values * (1.0 - tangent * tangent) * GELU_SLOPE * (
        1.0 + 3.0 * GELU_CUBIC * squared
    )
    return (values * half, slope)


def forward_body(
    z, w, source, memory, kept, kept_feed, fed, result, hidden, content, position, attention_done
):
    hidden[...] = jnp.zeros(hidden.shape, BF16)
    hidden[: z.seg, :] = source[...]
    for j in range(2 * HALVES):
        target = (kept.keys if j < HALVES else kept.values).at[j % HALVES]
        target[:, : z.mem] = dot(w.key_value()[j], memory[...]).astype(BF16)
        target[:, z.mem :] = dot_nt(w.key_value()[j], hidden[...]).astype(BF16)
    rows_in = hidden[: z.rows, :]
    real = iota((z.rows, 1), 0) < z.seg
    lines = w.lines()
    line = lambda number: lines[number : number + 1, : z.model]
    for half in range(HALVES):
        raw = dot(rows_in, w.query()[half])
        for stack, number in (
            (kept.content_stack, Line.bias_content), (kept.position_stack, Line.bias_position)
        ):
            bias = lines[number + half : number + half + 1, : z.width]
            stack_heads(z, stack.at[half], jnp.where(real, raw + bias, 0.0))
    rel = w.rel()

    def one_half(half, carry):
        content[...] = dot(kept.content_stack[half], kept.keys[half])
        position[...] = dot(kept.position_stack[half], rel[half])
        attention_rows(z, content, position, kept.attention.at[half])
        mixed = unstack_heads(z, dot_nt(kept.attention[half], kept.values[half]))
        kept.mixed[half, : z.tail, :] = mixed
        kept.mixed[half, z.tail :, :] = jnp.zeros((z.rows - z.tail, z.width), F32)
        return carry

    lax.fori_loop(0, HALVES, one_half, 0)
    attention_done()
    total = rows_in.astype(F32)
    for half in range(HALVES):
        mixed = kept.mixed[half].astype(BF16)
        fed.mixed_low[half] = mixed
        total = total + dot(mixed, w.output()[half])
    normed, inverse = normalize(total)
    kept_feed.first_normed[...] = normed
    kept_feed.first_inverse[...] = inverse
    middle = (normed * line(Line.attend_gain) + line(Line.attend_bias)).astype(BF16)
    fed.middle[...] = middle
    active, slope = gelu_and_slope(
        dot(middle, w.inner()[...]) + lines[Line.inner_bias : Line.inner_bias + 1, :]
    )
    kept_feed.slope[...] = slope.astype(BF16)
    active = active.astype(BF16)
    fed.active[...] = active
    feed = dot_nt(active, w.outer()[...]) + line(Line.outer_bias)
    normed, inverse = normalize(middle.astype(F32) + feed)
    kept_feed.second_normed[...] = normed
    kept_feed.second_inverse[...] = inverse
    out = (normed * line(Line.feed_gain) + line(Line.feed_bias)).astype(BF16)
    result[...] = out[: z.seg]


def feed_back_body(z, w, grad_in, kept, back, back_first, top):
    top[...] = jnp.zeros(top.shape, BF16)
    top[: z.seg, :] = grad_in[...]
    grad_top = top[...].astype(F32)
    lines = w.lines()
    line = lambda number: lines[number : number + 1, : z.model]
    normed = kept.second_normed()[...]
    second = normalize_back(
        grad_top * line(Line.feed_gain), normed, kept.second_inverse()[...]
    )
    outer = second.astype(BF16)
    back.outer[...] = outer
    pre = (dot(outer, w.outer()[...]) * kept.slope()[...].astype(F32)).astype(BF16)
    back.pre[...] = pre
    middle = second + dot_nt(pre, w.inner()[...])
    first_normed = kept.first_normed()[...]
    first = normalize_back(
        middle * line(Line.attend_gain), first_normed, kept.first_inverse()[...]
    )
    back_first[...] = first
    back.attend[...] = first.astype(BF16)
    sums = back.sums
    sums[...] = jnp.zeros(sums.shape, F32)
    rows = (middle * first_normed, middle, outer.astype(F32), grad_top * normed, grad_top)
    for k, values in enumerate(rows):
        sums[k : k + 1, :] = jnp.sum(values, axis=0, keepdims=True)


def attend_back_body(
    z, w, kept, back_first, back_attend, back, send, input_grad, stack, back_map, weighted, raw, table
):
    refs = Kept(*[item() for item in kept])
    output, rel = w.output(), w.rel()

    def one_half(half, carry):
        own = dot_nt(back_attend[...], output[half]).astype(BF16).astype(F32)
        stack_heads(z, stack, own)
        product = own[: z.tail] * refs.mixed[half, : z.tail, :]
        weighted[z.tail_at :, :] = jnp.zeros((z.tail_rows, 1), F32)
        for head in range(GROUP):
            inner = jnp.where(head_lanes(z, z.tail, head), product, 0.0)
            inner = jnp.sum(inner, axis=1, keepdims=True)
            weighted[z.body * head : z.body * (head + 1), :] = inner[: z.body]
            at = z.tail_at + 8 * head
            weighted[at : at + 8, :] = inner[z.body :]
        back_map[...] = dot(stack[...], refs.values[half])
        attention_rows_back(z, refs.attention.at[half], back_map, weighted, raw, table)
        back.key_value[half] = dot_tn(refs.content_stack[half], raw[...]).astype(BF16)
        back.key_value[HALVES + half] = dot_tn(stack[...], refs.attention[half]).astype(BF16)
        back.rel[half] = dot_tn(refs.position_stack[half], table[...]).astype(BF16)
        send(half)
        from_content = unstack_heads(z, dot_nt(raw[...], refs.keys[half]))
        from_position = unstack_heads(z, dot_nt(table[...], rel[half]))
        back.query[half, : z.tail, :] = (from_content + from_position).astype(BF16)
        back.query[half, z.tail :, :] = jnp.zeros((z.rows - z.tail, z.width), BF16)
        back.sums[half] = jnp.concatenate(
            [
                jnp.sum(from_content, axis=0, keepdims=True),
                jnp.sum(from_position, axis=0, keepdims=True),
                jnp.zeros((6, z.width), F32),
            ],
            axis=0,
        )
        return carry

    lax.fori_loop(0, HALVES, one_half, 0)
    total = back_first[...]
    for half in range(HALVES):
        total = total + dot_nt(back.query[half], w.query()[half])
    for j in range(2 * HALVES):
        recent = dot_tn(back.key_value[j, :, z.mem :], w.key_value()[j])
        total = total + recent[: z.rows]
    input_grad[...] = total[: z.seg].astype(BF16)


def back_scratch(z):
    return [
        pltpu.VMEM((z.stack, z.width), BF16),
        pltpu.VMEM((z.stack, z.cols), F32),
        pltpu.VMEM((z.stack, 1), F32),
        pltpu.VMEM((z.stack, z.cols), BF16),
        pltpu.VMEM((z.stack, z.cols), BF16),
    ]


def vmem(entries):
    return [pltpu.VMEM(s, t) for s, t in entries]


def tally(z, passes):
    return int(passes * 2e10)


ARRIVAL = (1, 6, 0, 3, 2, 4, 5)


def arriving(weights):
    return [(weights[k], None) for k in ARRIVAL]


def arrived_weights(items):
    own = dict(zip(ARRIVAL, items))
    return Weights(*[own[k] for k in range(len(ARRIVAL))])


def refs_of(kind, outs):
    return kind(*[out.ref for out in outs])


def send_all(outs):
    for out in outs:
        out.send()


def attend_sender(outs):
    query, key_value, rel, sums = outs

    def parts(half):
        yield key_value, half, half
        yield key_value, HALVES + half, HALVES + half
        yield rel, half, half

    def send(half):
        for out, index, slot in parts(half):
            out.part(index, slot)

    def finish():
        for half in range(HALVES):
            for out, index, slot in parts(half):
                pltpu.make_async_copy(
                    out.ref.at[index], out.target.at[index], out.sems.at[slot]
                ).wait()

    return send, finish


@partial(jax.jit, static_argnums=(0, 4, 5))
def forward_call(z, weights, source, memory, slot, count):
    kept, kept_feed, fed = layouts(z)[:3]
    direct = [segment(source, slot), segment(memory, slot)]

    def body(ins, items, outs, hidden, content, position):
        result, outs = outs[0], outs[1:]
        forward_body(
            z, arrived_weights(items), ins[0], ins[1], refs_of(Kept, outs[:6]),
            refs_of(KeptFeed, outs[6:11]), refs_of(Fed, outs[11:]), result.ref, hidden, content,
            position, lambda: send_all(outs[:6]),
        )
        send_all([result] + outs[6:])

    made = [((z.seg, z.model), BF16), *kept, *kept_feed, *fed]
    results = kernel_call(
        "forward", body, direct, arriving(weights), made,
        [
            pltpu.VMEM((z.recent, z.model), BF16),
            pltpu.VMEM((z.stack, z.cols), F32),
            pltpu.VMEM((z.stack, z.cols), F32),
        ],
        count, tally(z, count),
    )
    return results[0], Kept(*results[1:7]), KeptFeed(*results[7:12]), Fed(*results[12:])


@partial(jax.jit, static_argnums=0)
def both_call(z, weights, source, source_slot, memory, grad_in, slot):
    kept, kept_feed, fed, back_feed, back_attend = layouts(z)
    fetched = [(source, source_slot), (memory, slot)] + arriving(weights) + [(grad_in, slot)]

    def body(ins, items, outs, hidden, content, position, *scratch):
        w = arrived_weights(items[2:-1])
        result, input_grad = outs[:2]
        fed_outs, feed_outs, attend_outs = outs[2:5], outs[5:9], outs[9:13]
        held, held_feed = Kept(*scratch[:6]), KeptFeed(*scratch[6:11])
        first, top, stack, weighted, raw, table = scratch[11:]
        forward_body(
            z, w, items[0](), items[1](), held, held_feed, refs_of(Fed, fed_outs), result.ref,
            hidden, content, position, lambda: None,
        )
        send_all([result] + fed_outs)
        feed_refs = refs_of(BackFeed, feed_outs)
        feed_back_body(
            z, w, items[-1](), KeptFeed(*[Item(ref) for ref in held_feed]), feed_refs, first, top
        )
        send_all(feed_outs)
        send, finish = attend_sender(attend_outs)
        attend_back_body(
            z, w, Kept(*[Item(ref) for ref in held]), first, feed_refs.attend,
            refs_of(BackAttend, attend_outs), send, input_grad.ref, stack, content, weighted,
            raw, table,
        )
        send_all([input_grad, attend_outs[0], attend_outs[3]])
        finish()

    row = ((z.seg, z.model), BF16)
    scratch = back_scratch(z)
    del scratch[1]
    results = kernel_call(
        "forward_backward", body, [], fetched, [row, row, *fed, *back_feed, *back_attend],
        [
            pltpu.VMEM((z.recent, z.model), BF16),
            pltpu.VMEM((z.stack, z.cols), F32),
            pltpu.VMEM((z.stack, z.cols), F32),
        ]
        + vmem(kept)
        + vmem(kept_feed)
        + [pltpu.VMEM((z.rows, z.model), F32), pltpu.VMEM((z.rows, z.model), BF16)]
        + scratch,
        1, tally(z, 2),
    )
    return (
        results[0], results[1], Fed(*results[2:5]), BackFeed(*results[5:9]),
        BackAttend(*results[9:13]),
    )


@partial(jax.jit, static_argnums=0)
def feed_back_call(z, weights, grad_in, kept, slot):
    back_feed = layouts(z)[3]
    fetched = [(weights.lines, None)]
    fetched += [(a, slot) for a in (kept.second_normed, kept.second_inverse)]
    fetched += [(weights.outer, None), (kept.slope, slot), (weights.inner, None)]
    fetched += [(a, slot) for a in (kept.first_normed, kept.first_inverse)]

    def body(ins, items, outs, top):
        lines, second_normed, second_inverse, outer, slope, inner, first_normed, first_inverse = items
        w = Weights(*[None] * 4, inner, outer, lines)
        held = KeptFeed(first_normed, first_inverse, second_normed, second_inverse, slope)
        feed_back_body(z, w, ins[0], held, refs_of(BackFeed, outs[1:]), outs[0].ref, top)
        send_all(outs)

    results = kernel_call(
        "feed_backward", body, [segment(grad_in, 0)], fetched,
        [((z.rows, z.model), F32), *back_feed], [pltpu.VMEM((z.rows, z.model), BF16)],
        1, tally(z, 0.3),
    )
    return results[0], BackFeed(*results[1:])


@partial(jax.jit, static_argnums=0)
def attend_back_call(z, weights, back_first, back_attend, kept, slot):
    fetched = [(back_first, 0), (back_attend, 0), (weights.output, None)]
    fetched += [(array, slot) for array in kept]
    fetched += [(a, None) for a in (weights.rel, weights.query, weights.key_value)]

    def body(ins, items, outs, *scratch):
        first, attend, output = items[:3]
        rel, query, key_value = items[9:]
        w = Weights(query, key_value, output, rel, *[None] * 3)
        send, finish = attend_sender(outs[1:])
        attend_back_body(
            z, w, Kept(*items[3:9]), first(), attend(), refs_of(BackAttend, outs[1:]), send,
            outs[0].ref, *scratch,
        )
        send_all([outs[0], outs[1], outs[4]])
        finish()

    results = kernel_call(
        "attend_backward", body, [], fetched, [((z.seg, z.model), BF16), *layouts(z)[4]],
        back_scratch(z), 1, tally(z, 0.7),
    )
    return results[0], BackAttend(*results[1:])


class Part:
    def __init__(self, z, widths, extra, devices):
        self.rows = round_up(z.model, UNIT)
        self.per_tile = self.rows // UNIT
        self.first, at = [], 0
        for width in widths:
            self.first.append(at)
            at += round_up(width, LANES) // LANES
        self.extra_at = at * self.per_tile
        self.used = self.extra_at + extra
        bits = devices.bit_length() - 1
        assert devices == 1 << bits and bits >= 3
        order = list(range(1, bits))
        self.orders = (order, [order[1], order[0]] + order[2:])
        self.pieces = devices // 2
        per_piece = -(-self.used // devices)
        self.sizes = (-(-per_piece // 2), per_piece // 2)
        self.starts = (0, self.pieces * self.sizes[0])
        self.half = self.pieces * per_piece
        self.units = 2 * self.half

    def paths(self):
        return list(zip(self.orders, self.sizes, self.starts))

    def ports(self):
        return [self.pieces // 2 * size for size in self.sizes for _ in range(2)]


def rearranged(index, order):
    total = 0
    for place, bit in enumerate(reversed(order)):
        total = total + (((index >> bit) & 1) << place)
    return total


def exchanged(array, bit):
    count = lax.axis_size("dp")
    return lax.ppermute(array, "dp", [(i, i ^ (1 << bit)) for i in range(count)])


class Chain:
    def __init__(self, order, mine, came):
        self.order, self.reduced, self.spread = order, 1, len(order) - 1
        self.keep = mine[0] + came[0]
        self.flying = exchanged(mine[1] + came[1], order[0])

    def order_after(self, other):
        self.flying, other.keep = lax.optimization_barrier((self.flying, other.keep))

    def advance(self):
        came, keep = self.flying, self.keep
        if self.reduced < len(self.order):
            half = keep.shape[0] // 2
            self.keep = keep[:half] + came[:half]
            self.flying = exchanged(keep[half:] + came[half:], self.order[self.reduced])
            self.reduced += 1
            return
        if self.spread == len(self.order) - 1:
            self.keep = keep + came
        else:
            self.keep = jnp.concatenate([keep, came], axis=0)
        self.flying = exchanged(self.keep, self.order[self.spread])
        self.spread -= 1


def swapped_cores(arrays):
    return [exchanged(array, 0) for array in arrays]


def chains_of(part, mine, came):
    return [
        Chain(order, mine[2 * k : 2 * k + 2], came[2 * k : 2 * k + 2])
        for k, order in enumerate(part.orders)
    ]


def step_all(chains, last):
    for chain in chains:
        chain.order_after(last)
        chain.advance()
        last = chain
    return last


def finished(chains):
    own = sum([[chain.keep, chain.flying] for chain in chains], [])
    return own + swapped_cores(own)


def piece_places(part, device, core):
    places = []
    for rel_core in range(2):
        base = (core ^ rel_core) * part.half
        for k, (order, size, start) in enumerate(part.paths()):
            own = rearranged(device, order)
            for piece in range(part.pieces):
                number = rel_core * 2 * len(part.orders) + 2 * k + piece // (part.pieces // 2)
                within = piece % (part.pieces // 2) * size
                places.append((number, within, base + start + (piece ^ own) * size, size))
    return places


def put_block(part, packed, number, value, tile=0):
    for t in range(value.shape[1] // LANES):
        block = value[:, LANES * t : LANES * (t + 1)]
        if block.shape[0] < part.rows:
            fill = jnp.zeros((part.rows - block.shape[0], LANES), block.dtype)
            block = jnp.concatenate([block, fill], axis=0)
        at = (part.first[number] + tile + t) * part.per_tile
        packed[at : at + part.per_tile] = block.astype(BF16).reshape(part.per_tile, UNIT, LANES)


def packed_call(
    name, z, part, section, device, choices, direct, body, scratch, flops, lists=(), grouped=0,
    per_group=1,
):
    count, ports = len(choices), len(part.ports())
    buffers, place_of = [], []
    for k, ((array, _), _) in enumerate(choices + sum(lists, [])):
        shape = array.shape[1:]
        member = k % per_group
        if k < grouped and member:
            place_of.append((len(buffers) - 1, member))
            continue
        place_of.append((len(buffers), 0 if k < grouped else None))
        rows = shape[0] * (per_group if k < grouped else 1)
        buffers.append(pltpu.VMEM((rows,) + shape[1:], array.dtype))
    choices = choices + sum(lists, [])

    def kernel(place, *refs):
        ins, refs = refs[: len(direct)], refs[len(direct) :]
        sources, refs = refs[: 2 * len(choices)], refs[2 * len(choices) :]
        halves, refs = (refs[:ports], refs[ports : 2 * ports]), refs[2 * ports :]
        joined, refs = refs[: len(lists)], refs[len(lists) :]
        landed, refs = refs[: len(buffers)], refs[len(buffers) :]
        packed, in_sems, out_sems, joined_sems = refs[:4]
        items = []
        for k, pair in enumerate(choices):
            copies, target = [], landed[place_of[k][0]]
            if place_of[k][1] is not None:
                rows = pair[0][0].shape[1]
                target = target.at[pl.ds(place_of[k][1] * rows, rows)]
            for side, (_, slot) in enumerate(pair):
                copy = pltpu.make_async_copy(
                    sources[2 * k + side].at[slot], target, in_sems.at[k]
                )
                pl.when(place[0] == side)(copy.start)
                copies.append(copy)
            items.append(Item(landed[place_of[k][0]], copies[0], lambda act: act()))
        body(items[:count], ins, packed, *refs[4:])
        if part.units > part.used:
            packed[part.used :] = jnp.zeros((part.units - part.used, UNIT, LANES), BF16)
        copies = []
        core = place[1] & 1
        side = part.pieces // 2
        for rel_core, targets in enumerate(halves):
            base = (core ^ rel_core) * part.half
            for k, (order, size, start) in enumerate(part.paths()):
                own = rearranged(place[1], order)
                for piece in range(part.pieces):
                    copies.append(
                        pltpu.make_async_copy(
                            packed.at[pl.ds(base + start + (piece ^ own) * size, size)],
                            targets[2 * k + piece // side].at[pl.ds(piece % side * size, size)],
                            out_sems.at[len(copies)],
                        )
                    )
                    copies[-1].start()
        at = count
        for k, members in enumerate(lists):
            for i in range(len(members)):
                copies.append(
                    pltpu.make_async_copy(items[at](), joined[k].at[i], joined_sems.at[at - count])
                )
                copies[-1].start()
                at += 1
        for copy in copies:
            copy.wait()

    number = 2 * part.pieces * len(part.orders)
    shapes = [jax.ShapeDtypeStruct((units, UNIT, LANES), BF16) for units in part.ports()]
    anywhere = pl.BlockSpec(memory_space=pl.ANY)
    results = pl.pallas_call(
        kernel,
        in_specs=[pl.BlockSpec(memory_space=pltpu.SMEM)]
        + [pl.BlockSpec(memory_space=pltpu.VMEM)] * len(direct)
        + [anywhere] * (2 * len(choices)),
        out_specs=[anywhere] * (2 * ports + len(lists)),
        out_shape=shapes * 2
        + [
            jax.ShapeDtypeStruct((len(members),) + members[0][0][0].shape[1:], BF16)
            for members in lists
        ],
        scratch_shapes=buffers
        + [
            pltpu.VMEM((part.units, UNIT, LANES), BF16),
            pltpu.SemaphoreType.DMA((len(choices),)),
            pltpu.SemaphoreType.DMA((number,)),
            pltpu.SemaphoreType.DMA((max(len(choices) - count, 1),)),
        ]
        + scratch,
        compiler_params=pltpu.CompilerParams(vmem_limit_bytes=VMEM_BYTES),
        cost_estimate=pl.CostEstimate(flops=flops, bytes_accessed=1 << 23, transcendentals=0),
        name=name,
    )(
        jnp.stack([section, device]).astype(jnp.int32),
        *direct,
        *[array for pair in choices for array, _ in pair],
    )
    return results[:ports], results[ports : 2 * ports], *results[2 * ports :]


def feed_gradients(z, part, section, device, fed, back):
    count = len(fed[0])

    def both_sides(groups, field):
        return [
            tuple((getattr(groups[side][i][0], field), groups[side][i][1]) for side in range(2))
            for i in range(count)
        ]

    fields = (
        both_sides(fed, Fed._fields[1]), both_sides(back, BackFeed._fields[0]),
        both_sides(back, BackFeed._fields[1]), both_sides(fed, Fed._fields[2]),
    )

    def body(items, ins, packed):
        def rows_of(k):
            return [item() for item in items[k * count : (k + 1) * count]][0][...]

        def hidden_columns(number, left, right):
            left = jnp.transpose(left)
            for at in range(0, z.hidden, 512):
                stop = min(at + 512, z.hidden)
                value = dot(left, right[:, at:stop]).astype(BF16)
                short = round_up(stop - at, LANES) - (stop - at)
                if short:
                    fill = jnp.zeros((value.shape[0], short), BF16)
                    value = jnp.concatenate([value, fill], axis=1)
                put_block(part, packed, number, value, at // LANES)

        pre = rows_of(1)
        hidden_columns(0, rows_of(0), pre)
        hidden_columns(1, rows_of(2), rows_of(3))
        wide = round_up(z.hidden, LANES)
        line = jnp.sum(pre.astype(F32), axis=0, keepdims=True)
        line = jnp.concatenate([line, jnp.zeros((1, wide - z.hidden), F32)], axis=1)
        lines = [line[:, LANES * t : LANES * (t + 1)] for t in range(wide // LANES)]
        lines.append(jnp.zeros((UNIT - len(lines), LANES), F32))
        packed[part.extra_at] = jnp.concatenate(lines, axis=0).astype(BF16)

    return packed_call(
        "feed_gradients", z, part, section, device, sum(fields, []), [], body, [], tally(z, 0.4),
        (), 4 * count, count,
    )


def attend_gradients(
    z, part, section, device, table, memory, sources, fed, back_feed, back, lists
):
    count = len(fed[0])

    def both_sides(groups, field):
        return [
            tuple((getattr(groups[side][i][0], field), groups[side][i][1]) for side in range(2))
            for i in range(count)
        ]

    fields = (
        [tuple(sources[side][i] for side in range(2)) for i in range(count)],
        both_sides(back, BackAttend._fields[0]),
        both_sides(back_feed, BackFeed._fields[2]),
        both_sides(fed, Fed._fields[0]),
        [((memory, i), (memory, i)) for i in range(count)],
        both_sides(back, BackAttend._fields[1]),
        both_sides(back, BackAttend._fields[2]),
        both_sides(back, BackAttend._fields[3]),
        both_sides(back_feed, BackFeed._fields[3]),
    )

    def body(items, ins, packed, inputs):
        def refs(k):
            return [item() for item in items[k * count : (k + 1) * count]]

        inputs[...] = jnp.zeros(inputs.shape, BF16)
        for i, ref in enumerate(refs(0)):
            inputs[i, : z.seg, :] = ref[...]
        turned = [jnp.transpose(inputs[i]) for i in range(count)]
        rows_in = jnp.concatenate([inputs[i, : z.rows, :] for i in range(count)], axis=0)
        rows_in = jnp.transpose(rows_in)
        per_half = z.width // LANES
        query, mixed = refs(1), refs(3)
        attend = jnp.transpose(jnp.concatenate([ref[...] for ref in refs(2)], axis=0))
        for half in range(HALVES):
            value = dot(rows_in, jnp.concatenate([ref[half] for ref in query], axis=0))
            put_block(part, packed, 0, value, half * per_half)
            value = dot(attend, jnp.concatenate([ref[half] for ref in mixed], axis=0))
            put_block(part, packed, 3, value, half * per_half)
        memories, key_value = refs(4), refs(5)
        for j in range(2 * HALVES):
            value = None
            for i in range(count):
                grad = dot_nt(memories[i][...], key_value[i][j, :, : z.mem])
                grad = grad + dot_nt(turned[i], key_value[i][j, :, z.mem :])
                value = grad if value is None else value + grad
            put_block(part, packed, 1, value, j * per_half)
        rel = refs(6)
        for half in range(HALVES):
            total = rel[0][half].astype(F32)
            for ref in rel[1:]:
                total = total + ref[half].astype(F32)
            value = dot_nt(ins[0][...], total.astype(BF16))
            put_block(part, packed, 2, value, half * per_half)
        biases, feed = refs(7), refs(8)
        rows = []
        for half in range(HALVES):
            total = biases[0][half]
            for ref in biases[1:]:
                total = total + ref[half]
            rows += [total[:, LANES * t : LANES * (t + 1)] for t in range(per_half)]
        packed[part.extra_at] = jnp.concatenate(
            rows + [jnp.zeros((UNIT - 8 * len(rows), LANES), F32)] * (8 * len(rows) < UNIT), axis=0
        ).astype(BF16)
        total = feed[0][...]
        for ref in feed[1:]:
            total = total + ref[...]
        short = round_up(z.model, LANES) - z.model
        total = jnp.concatenate([total, jnp.zeros((8, short), F32)], axis=1)
        rows = [total[:, LANES * t : LANES * (t + 1)] for t in range(total.shape[1] // LANES)]
        packed[part.extra_at + 1] = jnp.concatenate(
            rows + [jnp.zeros((UNIT - 8 * len(rows), LANES), F32)] * (8 * len(rows) < UNIT), axis=0
        ).astype(BF16)

    return packed_call(
        "attend_gradients", z, part, section, device, sum(fields, []), [table], body,
        [pltpu.VMEM((count, z.recent, z.model), BF16)], tally(z, 0.4), lists,
    )


def half_selection(z, turned=False):
    shape = (HALVES * z.width, z.proj) if turned else (z.proj, HALVES * z.width)
    dense, split = iota(shape, int(turned)), iota(shape, int(not turned))
    within = split % z.width
    same = (split // z.width) * z.used + within == dense
    return jnp.where((within < z.used) & same, 1.0, 0.0).astype(BF16)


def unpack_call(name, z, part, device, arrays, shapes, body):
    number = len(arrays)
    places = 2 * part.pieces * len(part.orders)

    def kernel(place, *refs):
        sources, outs = refs[:number], refs[number:-2]
        buffer, sems = refs[-2:]
        copies = []
        for source, within, at, size in piece_places(part, place[0], place[0] & 1):
            copy = pltpu.make_async_copy(
                sources[source].at[pl.ds(within, size)], buffer.at[pl.ds(at, size)],
                sems.at[len(copies)],
            )
            copy.start()
            copies.append(copy)

        def block(matrix, tile, count):
            tiles = []
            for t in range(part.first[matrix] + tile, part.first[matrix] + tile + count):
                at = t * part.per_tile
                tiles.append(buffer[at : at + part.per_tile].reshape(part.rows, LANES))
            return jnp.concatenate(tiles, axis=1) if count > 1 else tiles[0]

        for copy in copies:
            copy.wait()
        body(block, buffer, *outs)

    return pl.pallas_call(
        kernel,
        in_specs=[pl.BlockSpec(memory_space=pltpu.SMEM)]
        + [pl.BlockSpec(memory_space=pl.ANY)] * number,
        out_shape=[jax.ShapeDtypeStruct(shape, F32) for shape in shapes],
        scratch_shapes=[
            pltpu.VMEM((part.units, UNIT, LANES), BF16), pltpu.SemaphoreType.DMA((places,))
        ],
        compiler_params=pltpu.CompilerParams(vmem_limit_bytes=VMEM_BYTES),
        cost_estimate=pl.CostEstimate(flops=tally(z, 0.2), bytes_accessed=1 << 23, transcendentals=0),
        name=name,
    )(device.reshape(1).astype(jnp.int32), *arrays)


def unpack_feed(z, part, device, arrays):
    def body(block, buffer, inner, outer, inner_bias):
        for number, out in ((0, inner), (1, outer)):
            for at in range(0, z.hidden, 512):
                stop = min(at + 512, z.hidden)
                value = block(number, at // LANES, -(-(stop - at) // LANES)).astype(F32)
                out[:, 0, at:stop] = value[: z.model, : stop - at]
        stacked = buffer[part.extra_at].astype(F32)
        tiles = round_up(z.hidden, LANES) // LANES
        line = jnp.concatenate([stacked[t : t + 1] for t in range(tiles)], axis=1)
        inner_bias[...] = line[:, : z.hidden]

    wide = (z.model, 1, z.hidden)
    inner, outer, inner_bias = unpack_call(
        "unpack_feed", z, part, device, arrays, (wide, wide, (1, z.hidden)), body
    )
    return jnp.transpose(inner, (1, 0, 2)), jnp.transpose(outer, (1, 2, 0)), inner_bias


def unpack_attend(z, part, device, arrays):
    def body(block, buffer, query, key_value, position, output, content_bias, position_bias, *rows):
        spread = half_selection(z)
        wide = HALVES * z.width // LANES
        query[:, 0, :] = dot_nt(block(0, 0, wide), spread)[: z.model]
        position[:, 0, :] = dot_nt(block(2, 0, wide), spread)[: z.model]
        output[:, 0, :] = dot_nt(spread, block(3, 0, wide))[:, : z.model]
        for side in range(2):
            value = dot_nt(block(1, side * wide, wide), spread)[: z.model]
            key_value[:, 0, side * z.proj : (side + 1) * z.proj] = value
        stacked = buffer[part.extra_at].astype(F32)
        sums = jnp.concatenate([stacked[8 * t : 8 * (t + 1)] for t in range(wide)], axis=1)
        sums = dot_nt(sums.astype(BF16), spread)
        content_bias[...] = sums[0:1]
        position_bias[...] = sums[1:2]
        stacked = buffer[part.extra_at + 1].astype(F32)
        tiles = round_up(z.model, LANES) // LANES
        sums = jnp.concatenate([stacked[8 * t : 8 * (t + 1)] for t in range(tiles)], axis=1)
        for k, out in enumerate(rows):
            out[...] = sums[k : k + 1, : z.model]

    square, row = (z.model, 1, z.proj), (1, z.model)
    shapes = (
        square, (z.model, 1, 2 * z.proj), square, (z.proj, 1, z.model), (1, z.proj), (1, z.proj),
        row, row, row, row, row,
    )
    results = unpack_call("unpack_attend", z, part, device, arrays, shapes, body)
    return [jnp.transpose(r, (1, 0, 2)) if r.ndim == 3 else r for r in results]


def frequencies(z):
    exponent = np.arange(0, z.model, 2).astype(np.float32) / np.float32(z.model)
    return np.power(np.float32(10000.0), -exponent).astype(np.float32)[:, None]


def prepare_call(z, query, key_value, position, output, biases, rows):
    farthest = z.keys - 1 + z.shift - z.seg + 1
    number = len(biases)

    def body(rate, query, key_value, position, output, *refs):
        ins, refs = refs[: number + len(rows)], refs[number + len(rows) :]
        query_out, key_value_out, output_out, rel_out, table, lines = refs
        lines[...] = jnp.zeros(lines.shape, F32)
        rest = iota((z.model // 2, LANES), 1).astype(F32)
        near = rate[...] * rest
        far = rate[...] * (farthest - LANES * rest)
        near_sin, near_cos = jnp.sin(near), jnp.cos(near)
        far_sin, far_cos = jnp.sin(far), jnp.cos(far)
        sines, cosines = [], []
        for t in range(z.tiles):
            a, b = far_sin[:, t : t + 1], far_cos[:, t : t + 1]
            sines.append(a * near_cos - b * near_sin)
            cosines.append(b * near_cos + a * near_sin)
        values = [jnp.concatenate(tiles, axis=1) for tiles in (sines, cosines)]
        table[...] = jnp.concatenate(values, axis=0).astype(BF16)
        spread, gather = half_selection(z), half_selection(z, True)
        for half in range(HALVES):
            lanes = slice(half * z.width, (half + 1) * z.width)
            part, turned = spread[:, lanes], gather[lanes, :]
            query_out[half] = dot(query[...], part).astype(BF16)
            output_out[half] = dot(turned, output[...]).astype(BF16)
            wide = dot_nt(turned, position[...]).astype(BF16)
            rel_out[half] = dot(wide, table[...]).astype(BF16)
            for side in range(2):
                own = key_value[:, side * z.proj : (side + 1) * z.proj]
                key_value_out[side * HALVES + half] = dot_nt(turned, own).astype(BF16)
            for k, source in enumerate(ins[:number]):
                at = k * HALVES + half
                lines[at : at + 1, : z.width] = dot(source[...], part)
        for k, source in enumerate(ins[number:]):
            at = number * HALVES + k
            lines[at : at + 1, : source.shape[1]] = source[...].astype(F32)

    shapes = [
        ((HALVES, z.model, z.width), BF16), ((2 * HALVES, z.width, z.model), BF16),
        ((HALVES, z.width, z.model), BF16), ((HALVES, z.width, z.cols), BF16),
        ((z.model, z.cols), BF16), ((Line.count, z.hidden), F32),
    ]
    return pl.pallas_call(
        body,
        out_shape=[jax.ShapeDtypeStruct(s, t) for s, t in shapes],
        compiler_params=pltpu.CompilerParams(vmem_limit_bytes=VMEM_BYTES),
        name="prepare",
    )(frequencies(z), query, key_value, position, output, *biases, *rows)


def unwritten(shapes):
    leaves, tree = jax.tree.flatten(shapes)
    if leaves:
        leaves = pl.pallas_call(
            lambda *refs: None,
            out_shape=leaves,
            out_specs=[pl.BlockSpec(memory_space=pl.ANY)] * len(leaves),
            name="unwritten",
        )()
    return jax.tree.unflatten(tree, leaves)


def moved_along(value, pairs):
    return lax.ppermute(value, "section", pairs)


def shards(
    stream_in, memories, cotangent, query_weight, key_value_matrix, position_weight,
    output_weight, bias_content, bias_position, attend_gain, attend_bias, inner_weight,
    inner_bias, outer_weight, outer_bias, feed_gain, feed_bias,
):
    count, seg_len, model = stream_in.shape
    z = Sizes(seg_len, memories.shape[2], model, query_weight.shape[2], inner_weight.shape[2])
    devices = lax.axis_size("dp")
    section, device = lax.axis_index("section"), lax.axis_index("dp")
    first = section == 0
    memory = jnp.transpose(memories[0], (0, 2, 1))
    made = prepare_call(
        z, query_weight[0], key_value_matrix[0], position_weight[0], output_weight[0],
        [bias_content, bias_position],
        [attend_gain, attend_bias, inner_bias, outer_bias, feed_gain, feed_bias],
    )
    table = made[4]
    weights = Weights(
        made[0], made[1], made[2], made[3], inner_weight[0], jnp.transpose(outer_weight[0]), made[5],
    )

    def shape_of(value):
        return jax.tree.map(lambda a: jax.ShapeDtypeStruct(a.shape, a.dtype), value)

    def pick(first_act, second_act, second_ahead=False):
        made = [jax.eval_shape(act) for act in (first_act, second_act)]

        def blank(side):
            return unwritten(shape_of(made[side][1]))

        def run_first():
            message, rest = first_act()
            if message is None:
                message = unwritten(shape_of(made[1][0]))
            return message, rest, blank(1)

        def run_second():
            message, rest = second_act()
            return message, blank(0), rest

        if second_ahead:
            return lax.cond(first, run_first, run_second)
        return lax.cond(jnp.logical_not(first), run_second, run_first)

    def forwarded(number):
        return (forward_zero, 0) if number == 0 else (forward_rest, number - 1)

    def feed_back(number):
        stored, slot = forwarded(number)
        return feed_back_call(z, weights, grads[number], stored[2], slot)

    def attend_back(number):
        back_first, feed = feeds[number]
        stored, slot = forwarded(number)
        return attend_back_call(z, weights, back_first, feed.attend, stored[1], slot)

    def both(number):
        made = both_call(z, weights, sent[number], 0, memory, cotangent, number)
        return made[1], (made[0],) + made[2:]

    forward_zero, forward_rest = forward_call(z, weights, stream_in, memory, 0, 1), None
    feeds, attends, both_made, grads = [], [], [], []
    sent = [moved_along(forward_zero[0], [(0, 1)])]
    for tick in range(1, count + 1):

        def first_act(tick=tick):
            if tick == 1:
                made = forward_call(z, weights, stream_in, memory, 1, count - 1)
                return made[0][:1], made
            message = forward_rest[0][tick - 1 : tick] if tick < count else None
            feeds.append(feed_back(tick - 2))
            made = feeds[-1], attend_back(tick - 2)
            feeds.pop()
            return message, made

        message, made, second = pick(first_act, lambda tick=tick: both(tick - 1))
        if tick == 1:
            forward_rest = made
        else:
            feeds.append(made[0])
            attends.append(made[1])
        both_made.append((second[0], message) + second[1:])
        came = moved_along(message, [(0, 1), (1, 0)] if tick < count else [(1, 0)])
        sent.append(came)
        grads.append(came)

    feed_part = Part(z, (z.hidden, z.hidden), 1, devices)
    wide = HALVES * z.width
    attend_part = Part(z, (wide, 2 * wide, wide, wide), 2, devices)
    fed = (
        [(stored[3], slot) for stored, slot in map(forwarded, range(count))],
        [(member[2], 0) for member in both_made],
    )
    def attend_back_there(number):
        return pick(lambda: ((), attend_back(number)), lambda: ((), ()))[1]

    final = count - 1
    feeds.append(pick(lambda: ((), feed_back(final)), lambda: ((), ()))[1])
    back_feed = (
        [(feed, 0) for _, feed in feeds], [(member[3], 0) for member in both_made]
    )
    feed_mine, feed_theirs = feed_gradients(z, feed_part, section, device, fed, back_feed)
    feed_chains = chains_of(feed_part, feed_mine, swapped_cores(feed_theirs))
    last = feed_chains[1]
    back_first, last.keep = lax.optimization_barrier((feeds[final][0], last.keep))
    feeds[final] = (back_first, feeds[final][1])
    attend = attend_back_there(final)
    last_grad, feed_chains[0].flying = lax.optimization_barrier(
        (attend[0], feed_chains[0].flying)
    )
    attends.append((last_grad, attend[1]))
    sources = (
        [(stream_in, i) for i in range(count)],
        [(sent[i], 0) for i in range(count)],
    )
    passes = [forwarded(i) for i in range(count)]
    layer_out = [((passes[i][0][0], passes[i][1]), (both_made[i][0], 0)) for i in range(count)]
    input_grad = [((attends[i][0], 0), (both_made[i][1], 0)) for i in range(count)]
    mine, theirs, outputs, input_grads = attend_gradients(
        z, attend_part, section, device, table, memory, sources, fed, back_feed,
        ([(member[1], 0) for member in attends], [(member[4], 0) for member in both_made]),
        (layer_out, input_grad),
    )
    came = swapped_cores(theirs)
    last = step_all(feed_chains, last)
    came[0], last.keep = lax.optimization_barrier((came[0], last.keep))
    attend_chains = chains_of(attend_part, mine, came)
    last = attend_chains[1]
    while feed_chains[0].spread >= 0:
        last = step_all(feed_chains, last)
        last = step_all(attend_chains, last)
    feed_arrays = finished(feed_chains)
    inner, outer, inner_bias_grad = unpack_feed(z, feed_part, device, feed_arrays)
    chain = attend_chains[0]
    chain.flying, inner_bias_grad = lax.optimization_barrier((chain.flying, inner_bias_grad))
    while chain.spread >= 0:
        last = step_all(attend_chains, last)
    attend_arrays = finished(attend_chains)
    (
        query, key_value, position, output, bias_c, bias_p, gain_a, bias_a, bias_o, gain_f, bias_f,
    ) = unpack_attend(z, attend_part, device, attend_arrays)
    return (
        outputs[None], input_grads[None], query, key_value, position, output, bias_c, bias_p,
        gain_a, bias_a, inner, inner_bias_grad, outer, bias_o, gain_f, bias_f,
    )


def solution(mesh):
    stacked, dp = P("section"), P("dp")
    both = P("section", "dp")
    return jax.shard_map(
        shards,
        mesh=mesh,
        in_specs=(dp, both, dp) + (stacked,) * 14,
        out_specs=(both, both) + (stacked,) * 14,
        check_vma=False,
    )
```

```python
from functools import partial
from typing import Any, NamedTuple

import jax
import jax.numpy as jnp
import numpy as np
from jax import lax
from jax.experimental import pallas as pl
from jax.experimental.pallas import tpu as pltpu
from jax.sharding import PartitionSpec as P

HEADS = 10
HALVES = 2
GROUP = HEADS // HALVES
LANES = 128
UNIT = 32
NORM_EPS = 1e-05
GELU_SLOPE = 0.7978845608028654
GELU_CUBIC = 0.044715
MASK_FILL = -1e30
LOG2_E = 1.4426950408889634
F32 = jnp.float32
BF16 = jnp.bfloat16
VMEM_BYTES = 60 * 1024 * 1024


def round_up(value, unit):
    return -(-value // unit) * unit


class Sizes:
    def __init__(self, seg_len, mem_len, model, proj, hidden):
        self.seg, self.mem, self.model, self.proj, self.hidden = seg_len, mem_len, model, proj, hidden
        self.keys = mem_len + seg_len
        self.head = proj // HEADS
        self.rows = round_up(seg_len, 16)
        self.body = seg_len // 16 * 16
        self.tail = self.body + 8
        self.used = GROUP * self.head
        self.width = round_up(self.used, 256)
        self.cols = round_up(self.keys, LANES)
        self.recent = self.cols - mem_len
        self.stack = round_up(GROUP * self.tail, 256)
        self.tail_at = GROUP * self.body
        self.tail_rows = self.stack - self.tail_at
        self.tiles = self.cols // LANES
        self.shift = round_up(seg_len - 1, 8)
        self.scale = self.head ** (-0.5)
        assert self.seg - self.body <= 8 and self.tail_rows % 16 == 0
        assert self.shift == self.tail and self.mem % LANES == 0 and self.shift <= LANES * 2


class Weights(NamedTuple):
    query: Any
    key_value: Any
    output: Any
    rel: Any
    inner: Any
    outer: Any
    lines: Any


class Line:
    bias_content, bias_position = 0, HALVES
    attend_gain, attend_bias, inner_bias, outer_bias, feed_gain, feed_bias = range(
        2 * HALVES, 2 * HALVES + 6
    )
    count = 16


class Kept(NamedTuple):
    attention: Any
    content_stack: Any
    position_stack: Any
    keys: Any
    values: Any
    mixed: Any


class KeptFeed(NamedTuple):
    first_normed: Any
    first_inverse: Any
    second_normed: Any
    second_inverse: Any
    slope: Any


class Fed(NamedTuple):
    mixed_low: Any
    middle: Any
    active: Any


class BackFeed(NamedTuple):
    pre: Any
    outer: Any
    attend: Any
    sums: Any


class BackAttend(NamedTuple):
    query: Any
    key_value: Any
    rel: Any
    sums: Any


def layouts(z):
    halves = lambda rows, cols, kind: ((HALVES, rows, cols), kind)
    kept = Kept(
        halves(z.stack, z.cols, BF16),
        halves(z.stack, z.width, BF16),
        halves(z.stack, z.width, BF16),
        halves(z.width, z.cols, BF16),
        halves(z.width, z.cols, BF16),
        halves(z.rows, z.width, F32),
    )
    wide, narrow = ((z.rows, z.model), F32), ((z.rows, 1), F32)
    kept_feed = KeptFeed(wide, narrow, wide, narrow, ((z.rows, z.hidden), BF16))
    low = ((z.rows, z.model), BF16)
    fed = Fed(halves(z.rows, z.width, BF16), low, ((z.rows, z.hidden), BF16))
    back_feed = BackFeed(((z.rows, z.hidden), BF16), low, low, ((8, z.model), F32))
    back_attend = BackAttend(
        halves(z.rows, z.width, BF16),
        ((2 * HALVES, z.width, z.cols), BF16),
        halves(z.width, z.cols, BF16),
        halves(8, z.width, F32),
    )
    return kept, kept_feed, fed, back_feed, back_attend


def dot(left, right):
    return lax.dot_general(left, right, (((1,), (0,)), ((), ())), preferred_element_type=F32)


def dot_nt(left, right):
    return lax.dot_general(left, right, (((1,), (1,)), ((), ())), preferred_element_type=F32)


def dot_tn(left, right):
    return lax.dot_general(left, right, (((0,), (0,)), ((), ())), preferred_element_type=F32)


def iota(shape, dim):
    return lax.broadcasted_iota(jnp.int32, shape, dim)


class Item:
    def __init__(self, ref, copy=None, once=None):
        self.ref, self.copy, self.once = ref, copy, once

    def __call__(self):
        if self.copy is not None:
            self.once(self.copy.wait)
            self.copy = None
        return self.ref


class Out:
    def __init__(self, ref, target, sems):
        self.ref, self.target, self.sems = ref, target, sems
        self.copies = []

    def part(self, index, slot):
        copy = pltpu.make_async_copy(self.ref.at[index], self.target.at[index], self.sems.at[slot])
        copy.start()
        return copy

    def send(self):
        copy = pltpu.make_async_copy(self.ref, self.target, self.sems.at[0])
        copy.start()
        self.copies.append(copy)


def kernel_call(name, body, direct, fetched, made, scratch, count=1, flops=0):
    made = list(made)
    parts = 4

    def kernel(*refs):
        refs = list(refs)

        def take(number):
            taken = refs[:number]
            del refs[:number]
            return taken

        ins, sources, targets = take(len(direct)), take(len(fetched)), take(len(made))
        landed, built = take(len(fetched)), take(len(made))
        in_sems, out_sems = take(2)
        first = pl.program_id(0) == 0
        once = (lambda act: act()) if count == 1 else (lambda act: pl.when(first)(act))
        items = []
        for k, (ref, (_, slot)) in enumerate(zip(sources, fetched)):
            source = ref if slot is None else ref.at[slot]
            copy = pltpu.make_async_copy(source, landed[k], in_sems.at[k])
            once(copy.start)
            items.append(Item(landed[k], copy, once))
        outs = [
            Out(ref, target.at[pl.program_id(0)], out_sems.at[k])
            for k, (ref, target) in enumerate(zip(built, targets))
        ]
        body(ins, items, outs, *refs)
        for item in items:
            item()
        for out in outs:
            for copy in out.copies:
                copy.wait()

    landing = [
        pltpu.VMEM(array.shape if slot is None else array.shape[1:], array.dtype)
        for array, slot in fetched
    ]
    results = pl.pallas_call(
        kernel,
        grid=(count,),
        in_specs=[spec for _, spec in direct]
        + [pl.BlockSpec(memory_space=pl.ANY)] * len(fetched),
        out_specs=[pl.BlockSpec(memory_space=pl.ANY)] * len(made),
        out_shape=[jax.ShapeDtypeStruct((count,) + tuple(s), t) for s, t in made],
        scratch_shapes=landing
        + [pltpu.VMEM(s, t) for s, t in made]
        + [
            pltpu.SemaphoreType.DMA((max(len(fetched), 1),)),
            pltpu.SemaphoreType.DMA((max(len(made), 1), parts)),
        ]
        + scratch,
        compiler_params=pltpu.CompilerParams(vmem_limit_bytes=VMEM_BYTES),
        cost_estimate=pl.CostEstimate(flops=flops, bytes_accessed=1 << 23, transcendentals=0),
        name=name,
    )(*[array for array, _ in direct], *[array for array, _ in fetched])
    return list(results)


def whole(array):
    zeros = (0,) * array.ndim
    return (array, pl.BlockSpec(array.shape, lambda i: zeros, pipeline_mode=pl.Buffered(1)))


def segment(array, slot):
    zeros = (0,) * (array.ndim - 1)
    return (array, pl.BlockSpec((None,) + array.shape[1:], lambda i: (i + slot,) + zeros))


def head_lanes(z, rows, head):
    lane = iota((rows, z.width), 1)
    return (lane >= z.head * head) & (lane < z.head * (head + 1))


def stack_heads(z, target, source):
    tails = []
    for head in range(GROUP):
        own = jnp.where(head_lanes(z, z.tail, head), source[: z.tail], 0.0)
        target[z.body * head : z.body * (head + 1), :] = own[: z.body].astype(BF16)
        tails.append(own[z.body :])
    tails.append(jnp.zeros((z.tail_rows - 8 * GROUP, z.width), F32))
    target[z.tail_at :, :] = jnp.concatenate(tails, axis=0).astype(BF16)


def unstack_heads(z, source):
    total = None
    for head in range(GROUP):
        rows = jnp.concatenate(
            [
                source[z.body * head : z.body * (head + 1)],
                source[z.tail_at + 8 * head : z.tail_at + 8 * (head + 1)],
            ],
            axis=0,
        )
        own = jnp.where(head_lanes(z, z.tail, head), rows, 0.0)
        total = own if total is None else total + own
    return total


def normalize(values):
    centered = values - jnp.mean(values, axis=-1, keepdims=True)
    variance = jnp.mean(centered * centered, axis=-1, keepdims=True)
    inverse = lax.rsqrt(variance + NORM_EPS)
    return (centered * inverse, inverse)


def normalize_back(grad_normed, normed, inverse):
    return inverse * (
        grad_normed
        - jnp.mean(grad_normed, axis=-1, keepdims=True)
        - normed * jnp.mean(grad_normed * normed, axis=-1, keepdims=True)
    )


def shifted_tiles(z, tiles, first_row):
    base = (first_row - z.shift) % LANES
    turns = (first_row - z.shift - base) // LANES
    lane, row = iota((8, LANES), 1), iota((8, LANES), 0)
    turned = [pltpu.roll(tile, base, 1, stride=1, stride_axis=0) for tile in tiles]
    kept = lane >= base + row
    return [
        jnp.where(kept, turned[(t - turns) % z.tiles], turned[(t - turns - 1) % z.tiles])
        for t in range(z.tiles)
    ]


def restored_tiles(z, tiles, first_row):
    lane, row = iota((8, LANES), 1), iota((8, LANES), 0)
    amount = z.shift - first_row
    place = (lane - amount + row) % LANES
    turned = [jnp.take_along_axis(tile, place, axis=1) for tile in tiles]
    base, turns = amount % LANES, amount // LANES
    if base >= 8:
        kept, other = lane >= base - row, -1
    else:
        assert base == 0
        kept, other = lane < LANES - row, 1
    return [
        jnp.where(kept, turned[(t - turns) % z.tiles], turned[(t - turns + other) % z.tiles])
        for t in range(z.tiles)
    ]


def split_tiles(z, block):
    return [block[:, LANES * t : LANES * (t + 1)] for t in range(z.tiles)]


def over_rows(z, chunk):
    for head in range(GROUP):
        for part in range(z.body // 16):
            chunk(head * z.body + 16 * part, 16 * part, 16 * part + 8)
    for part in range(z.tail_rows // 16):
        chunk(z.tail_at + 16 * part, z.body, z.body)


def attention_rows(z, content, position, attention):
    def chunk(row, first, second):
        for at, query in ((row, first), (row + 8, second)):
            rows = slice(at, at + 8)
            moved = shifted_tiles(z, split_tiles(z, position[rows, :]), query)
            for t in range(z.tiles):
                lanes = slice(LANES * t, LANES * (t + 1))
                scores = content[rows, lanes] + moved[t]
                if t >= z.mem // LANES:
                    ahead = iota((8, LANES), 1) - iota((8, LANES), 0)
                    allowed = ahead <= z.mem + query - LANES * t
                    scores = jnp.where(allowed, scores, MASK_FILL)
                content[rows, lanes] = scores

    over_rows(z, chunk)
    scores = content[...]
    largest = jnp.max(scores, axis=-1, keepdims=True)
    powers = jnp.exp2((scores - largest) * (z.scale * LOG2_E))
    inverse = 1.0 / jnp.sum(powers, axis=-1, keepdims=True)
    attention[...] = (powers * inverse).astype(BF16)


def attention_rows_back(z, attention, back_map, weighted, back_raw, back_table):
    def chunk(row, first, second):
        rows = slice(row, row + 16)
        inner = weighted[rows, :]
        tops, lows = [], []
        for t in range(z.tiles):
            lanes = slice(LANES * t, LANES * (t + 1))
            raw = attention[rows, lanes].astype(F32) * ((back_map[rows, lanes] - inner) * z.scale)
            back_raw[rows, lanes] = raw.astype(BF16)
            tops.append(raw[:8])
            lows.append(raw[8:])
        tops, lows = restored_tiles(z, tops, first), restored_tiles(z, lows, second)
        for t in range(z.tiles):
            pair = jnp.concatenate([tops[t], lows[t]], axis=0).astype(BF16)
            back_table[rows, LANES * t : LANES * (t + 1)] = pair

    over_rows(z, chunk)


def gelu_and_slope(values):
    squared = values * values
    tangent = jnp.tanh(GELU_SLOPE * (values + GELU_CUBIC * squared * values))
    half = 0.5 * (1.0 + tangent)
    slope = half + 0.5 * values * (1.0 - tangent * tangent) * GELU_SLOPE * (
        1.0 + 3.0 * GELU_CUBIC * squared
    )
    return (values * half, slope)


def forward_body(
    z, w, source, memory, kept, kept_feed, fed, result, hidden, content, position, attention_done
):
    hidden[...] = jnp.zeros(hidden.shape, BF16)
    hidden[: z.seg, :] = source[...]
    for j in range(2 * HALVES):
        target = (kept.keys if j < HALVES else kept.values).at[j % HALVES]
        target[:, : z.mem] = dot(w.key_value()[j], memory[...]).astype(BF16)
        target[:, z.mem :] = dot_nt(w.key_value()[j], hidden[...]).astype(BF16)
    rows_in = hidden[: z.rows, :]
    real = iota((z.rows, 1), 0) < z.seg
    lines = w.lines()
    line = lambda number: lines[number : number + 1, : z.model]
    for half in range(HALVES):
        raw = dot(rows_in, w.query()[half])
        for stack, number in (
            (kept.content_stack, Line.bias_content), (kept.position_stack, Line.bias_position)
        ):
            bias = lines[number + half : number + half + 1, : z.width]
            stack_heads(z, stack.at[half], jnp.where(real, raw + bias, 0.0))
    rel = w.rel()

    def one_half(half, carry):
        content[...] = dot(kept.content_stack[half], kept.keys[half])
        position[...] = dot(kept.position_stack[half], rel[half])
        attention_rows(z, content, position, kept.attention.at[half])
        mixed = unstack_heads(z, dot_nt(kept.attention[half], kept.values[half]))
        kept.mixed[half, : z.tail, :] = mixed
        kept.mixed[half, z.tail :, :] = jnp.zeros((z.rows - z.tail, z.width), F32)
        return carry

    lax.fori_loop(0, HALVES, one_half, 0)
    attention_done()
    total = rows_in.astype(F32)
    for half in range(HALVES):
        mixed = kept.mixed[half].astype(BF16)
        fed.mixed_low[half] = mixed
        total = total + dot(mixed, w.output()[half])
    normed, inverse = normalize(total)
    kept_feed.first_normed[...] = normed
    kept_feed.first_inverse[...] = inverse
    middle = (normed * line(Line.attend_gain) + line(Line.attend_bias)).astype(BF16)
    fed.middle[...] = middle
    active, slope = gelu_and_slope(
        dot(middle, w.inner()[...]) + lines[Line.inner_bias : Line.inner_bias + 1, :]
    )
    kept_feed.slope[...] = slope.astype(BF16)
    active = active.astype(BF16)
    fed.active[...] = active
    feed = dot_nt(active, w.outer()[...]) + line(Line.outer_bias)
    normed, inverse = normalize(middle.astype(F32) + feed)
    kept_feed.second_normed[...] = normed
    kept_feed.second_inverse[...] = inverse
    out = (normed * line(Line.feed_gain) + line(Line.feed_bias)).astype(BF16)
    result[...] = out[: z.seg]


def feed_back_body(z, w, grad_in, kept, back, back_first, top):
    top[...] = jnp.zeros(top.shape, BF16)
    top[: z.seg, :] = grad_in[...]
    grad_top = top[...].astype(F32)
    lines = w.lines()
    line = lambda number: lines[number : number + 1, : z.model]
    normed = kept.second_normed()[...]
    second = normalize_back(
        grad_top * line(Line.feed_gain), normed, kept.second_inverse()[...]
    )
    outer = second.astype(BF16)
    back.outer[...] = outer
    pre = (dot(outer, w.outer()[...]) * kept.slope()[...].astype(F32)).astype(BF16)
    back.pre[...] = pre
    middle = second + dot_nt(pre, w.inner()[...])
    first_normed = kept.first_normed()[...]
    first = normalize_back(
        middle * line(Line.attend_gain), first_normed, kept.first_inverse()[...]
    )
    back_first[...] = first
    back.attend[...] = first.astype(BF16)
    sums = back.sums
    sums[...] = jnp.zeros(sums.shape, F32)
    rows = (middle * first_normed, middle, outer.astype(F32), grad_top * normed, grad_top)
    for k, values in enumerate(rows):
        sums[k : k + 1, :] = jnp.sum(values, axis=0, keepdims=True)


def attend_back_body(
    z, w, kept, back_first, back_attend, back, send, input_grad, stack, back_map, weighted, raw, table
):
    refs = Kept(*[item() for item in kept])
    output, rel = w.output(), w.rel()

    def one_half(half, carry):
        own = dot_nt(back_attend[...], output[half]).astype(BF16).astype(F32)
        stack_heads(z, stack, own)
        product = own[: z.tail] * refs.mixed[half, : z.tail, :]
        weighted[z.tail_at :, :] = jnp.zeros((z.tail_rows, 1), F32)
        for head in range(GROUP):
            inner = jnp.where(head_lanes(z, z.tail, head), product, 0.0)
            inner = jnp.sum(inner, axis=1, keepdims=True)
            weighted[z.body * head : z.body * (head + 1), :] = inner[: z.body]
            at = z.tail_at + 8 * head
            weighted[at : at + 8, :] = inner[z.body :]
        back_map[...] = dot(stack[...], refs.values[half])
        attention_rows_back(z, refs.attention.at[half], back_map, weighted, raw, table)
        back.key_value[half] = dot_tn(refs.content_stack[half], raw[...]).astype(BF16)
        back.key_value[HALVES + half] = dot_tn(stack[...], refs.attention[half]).astype(BF16)
        back.rel[half] = dot_tn(refs.position_stack[half], table[...]).astype(BF16)
        send(half)
        from_content = unstack_heads(z, dot_nt(raw[...], refs.keys[half]))
        from_position = unstack_heads(z, dot_nt(table[...], rel[half]))
        back.query[half, : z.tail, :] = (from_content + from_position).astype(BF16)
        back.query[half, z.tail :, :] = jnp.zeros((z.rows - z.tail, z.width), BF16)
        back.sums[half] = jnp.concatenate(
            [
                jnp.sum(from_content, axis=0, keepdims=True),
                jnp.sum(from_position, axis=0, keepdims=True),
                jnp.zeros((6, z.width), F32),
            ],
            axis=0,
        )
        return carry

    lax.fori_loop(0, HALVES, one_half, 0)
    total = back_first[...]
    for half in range(HALVES):
        total = total + dot_nt(back.query[half], w.query()[half])
    for j in range(2 * HALVES):
        recent = dot_tn(back.key_value[j, :, z.mem :], w.key_value()[j])
        total = total + recent[: z.rows]
    input_grad[...] = total[: z.seg].astype(BF16)


def back_scratch(z):
    return [
        pltpu.VMEM((z.stack, z.width), BF16),
        pltpu.VMEM((z.stack, z.cols), F32),
        pltpu.VMEM((z.stack, 1), F32),
        pltpu.VMEM((z.stack, z.cols), BF16),
        pltpu.VMEM((z.stack, z.cols), BF16),
    ]


def vmem(entries):
    return [pltpu.VMEM(s, t) for s, t in entries]


def tally(z, passes):
    return int(passes * 2e10)


ARRIVAL = (1, 6, 0, 3, 2, 4, 5)


def arriving(weights):
    return [(weights[k], None) for k in ARRIVAL]


def arrived_weights(items):
    own = dict(zip(ARRIVAL, items))
    return Weights(*[own[k] for k in range(len(ARRIVAL))])


def refs_of(kind, outs):
    return kind(*[out.ref for out in outs])


def send_all(outs):
    for out in outs:
        out.send()


def attend_sender(outs):
    query, key_value, rel, sums = outs

    def parts(half):
        yield key_value, half, half
        yield key_value, HALVES + half, HALVES + half
        yield rel, half, half

    def send(half):
        for out, index, slot in parts(half):
            out.part(index, slot)

    def finish():
        for half in range(HALVES):
            for out, index, slot in parts(half):
                pltpu.make_async_copy(
                    out.ref.at[index], out.target.at[index], out.sems.at[slot]
                ).wait()

    return send, finish


@partial(jax.jit, static_argnums=(0, 4, 5))
def forward_call(z, weights, source, memory, slot, count):
    kept, kept_feed, fed = layouts(z)[:3]
    direct = [segment(source, slot), segment(memory, slot)]

    def body(ins, items, outs, hidden, content, position):
        result, outs = outs[0], outs[1:]
        forward_body(
            z, arrived_weights(items), ins[0], ins[1], refs_of(Kept, outs[:6]),
            refs_of(KeptFeed, outs[6:11]), refs_of(Fed, outs[11:]), result.ref, hidden, content,
            position, lambda: send_all(outs[:6]),
        )
        send_all([result] + outs[6:])

    made = [((z.seg, z.model), BF16), *kept, *kept_feed, *fed]
    results = kernel_call(
        "forward", body, direct, arriving(weights), made,
        [
            pltpu.VMEM((z.recent, z.model), BF16),
            pltpu.VMEM((z.stack, z.cols), F32),
            pltpu.VMEM((z.stack, z.cols), F32),
        ],
        count, tally(z, count),
    )
    return results[0], Kept(*results[1:7]), KeptFeed(*results[7:12]), Fed(*results[12:])


@partial(jax.jit, static_argnums=(0, 3, 6))
def both_call(z, weights, source, source_slot, memory, grad_in, slot):
    kept, kept_feed, fed, back_feed, back_attend = layouts(z)
    fetched = [(source, source_slot), (memory, slot)] + arriving(weights) + [(grad_in, slot)]

    def body(ins, items, outs, hidden, content, position, *scratch):
        w = arrived_weights(items[2:-1])
        result, input_grad = outs[:2]
        fed_outs, feed_outs, attend_outs = outs[2:5], outs[5:9], outs[9:13]
        held, held_feed = Kept(*scratch[:6]), KeptFeed(*scratch[6:11])
        first, top, stack, weighted, raw, table = scratch[11:]
        forward_body(
            z, w, items[0](), items[1](), held, held_feed, refs_of(Fed, fed_outs), result.ref,
            hidden, content, position, lambda: None,
        )
        send_all([result] + fed_outs)
        feed_refs = refs_of(BackFeed, feed_outs)
        feed_back_body(
            z, w, items[-1](), KeptFeed(*[Item(ref) for ref in held_feed]), feed_refs, first, top
        )
        send_all(feed_outs)
        send, finish = attend_sender(attend_outs)
        attend_back_body(
            z, w, Kept(*[Item(ref) for ref in held]), first, feed_refs.attend,
            refs_of(BackAttend, attend_outs), send, input_grad.ref, stack, content, weighted,
            raw, table,
        )
        send_all([input_grad, attend_outs[0], attend_outs[3]])
        finish()

    row = ((z.seg, z.model), BF16)
    scratch = back_scratch(z)
    del scratch[1]
    results = kernel_call(
        "forward_backward", body, [], fetched, [row, row, *fed, *back_feed, *back_attend],
        [
            pltpu.VMEM((z.recent, z.model), BF16),
            pltpu.VMEM((z.stack, z.cols), F32),
            pltpu.VMEM((z.stack, z.cols), F32),
        ]
        + vmem(kept)
        + vmem(kept_feed)
        + [pltpu.VMEM((z.rows, z.model), F32), pltpu.VMEM((z.rows, z.model), BF16)]
        + scratch,
        1, tally(z, 2),
    )
    return (
        results[0], results[1], Fed(*results[2:5]), BackFeed(*results[5:9]),
        BackAttend(*results[9:13]),
    )


@partial(jax.jit, static_argnums=(0, 4))
def feed_back_call(z, weights, grad_in, kept, slot):
    back_feed = layouts(z)[3]
    fetched = [(weights.lines, None)]
    fetched += [(a, slot) for a in (kept.second_normed, kept.second_inverse)]
    fetched += [(weights.outer, None), (kept.slope, slot), (weights.inner, None)]
    fetched += [(a, slot) for a in (kept.first_normed, kept.first_inverse)]

    def body(ins, items, outs, top):
        lines, second_normed, second_inverse, outer, slope, inner, first_normed, first_inverse = items
        w = Weights(*[None] * 4, inner, outer, lines)
        held = KeptFeed(first_normed, first_inverse, second_normed, second_inverse, slope)
        feed_back_body(z, w, ins[0], held, refs_of(BackFeed, outs[1:]), outs[0].ref, top)
        send_all(outs)

    results = kernel_call(
        "feed_backward", body, [segment(grad_in, 0)], fetched,
        [((z.rows, z.model), F32), *back_feed], [pltpu.VMEM((z.rows, z.model), BF16)],
        1, tally(z, 0.3),
    )
    return results[0], BackFeed(*results[1:])


@partial(jax.jit, static_argnums=(0, 5))
def attend_back_call(z, weights, back_first, back_attend, kept, slot):
    fetched = [(back_first, 0), (back_attend, 0), (weights.output, None)]
    fetched += [(array, slot) for array in kept]
    fetched += [(a, None) for a in (weights.rel, weights.query, weights.key_value)]

    def body(ins, items, outs, *scratch):
        first, attend, output = items[:3]
        rel, query, key_value = items[9:]
        w = Weights(query, key_value, output, rel, *[None] * 3)
        send, finish = attend_sender(outs[1:])
        attend_back_body(
            z, w, Kept(*items[3:9]), first(), attend(), refs_of(BackAttend, outs[1:]), send,
            outs[0].ref, *scratch,
        )
        send_all([outs[0], outs[1], outs[4]])
        finish()

    results = kernel_call(
        "attend_backward", body, [], fetched, [((z.seg, z.model), BF16), *layouts(z)[4]],
        back_scratch(z), 1, tally(z, 0.7),
    )
    return results[0], BackAttend(*results[1:])


class Part:
    def __init__(self, z, widths, extra, devices):
        self.rows = round_up(z.model, UNIT)
        self.per_tile = self.rows // UNIT
        self.first, at = [], 0
        for width in widths:
            self.first.append(at)
            at += round_up(width, LANES) // LANES
        self.extra_at = at * self.per_tile
        self.used = self.extra_at + extra
        bits = devices.bit_length() - 1
        assert devices == 1 << bits and bits >= 3
        order = list(range(1, bits))
        self.orders = (order, [order[1], order[0]] + order[2:])
        self.pieces = devices // 2
        per_piece = -(-self.used // devices)
        self.sizes = (-(-per_piece // 2), per_piece // 2)
        self.starts = (0, self.pieces * self.sizes[0])
        self.half = self.pieces * per_piece
        self.units = 2 * self.half

    def paths(self):
        return list(zip(self.orders, self.sizes, self.starts))

    def ports(self):
        return [self.pieces // 2 * size for size in self.sizes for _ in range(2)]


def rearranged(index, order):
    total = 0
    for place, bit in enumerate(reversed(order)):
        total = total + (((index >> bit) & 1) << place)
    return total


def exchanged(array, bit):
    count = lax.axis_size("dp")
    return lax.ppermute(array, "dp", [(i, i ^ (1 << bit)) for i in range(count)])


class Chain:
    def __init__(self, order, mine, came):
        self.order, self.reduced, self.spread = order, 1, len(order) - 1
        self.keep = mine[0] + came[0]
        self.flying = exchanged(mine[1] + came[1], order[0])

    def order_after(self, other):
        self.flying, other.keep = lax.optimization_barrier((self.flying, other.keep))

    def advance(self):
        came, keep = self.flying, self.keep
        if self.reduced < len(self.order):
            half = keep.shape[0] // 2
            self.keep = keep[:half] + came[:half]
            self.flying = exchanged(keep[half:] + came[half:], self.order[self.reduced])
            self.reduced += 1
            return
        if self.spread == len(self.order) - 1:
            self.keep = keep + came
        else:
            self.keep = jnp.concatenate([keep, came], axis=0)
        self.flying = exchanged(self.keep, self.order[self.spread])
        self.spread -= 1


def swapped_cores(arrays):
    return [exchanged(array, 0) for array in arrays]


def chains_of(part, mine, came):
    return [
        Chain(order, mine[2 * k : 2 * k + 2], came[2 * k : 2 * k + 2])
        for k, order in enumerate(part.orders)
    ]


def step_all(chains, last):
    for chain in chains:
        chain.order_after(last)
        chain.advance()
        last = chain
    return last


def finished(chains):
    own = sum([[chain.keep, chain.flying] for chain in chains], [])
    return own + swapped_cores(own)


def piece_places(part, device, core):
    places = []
    for rel_core in range(2):
        base = (core ^ rel_core) * part.half
        for k, (order, size, start) in enumerate(part.paths()):
            own = rearranged(device, order)
            for piece in range(part.pieces):
                number = rel_core * 2 * len(part.orders) + 2 * k + piece // (part.pieces // 2)
                within = piece % (part.pieces // 2) * size
                places.append((number, within, base + start + (piece ^ own) * size, size))
    return places


def put_block(part, packed, number, value, tile=0):
    for t in range(value.shape[1] // LANES):
        block = value[:, LANES * t : LANES * (t + 1)]
        if block.shape[0] < part.rows:
            fill = jnp.zeros((part.rows - block.shape[0], LANES), block.dtype)
            block = jnp.concatenate([block, fill], axis=0)
        at = (part.first[number] + tile + t) * part.per_tile
        packed[at : at + part.per_tile] = block.astype(BF16).reshape(part.per_tile, UNIT, LANES)


def packed_call(
    name, z, part, section, device, choices, direct, body, scratch, flops, lists=(), grouped=0,
    per_group=1,
):
    count, ports = len(choices), len(part.ports())
    buffers, place_of = [], []
    for k, ((array, _), _) in enumerate(choices + sum(lists, [])):
        shape = array.shape[1:]
        member = k % per_group
        if k < grouped and member:
            place_of.append((len(buffers) - 1, member))
            continue
        place_of.append((len(buffers), 0 if k < grouped else None))
        rows = shape[0] * (per_group if k < grouped else 1)
        buffers.append(pltpu.VMEM((rows,) + shape[1:], array.dtype))
    choices = choices + sum(lists, [])

    def kernel(place, *refs):
        ins, refs = refs[: len(direct)], refs[len(direct) :]
        sources, refs = refs[: 2 * len(choices)], refs[2 * len(choices) :]
        halves, refs = (refs[:ports], refs[ports : 2 * ports]), refs[2 * ports :]
        joined, refs = refs[: len(lists)], refs[len(lists) :]
        landed, refs = refs[: len(buffers)], refs[len(buffers) :]
        packed, in_sems, out_sems, joined_sems = refs[:4]
        items = []
        for k, pair in enumerate(choices):
            copies, target = [], landed[place_of[k][0]]
            if place_of[k][1] is not None:
                rows = pair[0][0].shape[1]
                target = target.at[pl.ds(place_of[k][1] * rows, rows)]
            for side, (_, slot) in enumerate(pair):
                copy = pltpu.make_async_copy(
                    sources[2 * k + side].at[slot], target, in_sems.at[k]
                )
                pl.when(place[0] == side)(copy.start)
                copies.append(copy)
            items.append(Item(landed[place_of[k][0]], copies[0], lambda act: act()))
        body(items[:count], ins, packed, *refs[4:])
        if part.units > part.used:
            packed[part.used :] = jnp.zeros((part.units - part.used, UNIT, LANES), BF16)
        copies = []
        core = place[1] & 1
        side = part.pieces // 2
        for rel_core, targets in enumerate(halves):
            base = (core ^ rel_core) * part.half
            for k, (order, size, start) in enumerate(part.paths()):
                own = rearranged(place[1], order)
                for piece in range(part.pieces):
                    copies.append(
                        pltpu.make_async_copy(
                            packed.at[pl.ds(base + start + (piece ^ own) * size, size)],
                            targets[2 * k + piece // side].at[pl.ds(piece % side * size, size)],
                            out_sems.at[len(copies)],
                        )
                    )
                    copies[-1].start()
        at = count
        for k, members in enumerate(lists):
            for i in range(len(members)):
                copies.append(
                    pltpu.make_async_copy(items[at](), joined[k].at[i], joined_sems.at[at - count])
                )
                copies[-1].start()
                at += 1
        for copy in copies:
            copy.wait()

    number = 2 * part.pieces * len(part.orders)
    shapes = [jax.ShapeDtypeStruct((units, UNIT, LANES), BF16) for units in part.ports()]
    anywhere = pl.BlockSpec(memory_space=pl.ANY)
    results = pl.pallas_call(
        kernel,
        in_specs=[pl.BlockSpec(memory_space=pltpu.SMEM)]
        + [pl.BlockSpec(memory_space=pltpu.VMEM)] * len(direct)
        + [anywhere] * (2 * len(choices)),
        out_specs=[anywhere] * (2 * ports + len(lists)),
        out_shape=shapes * 2
        + [
            jax.ShapeDtypeStruct((len(members),) + members[0][0][0].shape[1:], BF16)
            for members in lists
        ],
        scratch_shapes=buffers
        + [
            pltpu.VMEM((part.units, UNIT, LANES), BF16),
            pltpu.SemaphoreType.DMA((len(choices),)),
            pltpu.SemaphoreType.DMA((number,)),
            pltpu.SemaphoreType.DMA((max(len(choices) - count, 1),)),
        ]
        + scratch,
        compiler_params=pltpu.CompilerParams(vmem_limit_bytes=VMEM_BYTES),
        cost_estimate=pl.CostEstimate(flops=flops, bytes_accessed=1 << 23, transcendentals=0),
        name=name,
    )(
        jnp.stack([section, device]).astype(jnp.int32),
        *direct,
        *[array for pair in choices for array, _ in pair],
    )
    return results[:ports], results[ports : 2 * ports], *results[2 * ports :]


def feed_gradients(z, part, section, device, fed, back):
    count = len(fed[0])

    def both_sides(groups, field):
        return [
            tuple((getattr(groups[side][i][0], field), groups[side][i][1]) for side in range(2))
            for i in range(count)
        ]

    fields = (
        both_sides(fed, Fed._fields[1]), both_sides(back, BackFeed._fields[0]),
        both_sides(back, BackFeed._fields[1]), both_sides(fed, Fed._fields[2]),
    )

    def body(items, ins, packed):
        def rows_of(k):
            return [item() for item in items[k * count : (k + 1) * count]][0][...]

        def hidden_columns(number, left, right):
            left = jnp.transpose(left)
            for at in range(0, z.hidden, 512):
                stop = min(at + 512, z.hidden)
                value = dot(left, right[:, at:stop]).astype(BF16)
                short = round_up(stop - at, LANES) - (stop - at)
                if short:
                    fill = jnp.zeros((value.shape[0], short), BF16)
                    value = jnp.concatenate([value, fill], axis=1)
                put_block(part, packed, number, value, at // LANES)

        pre = rows_of(1)
        hidden_columns(0, rows_of(0), pre)
        hidden_columns(1, rows_of(2), rows_of(3))
        wide = round_up(z.hidden, LANES)
        line = jnp.sum(pre.astype(F32), axis=0, keepdims=True)
        line = jnp.concatenate([line, jnp.zeros((1, wide - z.hidden), F32)], axis=1)
        lines = [line[:, LANES * t : LANES * (t + 1)] for t in range(wide // LANES)]
        lines.append(jnp.zeros((UNIT - len(lines), LANES), F32))
        packed[part.extra_at] = jnp.concatenate(lines, axis=0).astype(BF16)

    return packed_call(
        "feed_gradients", z, part, section, device, sum(fields, []), [], body, [], tally(z, 0.4),
        (), 4 * count, count,
    )


def attend_gradients(
    z, part, section, device, table, memory, sources, fed, back_feed, back, lists
):
    count = len(fed[0])

    def both_sides(groups, field):
        return [
            tuple((getattr(groups[side][i][0], field), groups[side][i][1]) for side in range(2))
            for i in range(count)
        ]

    fields = (
        [tuple(sources[side][i] for side in range(2)) for i in range(count)],
        both_sides(back, BackAttend._fields[0]),
        both_sides(back_feed, BackFeed._fields[2]),
        both_sides(fed, Fed._fields[0]),
        [((memory, i), (memory, i)) for i in range(count)],
        both_sides(back, BackAttend._fields[1]),
        both_sides(back, BackAttend._fields[2]),
        both_sides(back, BackAttend._fields[3]),
        both_sides(back_feed, BackFeed._fields[3]),
    )

    def body(items, ins, packed, inputs):
        def refs(k):
            return [item() for item in items[k * count : (k + 1) * count]]

        inputs[...] = jnp.zeros(inputs.shape, BF16)
        for i, ref in enumerate(refs(0)):
            inputs[i, : z.seg, :] = ref[...]
        turned = [jnp.transpose(inputs[i]) for i in range(count)]
        rows_in = jnp.concatenate([inputs[i, : z.rows, :] for i in range(count)], axis=0)
        rows_in = jnp.transpose(rows_in)
        per_half = z.width // LANES
        query, mixed = refs(1), refs(3)
        attend = jnp.transpose(jnp.concatenate([ref[...] for ref in refs(2)], axis=0))
        for half in range(HALVES):
            value = dot(rows_in, jnp.concatenate([ref[half] for ref in query], axis=0))
            put_block(part, packed, 0, value, half * per_half)
            value = dot(attend, jnp.concatenate([ref[half] for ref in mixed], axis=0))
            put_block(part, packed, 3, value, half * per_half)
        memories, key_value = refs(4), refs(5)
        value = None
        for i in range(count):
            made = key_value[i][...].reshape(2 * HALVES * z.width, z.cols)
            grad = dot_nt(memories[i][...], made[:, : z.mem])
            grad = grad + dot_nt(turned[i], made[:, z.mem :])
            value = grad if value is None else value + grad
        put_block(part, packed, 1, value)
        rel = refs(6)
        for half in range(HALVES):
            total = rel[0][half].astype(F32)
            for ref in rel[1:]:
                total = total + ref[half].astype(F32)
            value = dot_nt(ins[0][...], total.astype(BF16))
            put_block(part, packed, 2, value, half * per_half)
        biases, feed = refs(7), refs(8)
        rows = []
        for half in range(HALVES):
            total = biases[0][half]
            for ref in biases[1:]:
                total = total + ref[half]
            rows += [total[:, LANES * t : LANES * (t + 1)] for t in range(per_half)]
        packed[part.extra_at] = jnp.concatenate(
            rows + [jnp.zeros((UNIT - 8 * len(rows), LANES), F32)] * (8 * len(rows) < UNIT), axis=0
        ).astype(BF16)
        total = feed[0][...]
        for ref in feed[1:]:
            total = total + ref[...]
        short = round_up(z.model, LANES) - z.model
        total = jnp.concatenate([total, jnp.zeros((8, short), F32)], axis=1)
        rows = [total[:, LANES * t : LANES * (t + 1)] for t in range(total.shape[1] // LANES)]
        packed[part.extra_at + 1] = jnp.concatenate(
            rows + [jnp.zeros((UNIT - 8 * len(rows), LANES), F32)] * (8 * len(rows) < UNIT), axis=0
        ).astype(BF16)

    return packed_call(
        "attend_gradients", z, part, section, device, sum(fields, []), [table], body,
        [pltpu.VMEM((count, z.recent, z.model), BF16)], tally(z, 0.4), lists,
    )


def half_selection(z, turned=False):
    shape = (HALVES * z.width, z.proj) if turned else (z.proj, HALVES * z.width)
    dense, split = iota(shape, int(turned)), iota(shape, int(not turned))
    within = split % z.width
    same = (split // z.width) * z.used + within == dense
    return jnp.where((within < z.used) & same, 1.0, 0.0).astype(BF16)


def unpack_call(name, z, part, device, arrays, shapes, body):
    number = len(arrays)
    places = 2 * part.pieces * len(part.orders)

    def kernel(place, *refs):
        sources, outs = refs[:number], refs[number:-2]
        buffer, sems = refs[-2:]
        copies = []
        for source, within, at, size in piece_places(part, place[0], place[0] & 1):
            copy = pltpu.make_async_copy(
                sources[source].at[pl.ds(within, size)], buffer.at[pl.ds(at, size)],
                sems.at[len(copies)],
            )
            copy.start()
            copies.append(copy)

        def block(matrix, tile, count):
            tiles = []
            for t in range(part.first[matrix] + tile, part.first[matrix] + tile + count):
                at = t * part.per_tile
                tiles.append(buffer[at : at + part.per_tile].reshape(part.rows, LANES))
            return jnp.concatenate(tiles, axis=1) if count > 1 else tiles[0]

        for copy in copies:
            copy.wait()
        body(block, buffer, *outs)

    return pl.pallas_call(
        kernel,
        in_specs=[pl.BlockSpec(memory_space=pltpu.SMEM)]
        + [pl.BlockSpec(memory_space=pl.ANY)] * number,
        out_shape=[jax.ShapeDtypeStruct(shape, F32) for shape in shapes],
        scratch_shapes=[
            pltpu.VMEM((part.units, UNIT, LANES), BF16), pltpu.SemaphoreType.DMA((places,))
        ],
        compiler_params=pltpu.CompilerParams(vmem_limit_bytes=VMEM_BYTES),
        cost_estimate=pl.CostEstimate(flops=tally(z, 0.2), bytes_accessed=1 << 23, transcendentals=0),
        name=name,
    )(device.reshape(1).astype(jnp.int32), *arrays)


def unpack_feed(z, part, device, arrays):
    def body(block, buffer, inner, outer, inner_bias):
        for number, out in ((0, inner), (1, outer)):
            for at in range(0, z.hidden, 512):
                stop = min(at + 512, z.hidden)
                value = block(number, at // LANES, -(-(stop - at) // LANES)).astype(F32)
                out[:, 0, at:stop] = value[: z.model, : stop - at]
        stacked = buffer[part.extra_at].astype(F32)
        tiles = round_up(z.hidden, LANES) // LANES
        line = jnp.concatenate([stacked[t : t + 1] for t in range(tiles)], axis=1)
        inner_bias[...] = line[:, : z.hidden]

    wide = (z.model, 1, z.hidden)
    inner, outer, inner_bias = unpack_call(
        "unpack_feed", z, part, device, arrays, (wide, wide, (1, z.hidden)), body
    )
    return jnp.transpose(inner, (1, 0, 2)), jnp.transpose(outer, (1, 2, 0)), inner_bias


def unpack_attend(z, part, device, arrays):
    def body(block, buffer, query, key_value, position, output, content_bias, position_bias, *rows):
        spread = half_selection(z)
        wide = HALVES * z.width // LANES
        query[:, 0, :] = dot_nt(block(0, 0, wide), spread)[: z.model]
        position[:, 0, :] = dot_nt(block(2, 0, wide), spread)[: z.model]
        output[:, 0, :] = dot_nt(spread, block(3, 0, wide))[:, : z.model]
        for side in range(2):
            value = dot_nt(block(1, side * wide, wide), spread)[: z.model]
            key_value[:, 0, side * z.proj : (side + 1) * z.proj] = value
        stacked = buffer[part.extra_at].astype(F32)
        sums = jnp.concatenate([stacked[8 * t : 8 * (t + 1)] for t in range(wide)], axis=1)
        sums = dot_nt(sums.astype(BF16), spread)
        content_bias[...] = sums[0:1]
        position_bias[...] = sums[1:2]
        stacked = buffer[part.extra_at + 1].astype(F32)
        tiles = round_up(z.model, LANES) // LANES
        sums = jnp.concatenate([stacked[8 * t : 8 * (t + 1)] for t in range(tiles)], axis=1)
        for k, out in enumerate(rows):
            out[...] = sums[k : k + 1, : z.model]

    square, row = (z.model, 1, z.proj), (1, z.model)
    shapes = (
        square, (z.model, 1, 2 * z.proj), square, (z.proj, 1, z.model), (1, z.proj), (1, z.proj),
        row, row, row, row, row,
    )
    results = unpack_call("unpack_attend", z, part, device, arrays, shapes, body)
    return [jnp.transpose(r, (1, 0, 2)) if r.ndim == 3 else r for r in results]


def frequencies(z):
    exponent = np.arange(0, z.model, 2).astype(np.float32) / np.float32(z.model)
    return np.power(np.float32(10000.0), -exponent).astype(np.float32)[:, None]


def prepare_call(z, query, key_value, position, output, biases, rows):
    farthest = z.keys - 1 + z.shift - z.seg + 1
    number = len(biases)

    def body(ins, items, outs):
        key_value, query, position, output = items[:4]
        vectors = items[4:]
        query_out, key_value_out, output_out, rel_out, table, lines = [out.ref for out in outs]
        lines[...] = jnp.zeros(lines.shape, F32)
        rate = ins[0]
        rest = iota((z.model // 2, LANES), 1).astype(F32)
        near = rate[...] * rest
        far = rate[...] * (farthest - LANES * rest)
        near_sin, near_cos = jnp.sin(near), jnp.cos(near)
        far_sin, far_cos = jnp.sin(far), jnp.cos(far)
        sines, cosines = [], []
        for t in range(z.tiles):
            a, b = far_sin[:, t : t + 1], far_cos[:, t : t + 1]
            sines.append(a * near_cos - b * near_sin)
            cosines.append(b * near_cos + a * near_sin)
        values = [jnp.concatenate(tiles, axis=1) for tiles in (sines, cosines)]
        table[...] = jnp.concatenate(values, axis=0).astype(BF16)
        outs[4].send()
        spread, gather = half_selection(z), half_selection(z, True)
        parts = [slice(half * z.width, (half + 1) * z.width) for half in range(HALVES)]
        for half, lanes in enumerate(parts):
            for side in range(2):
                own = key_value()[:, side * z.proj : (side + 1) * z.proj]
                key_value_out[side * HALVES + half] = dot_nt(gather[lanes, :], own).astype(BF16)
        outs[1].send()
        for half, lanes in enumerate(parts):
            query_out[half] = dot(query()[...], spread[:, lanes]).astype(BF16)
        outs[0].send()
        for half, lanes in enumerate(parts):
            wide = dot_nt(gather[lanes, :], position()[...]).astype(BF16)
            rel_out[half] = dot(wide, table[...]).astype(BF16)
        outs[3].send()
        for half, lanes in enumerate(parts):
            output_out[half] = dot(gather[lanes, :], output()[...]).astype(BF16)
        outs[2].send()
        for half, lanes in enumerate(parts):
            for k, source in enumerate(vectors[:number]):
                at = k * HALVES + half
                lines[at : at + 1, : z.width] = dot(source()[...], spread[:, lanes])
        for k, source in enumerate(vectors[number:]):
            at = number * HALVES + k
            lines[at : at + 1, : source().shape[1]] = source()[...].astype(F32)
        outs[5].send()

    shapes = [
        ((HALVES, z.model, z.width), BF16), ((2 * HALVES, z.width, z.model), BF16),
        ((HALVES, z.width, z.model), BF16), ((HALVES, z.width, z.cols), BF16),
        ((z.model, z.cols), BF16), ((Line.count, z.hidden), F32),
    ]
    arrays = [key_value, query, position, output, *biases, *rows]
    results = kernel_call(
        "prepare", body, [whole(jnp.asarray(frequencies(z)))], [(array, None) for array in arrays],
        shapes, [],
    )
    return [array[0] for array in results]


def unwritten(shapes):
    leaves, tree = jax.tree.flatten(shapes)
    if leaves:
        leaves = pl.pallas_call(
            lambda *refs: None,
            out_shape=leaves,
            out_specs=[pl.BlockSpec(memory_space=pl.ANY)] * len(leaves),
            name="unwritten",
        )()
    return jax.tree.unflatten(tree, leaves)


def moved_along(value, pairs):
    return lax.ppermute(value, "section", pairs)


def shards(
    stream_in, memories, cotangent, query_weight, key_value_matrix, position_weight,
    output_weight, bias_content, bias_position, attend_gain, attend_bias, inner_weight,
    inner_bias, outer_weight, outer_bias, feed_gain, feed_bias,
):
    count, seg_len, model = stream_in.shape
    z = Sizes(seg_len, memories.shape[2], model, query_weight.shape[2], inner_weight.shape[2])
    devices = lax.axis_size("dp")
    section, device = lax.axis_index("section"), lax.axis_index("dp")
    first = section == 0
    memory = jnp.transpose(memories[0], (0, 2, 1))
    made = prepare_call(
        z, query_weight[0], key_value_matrix[0], position_weight[0], output_weight[0],
        [bias_content, bias_position],
        [attend_gain, attend_bias, inner_bias, outer_bias, feed_gain, feed_bias],
    )
    table = made[4]
    weights = Weights(
        made[0], made[1], made[2], made[3], inner_weight[0], jnp.transpose(outer_weight[0]), made[5],
    )

    def shape_of(value):
        return jax.tree.map(lambda a: jax.ShapeDtypeStruct(a.shape, a.dtype), value)

    def pick(first_act, second_act, second_ahead=False):
        made = [jax.eval_shape(act) for act in (first_act, second_act)]

        def blank(side):
            return unwritten(shape_of(made[side][1]))

        def run_first():
            message, rest = first_act()
            if message is None:
                message = unwritten(shape_of(made[1][0]))
            return message, rest, blank(1)

        def run_second():
            message, rest = second_act()
            return message, blank(0), rest

        if second_ahead:
            return lax.cond(first, run_first, run_second)
        return lax.cond(jnp.logical_not(first), run_second, run_first)

    def forwarded(number):
        return (forward_zero, 0) if number == 0 else (forward_rest, number - 1)

    def feed_back(number):
        stored, slot = forwarded(number)
        return feed_back_call(z, weights, grads[number], stored[2], slot)

    def attend_back(number):
        back_first, feed = feeds[number]
        stored, slot = forwarded(number)
        return attend_back_call(z, weights, back_first, feed.attend, stored[1], slot)

    def both(number):
        made = both_call(z, weights, sent[number], 0, memory, cotangent, number)
        return made[1], (made[0],) + made[2:]

    forward_zero, forward_rest = forward_call(z, weights, stream_in, memory, 0, 1), None
    feeds, attends, both_made, grads = [], [], [], []
    sent = [moved_along(forward_zero[0], [(0, 1)])]
    for tick in range(1, count + 1):

        def first_act(tick=tick):
            if tick == 1:
                made = forward_call(z, weights, stream_in, memory, 1, count - 1)
                return made[0][:1], made
            message = forward_rest[0][tick - 1 : tick] if tick < count else None
            feeds.append(feed_back(tick - 2))
            made = feeds[-1], attend_back(tick - 2)
            feeds.pop()
            return message, made

        message, made, second = pick(first_act, lambda tick=tick: both(tick - 1))
        if tick == 1:
            forward_rest = made
        else:
            feeds.append(made[0])
            attends.append(made[1])
        both_made.append((second[0], message) + second[1:])
        came = moved_along(message, [(0, 1), (1, 0)] if tick < count else [(1, 0)])
        sent.append(came)
        grads.append(came)

    feed_part = Part(z, (z.hidden, z.hidden), 1, devices)
    wide = HALVES * z.width
    attend_part = Part(z, (wide, 2 * wide, wide, wide), 2, devices)
    fed = (
        [(stored[3], slot) for stored, slot in map(forwarded, range(count))],
        [(member[2], 0) for member in both_made],
    )
    def attend_back_there(number):
        return pick(lambda: ((), attend_back(number)), lambda: ((), ()))[1]

    final = count - 1
    feeds.append(pick(lambda: ((), feed_back(final)), lambda: ((), ()))[1])
    back_feed = (
        [(feed, 0) for _, feed in feeds], [(member[3], 0) for member in both_made]
    )
    feed_mine, feed_theirs = feed_gradients(z, feed_part, section, device, fed, back_feed)
    feed_chains = chains_of(feed_part, feed_mine, swapped_cores(feed_theirs))
    last = feed_chains[1]
    back_first, last.keep = lax.optimization_barrier((feeds[final][0], last.keep))
    feeds[final] = (back_first, feeds[final][1])
    attend = attend_back_there(final)
    last_grad, feed_chains[0].flying = lax.optimization_barrier(
        (attend[0], feed_chains[0].flying)
    )
    attends.append((last_grad, attend[1]))
    sources = (
        [(stream_in, i) for i in range(count)],
        [(sent[i], 0) for i in range(count)],
    )
    passes = [forwarded(i) for i in range(count)]
    layer_out = [((passes[i][0][0], passes[i][1]), (both_made[i][0], 0)) for i in range(count)]
    input_grad = [((attends[i][0], 0), (both_made[i][1], 0)) for i in range(count)]
    mine, theirs, outputs, input_grads = attend_gradients(
        z, attend_part, section, device, table, memory, sources, fed, back_feed,
        ([(member[1], 0) for member in attends], [(member[4], 0) for member in both_made]),
        (layer_out, input_grad),
    )
    came = swapped_cores(theirs)
    last = step_all(feed_chains, last)
    came[0], last.keep = lax.optimization_barrier((came[0], last.keep))
    attend_chains = chains_of(attend_part, mine, came)
    last = attend_chains[1]
    while feed_chains[0].spread >= 0:
        last = step_all(feed_chains, last)
        last = step_all(attend_chains, last)
    feed_arrays = finished(feed_chains)
    inner, outer, inner_bias_grad = unpack_feed(z, feed_part, device, feed_arrays)
    chain = attend_chains[0]
    chain.flying, inner_bias_grad = lax.optimization_barrier((chain.flying, inner_bias_grad))
    while chain.spread >= 0:
        last = step_all(attend_chains, last)
    attend_arrays = finished(attend_chains)
    (
        query, key_value, position, output, bias_c, bias_p, gain_a, bias_a, bias_o, gain_f, bias_f,
    ) = unpack_attend(z, attend_part, device, attend_arrays)
    return (
        outputs[None], input_grads[None], query, key_value, position, output, bias_c, bias_p,
        gain_a, bias_a, inner, inner_bias_grad, outer, bias_o, gain_f, bias_f,
    )


def solution(mesh):
    stacked, dp = P("section"), P("dp")
    both = P("section", "dp")
    return jax.shard_map(
        shards,
        mesh=mesh,
        in_specs=(dp, both, dp) + (stacked,) * 14,
        out_specs=(both, both) + (stacked,) * 14,
        check_vma=False,
    )
```

```python
from functools import partial
from typing import Any, NamedTuple

import jax
import jax.numpy as jnp
import numpy as np
from jax import lax
from jax.experimental import pallas as pl
from jax.experimental.pallas import tpu as pltpu
from jax.sharding import PartitionSpec as P

HEADS = 10
HALVES = 2
GROUP = HEADS // HALVES
LANES = 128
UNIT = 32
NORM_EPS = 1e-05
GELU_SLOPE = 0.7978845608028654
GELU_CUBIC = 0.044715
MASK_FILL = -1e30
LOG2_E = 1.4426950408889634
F32 = jnp.float32
BF16 = jnp.bfloat16
VMEM_BYTES = 60 * 1024 * 1024


def round_up(value, unit):
    return -(-value // unit) * unit


class Sizes:
    def __init__(self, seg_len, mem_len, model, proj, hidden):
        self.seg, self.mem, self.model, self.proj, self.hidden = seg_len, mem_len, model, proj, hidden
        self.keys = mem_len + seg_len
        self.head = proj // HEADS
        self.rows = round_up(seg_len, 16)
        self.body = seg_len // 16 * 16
        self.tail = self.body + 8
        self.used = GROUP * self.head
        self.width = round_up(self.used, 256)
        self.cols = round_up(self.keys, LANES)
        self.recent = self.cols - mem_len
        self.stack = round_up(GROUP * self.tail, 256)
        self.tail_at = GROUP * self.body
        self.tail_rows = self.stack - self.tail_at
        self.tiles = self.cols // LANES
        self.shift = round_up(seg_len - 1, 8)
        self.scale = self.head ** (-0.5)
        assert self.seg - self.body <= 8 and self.tail_rows % 16 == 0
        assert self.shift == self.tail and self.mem % LANES == 0 and self.shift <= LANES * 2


class Weights(NamedTuple):
    query: Any
    key_value: Any
    output: Any
    rel: Any
    inner: Any
    outer: Any
    lines: Any


class Line:
    bias_content, bias_position = 0, HALVES
    attend_gain, attend_bias, inner_bias, outer_bias, feed_gain, feed_bias = range(
        2 * HALVES, 2 * HALVES + 6
    )
    count = 16


class Kept(NamedTuple):
    attention: Any
    content_stack: Any
    position_stack: Any
    keys: Any
    values: Any
    mixed: Any


class KeptFeed(NamedTuple):
    first_normed: Any
    first_inverse: Any
    second_normed: Any
    second_inverse: Any
    slope: Any


class Fed(NamedTuple):
    mixed_low: Any
    middle: Any
    active: Any


class BackFeed(NamedTuple):
    pre: Any
    outer: Any
    attend: Any
    sums: Any


class BackAttend(NamedTuple):
    query: Any
    key_value: Any
    rel: Any
    sums: Any


def layouts(z):
    halves = lambda rows, cols, kind: ((HALVES, rows, cols), kind)
    kept = Kept(
        halves(z.stack, z.cols, BF16),
        halves(z.stack, z.width, BF16),
        halves(z.stack, z.width, BF16),
        halves(z.width, z.cols, BF16),
        halves(z.width, z.cols, BF16),
        halves(z.rows, z.width, F32),
    )
    wide, narrow = ((z.rows, z.model), F32), ((z.rows, 1), F32)
    kept_feed = KeptFeed(wide, narrow, wide, narrow, ((z.rows, z.hidden), BF16))
    low = ((z.rows, z.model), BF16)
    fed = Fed(halves(z.rows, z.width, BF16), low, ((z.rows, z.hidden), BF16))
    back_feed = BackFeed(((z.rows, z.hidden), BF16), low, low, ((8, z.model), F32))
    back_attend = BackAttend(
        halves(z.rows, z.width, BF16),
        ((2 * HALVES, z.width, z.cols), BF16),
        halves(z.width, z.cols, BF16),
        halves(8, z.width, F32),
    )
    return kept, kept_feed, fed, back_feed, back_attend


def dot(left, right):
    return lax.dot_general(left, right, (((1,), (0,)), ((), ())), preferred_element_type=F32)


def dot_nt(left, right):
    return lax.dot_general(left, right, (((1,), (1,)), ((), ())), preferred_element_type=F32)


def dot_tn(left, right):
    return lax.dot_general(left, right, (((0,), (0,)), ((), ())), preferred_element_type=F32)


def iota(shape, dim):
    return lax.broadcasted_iota(jnp.int32, shape, dim)


class Item:
    def __init__(self, ref, copy=None, once=None):
        self.ref, self.copy, self.once = ref, copy, once

    def __call__(self):
        if self.copy is not None:
            self.once(self.copy.wait)
            self.copy = None
        return self.ref


class Out:
    def __init__(self, ref, target, sems):
        self.ref, self.target, self.sems = ref, target, sems
        self.copies = []

    def part(self, index, slot):
        copy = pltpu.make_async_copy(self.ref.at[index], self.target.at[index], self.sems.at[slot])
        copy.start()
        return copy

    def send(self):
        copy = pltpu.make_async_copy(self.ref, self.target, self.sems.at[0])
        copy.start()
        self.copies.append(copy)


def kernel_call(name, body, direct, fetched, made, scratch, count=1, flops=0):
    made = list(made)
    parts = 4

    def kernel(*refs):
        refs = list(refs)

        def take(number):
            taken = refs[:number]
            del refs[:number]
            return taken

        ins, sources, targets = take(len(direct)), take(len(fetched)), take(len(made))
        landed, built = take(len(fetched)), take(len(made))
        in_sems, out_sems = take(2)
        first = pl.program_id(0) == 0
        once = (lambda act: act()) if count == 1 else (lambda act: pl.when(first)(act))
        items = []
        for k, (ref, (_, slot)) in enumerate(zip(sources, fetched)):
            source = ref if slot is None else ref.at[slot]
            copy = pltpu.make_async_copy(source, landed[k], in_sems.at[k])
            once(copy.start)
            items.append(Item(landed[k], copy, once))
        outs = [
            Out(ref, target.at[pl.program_id(0)], out_sems.at[k])
            for k, (ref, target) in enumerate(zip(built, targets))
        ]
        body(ins, items, outs, *refs)
        for item in items:
            item()
        for out in outs:
            for copy in out.copies:
                copy.wait()

    landing = [
        pltpu.VMEM(array.shape if slot is None else array.shape[1:], array.dtype)
        for array, slot in fetched
    ]
    results = pl.pallas_call(
        kernel,
        grid=(count,),
        in_specs=[spec for _, spec in direct]
        + [pl.BlockSpec(memory_space=pl.ANY)] * len(fetched),
        out_specs=[pl.BlockSpec(memory_space=pl.ANY)] * len(made),
        out_shape=[jax.ShapeDtypeStruct((count,) + tuple(s), t) for s, t in made],
        scratch_shapes=landing
        + [pltpu.VMEM(s, t) for s, t in made]
        + [
            pltpu.SemaphoreType.DMA((max(len(fetched), 1),)),
            pltpu.SemaphoreType.DMA((max(len(made), 1), parts)),
        ]
        + scratch,
        compiler_params=pltpu.CompilerParams(vmem_limit_bytes=VMEM_BYTES),
        cost_estimate=pl.CostEstimate(flops=flops, bytes_accessed=1 << 23, transcendentals=0),
        name=name,
    )(*[array for array, _ in direct], *[array for array, _ in fetched])
    return list(results)


def whole(array):
    zeros = (0,) * array.ndim
    return (array, pl.BlockSpec(array.shape, lambda i: zeros, pipeline_mode=pl.Buffered(1)))


def segment(array, slot):
    zeros = (0,) * (array.ndim - 1)
    return (array, pl.BlockSpec((None,) + array.shape[1:], lambda i: (i + slot,) + zeros))


def head_lanes(z, rows, head):
    lane = iota((rows, z.width), 1)
    return (lane >= z.head * head) & (lane < z.head * (head + 1))


def stack_heads(z, target, source):
    tails = []
    for head in range(GROUP):
        own = jnp.where(head_lanes(z, z.tail, head), source[: z.tail], 0.0)
        target[z.body * head : z.body * (head + 1), :] = own[: z.body].astype(BF16)
        tails.append(own[z.body :])
    tails.append(jnp.zeros((z.tail_rows - 8 * GROUP, z.width), F32))
    target[z.tail_at :, :] = jnp.concatenate(tails, axis=0).astype(BF16)


def unstack_heads(z, source):
    total = None
    for head in range(GROUP):
        rows = jnp.concatenate(
            [
                source[z.body * head : z.body * (head + 1)],
                source[z.tail_at + 8 * head : z.tail_at + 8 * (head + 1)],
            ],
            axis=0,
        )
        own = jnp.where(head_lanes(z, z.tail, head), rows, 0.0)
        total = own if total is None else total + own
    return total


def normalize(values):
    centered = values - jnp.mean(values, axis=-1, keepdims=True)
    variance = jnp.mean(centered * centered, axis=-1, keepdims=True)
    inverse = lax.rsqrt(variance + NORM_EPS)
    return (centered * inverse, inverse)


def normalize_back(grad_normed, normed, inverse):
    return inverse * (
        grad_normed
        - jnp.mean(grad_normed, axis=-1, keepdims=True)
        - normed * jnp.mean(grad_normed * normed, axis=-1, keepdims=True)
    )


def shifted_tiles(z, tiles, first_row):
    base = (first_row - z.shift) % LANES
    turns = (first_row - z.shift - base) // LANES
    lane, row = iota((8, LANES), 1), iota((8, LANES), 0)
    turned = [pltpu.roll(tile, base, 1, stride=1, stride_axis=0) for tile in tiles]
    kept = lane >= base + row
    return [
        jnp.where(kept, turned[(t - turns) % z.tiles], turned[(t - turns - 1) % z.tiles])
        for t in range(z.tiles)
    ]


def restored_tiles(z, tiles, first_row):
    lane, row = iota((8, LANES), 1), iota((8, LANES), 0)
    amount = z.shift - first_row
    place = (lane - amount + row) % LANES
    turned = [jnp.take_along_axis(tile, place, axis=1) for tile in tiles]
    base, turns = amount % LANES, amount // LANES
    if base >= 8:
        kept, other = lane >= base - row, -1
    else:
        assert base == 0
        kept, other = lane < LANES - row, 1
    return [
        jnp.where(kept, turned[(t - turns) % z.tiles], turned[(t - turns + other) % z.tiles])
        for t in range(z.tiles)
    ]


def split_tiles(z, block):
    return [block[:, LANES * t : LANES * (t + 1)] for t in range(z.tiles)]


def over_rows(z, chunk):
    for head in range(GROUP):
        for part in range(z.body // 16):
            chunk(head * z.body + 16 * part, 16 * part, 16 * part + 8)
    for part in range(z.tail_rows // 16):
        chunk(z.tail_at + 16 * part, z.body, z.body)


def attention_rows(z, content, position, attention):
    def chunk(row, first, second):
        for at, query in ((row, first), (row + 8, second)):
            rows = slice(at, at + 8)
            moved = shifted_tiles(z, split_tiles(z, position[rows, :]), query)
            for t in range(z.tiles):
                lanes = slice(LANES * t, LANES * (t + 1))
                scores = content[rows, lanes] + moved[t]
                if t >= z.mem // LANES:
                    ahead = iota((8, LANES), 1) - iota((8, LANES), 0)
                    allowed = ahead <= z.mem + query - LANES * t
                    scores = jnp.where(allowed, scores, MASK_FILL)
                content[rows, lanes] = scores

    over_rows(z, chunk)
    scores = content[...]
    largest = jnp.max(scores, axis=-1, keepdims=True)
    powers = jnp.exp2((scores - largest) * (z.scale * LOG2_E))
    inverse = 1.0 / jnp.sum(powers, axis=-1, keepdims=True)
    attention[...] = (powers * inverse).astype(BF16)


def attention_rows_back(z, attention, back_map, weighted, back_raw, back_table):
    def chunk(row, first, second):
        rows = slice(row, row + 16)
        inner = weighted[rows, :]
        tops, lows = [], []
        for t in range(z.tiles):
            lanes = slice(LANES * t, LANES * (t + 1))
            raw = attention[rows, lanes].astype(F32) * ((back_map[rows, lanes] - inner) * z.scale)
            back_raw[rows, lanes] = raw.astype(BF16)
            tops.append(raw[:8])
            lows.append(raw[8:])
        tops, lows = restored_tiles(z, tops, first), restored_tiles(z, lows, second)
        for t in range(z.tiles):
            pair = jnp.concatenate([tops[t], lows[t]], axis=0).astype(BF16)
            back_table[rows, LANES * t : LANES * (t + 1)] = pair

    over_rows(z, chunk)


def gelu_and_slope(values):
    squared = values * values
    tangent = jnp.tanh(GELU_SLOPE * (values + GELU_CUBIC * squared * values))
    half = 0.5 * (1.0 + tangent)
    slope = half + 0.5 * values * (1.0 - tangent * tangent) * GELU_SLOPE * (
        1.0 + 3.0 * GELU_CUBIC * squared
    )
    return (values * half, slope)


def forward_body(
    z, w, source, memory, kept, kept_feed, fed, result, hidden, content, position, attention_done
):
    hidden[...] = jnp.zeros(hidden.shape, BF16)
    hidden[: z.seg, :] = source[...]
    for j in range(2 * HALVES):
        target = (kept.keys if j < HALVES else kept.values).at[j % HALVES]
        target[:, : z.mem] = dot(w.key_value()[j], memory[...]).astype(BF16)
        target[:, z.mem :] = dot_nt(w.key_value()[j], hidden[...]).astype(BF16)
    rows_in = hidden[: z.rows, :]
    real = iota((z.rows, 1), 0) < z.seg
    lines = w.lines()
    line = lambda number: lines[number : number + 1, : z.model]
    for half in range(HALVES):
        raw = dot(rows_in, w.query()[half])
        for stack, number in (
            (kept.content_stack, Line.bias_content), (kept.position_stack, Line.bias_position)
        ):
            bias = lines[number + half : number + half + 1, : z.width]
            stack_heads(z, stack.at[half], jnp.where(real, raw + bias, 0.0))
    rel = w.rel()

    def one_half(half, carry):
        content[...] = dot(kept.content_stack[half], kept.keys[half])
        position[...] = dot(kept.position_stack[half], rel[half])
        attention_rows(z, content, position, kept.attention.at[half])
        mixed = unstack_heads(z, dot_nt(kept.attention[half], kept.values[half]))
        kept.mixed[half, : z.tail, :] = mixed
        kept.mixed[half, z.tail :, :] = jnp.zeros((z.rows - z.tail, z.width), F32)
        return carry

    lax.fori_loop(0, HALVES, one_half, 0)
    attention_done()
    total = rows_in.astype(F32)
    for half in range(HALVES):
        mixed = kept.mixed[half].astype(BF16)
        fed.mixed_low[half] = mixed
        total = total + dot(mixed, w.output()[half])
    normed, inverse = normalize(total)
    kept_feed.first_normed[...] = normed
    kept_feed.first_inverse[...] = inverse
    middle = (normed * line(Line.attend_gain) + line(Line.attend_bias)).astype(BF16)
    fed.middle[...] = middle
    active, slope = gelu_and_slope(
        dot(middle, w.inner()[...]) + lines[Line.inner_bias : Line.inner_bias + 1, :]
    )
    kept_feed.slope[...] = slope.astype(BF16)
    active = active.astype(BF16)
    fed.active[...] = active
    feed = dot_nt(active, w.outer()[...]) + line(Line.outer_bias)
    normed, inverse = normalize(middle.astype(F32) + feed)
    kept_feed.second_normed[...] = normed
    kept_feed.second_inverse[...] = inverse
    out = (normed * line(Line.feed_gain) + line(Line.feed_bias)).astype(BF16)
    result[...] = out[: z.seg]


def feed_back_body(z, w, grad_in, kept, back, back_first, top):
    top[...] = jnp.zeros(top.shape, BF16)
    top[: z.seg, :] = grad_in[...]
    grad_top = top[...].astype(F32)
    lines = w.lines()
    line = lambda number: lines[number : number + 1, : z.model]
    normed = kept.second_normed()[...]
    second = normalize_back(
        grad_top * line(Line.feed_gain), normed, kept.second_inverse()[...]
    )
    outer = second.astype(BF16)
    back.outer[...] = outer
    pre = (dot(outer, w.outer()[...]) * kept.slope()[...].astype(F32)).astype(BF16)
    back.pre[...] = pre
    middle = second + dot_nt(pre, w.inner()[...])
    first_normed = kept.first_normed()[...]
    first = normalize_back(
        middle * line(Line.attend_gain), first_normed, kept.first_inverse()[...]
    )
    back_first[...] = first
    back.attend[...] = first.astype(BF16)
    sums = back.sums
    sums[...] = jnp.zeros(sums.shape, F32)
    rows = (middle * first_normed, middle, outer.astype(F32), grad_top * normed, grad_top)
    for k, values in enumerate(rows):
        sums[k : k + 1, :] = jnp.sum(values, axis=0, keepdims=True)


def attend_back_body(
    z, w, kept, back_first, back_attend, back, send, input_grad, stack, back_map, weighted, raw, table
):
    refs = Kept(*[item() for item in kept])
    output, rel = w.output(), w.rel()

    def one_half(half, carry):
        own = dot_nt(back_attend[...], output[half]).astype(BF16).astype(F32)
        stack_heads(z, stack, own)
        product = own[: z.tail] * refs.mixed[half, : z.tail, :]
        weighted[z.tail_at :, :] = jnp.zeros((z.tail_rows, 1), F32)
        for head in range(GROUP):
            inner = jnp.where(head_lanes(z, z.tail, head), product, 0.0)
            inner = jnp.sum(inner, axis=1, keepdims=True)
            weighted[z.body * head : z.body * (head + 1), :] = inner[: z.body]
            at = z.tail_at + 8 * head
            weighted[at : at + 8, :] = inner[z.body :]
        back_map[...] = dot(stack[...], refs.values[half])
        attention_rows_back(z, refs.attention.at[half], back_map, weighted, raw, table)
        back.key_value[half] = dot_tn(refs.content_stack[half], raw[...]).astype(BF16)
        back.key_value[HALVES + half] = dot_tn(stack[...], refs.attention[half]).astype(BF16)
        back.rel[half] = dot_tn(refs.position_stack[half], table[...]).astype(BF16)
        send(half)
        from_content = unstack_heads(z, dot_nt(raw[...], refs.keys[half]))
        from_position = unstack_heads(z, dot_nt(table[...], rel[half]))
        back.query[half, : z.tail, :] = (from_content + from_position).astype(BF16)
        back.query[half, z.tail :, :] = jnp.zeros((z.rows - z.tail, z.width), BF16)
        back.sums[half] = jnp.concatenate(
            [
                jnp.sum(from_content, axis=0, keepdims=True),
                jnp.sum(from_position, axis=0, keepdims=True),
                jnp.zeros((6, z.width), F32),
            ],
            axis=0,
        )
        return carry

    lax.fori_loop(0, HALVES, one_half, 0)
    total = back_first[...]
    for half in range(HALVES):
        total = total + dot_nt(back.query[half], w.query()[half])
    for j in range(2 * HALVES):
        recent = dot_tn(back.key_value[j, :, z.mem :], w.key_value()[j])
        total = total + recent[: z.rows]
    input_grad[...] = total[: z.seg].astype(BF16)


def back_scratch(z):
    return [
        pltpu.VMEM((z.stack, z.width), BF16),
        pltpu.VMEM((z.stack, z.cols), F32),
        pltpu.VMEM((z.stack, 1), F32),
        pltpu.VMEM((z.stack, z.cols), BF16),
        pltpu.VMEM((z.stack, z.cols), BF16),
    ]


def vmem(entries):
    return [pltpu.VMEM(s, t) for s, t in entries]


def tally(z, passes):
    return int(passes * 2e10)


ARRIVAL = (1, 6, 0, 3, 2, 4, 5)


def arriving(weights):
    return [(weights[k], None) for k in ARRIVAL]


def arrived_weights(items):
    own = dict(zip(ARRIVAL, items))
    return Weights(*[own[k] for k in range(len(ARRIVAL))])


def refs_of(kind, outs):
    return kind(*[out.ref for out in outs])


def send_all(outs):
    for out in outs:
        out.send()


def attend_sender(outs):
    query, key_value, rel, sums = outs

    def parts(half):
        yield key_value, half, half
        yield key_value, HALVES + half, HALVES + half
        yield rel, half, half

    def send(half):
        for out, index, slot in parts(half):
            out.part(index, slot)

    def finish():
        for half in range(HALVES):
            for out, index, slot in parts(half):
                pltpu.make_async_copy(
                    out.ref.at[index], out.target.at[index], out.sems.at[slot]
                ).wait()

    return send, finish


@partial(jax.jit, static_argnums=(0, 4, 5))
def forward_call(z, weights, source, memory, slot, count):
    kept, kept_feed, fed = layouts(z)[:3]
    direct = [segment(source, slot), segment(memory, slot)]

    def body(ins, items, outs, hidden, content, position):
        result, outs = outs[0], outs[1:]
        forward_body(
            z, arrived_weights(items), ins[0], ins[1], refs_of(Kept, outs[:6]),
            refs_of(KeptFeed, outs[6:11]), refs_of(Fed, outs[11:]), result.ref, hidden, content,
            position, lambda: send_all(outs[:6]),
        )
        send_all([result] + outs[6:])

    made = [((z.seg, z.model), BF16), *kept, *kept_feed, *fed]
    results = kernel_call(
        "forward", body, direct, arriving(weights), made,
        [
            pltpu.VMEM((z.recent, z.model), BF16),
            pltpu.VMEM((z.stack, z.cols), F32),
            pltpu.VMEM((z.stack, z.cols), F32),
        ],
        count, tally(z, count),
    )
    return results[0], Kept(*results[1:7]), KeptFeed(*results[7:12]), Fed(*results[12:])


@partial(jax.jit, static_argnums=(0, 3, 6))
def both_call(z, weights, source, source_slot, memory, grad_in, slot):
    kept, kept_feed, fed, back_feed, back_attend = layouts(z)
    fetched = [(source, source_slot), (memory, slot)] + arriving(weights) + [(grad_in, slot)]

    def body(ins, items, outs, hidden, content, position, *scratch):
        w = arrived_weights(items[2:-1])
        result, input_grad = outs[:2]
        fed_outs, feed_outs, attend_outs = outs[2:5], outs[5:9], outs[9:13]
        held, held_feed = Kept(*scratch[:6]), KeptFeed(*scratch[6:11])
        first, top, stack, weighted, raw, table = scratch[11:]
        forward_body(
            z, w, items[0](), items[1](), held, held_feed, refs_of(Fed, fed_outs), result.ref,
            hidden, content, position, lambda: None,
        )
        send_all([result] + fed_outs)
        feed_refs = refs_of(BackFeed, feed_outs)
        feed_back_body(
            z, w, items[-1](), KeptFeed(*[Item(ref) for ref in held_feed]), feed_refs, first, top
        )
        send_all(feed_outs)
        send, finish = attend_sender(attend_outs)
        attend_back_body(
            z, w, Kept(*[Item(ref) for ref in held]), first, feed_refs.attend,
            refs_of(BackAttend, attend_outs), send, input_grad.ref, stack, content, weighted,
            raw, table,
        )
        send_all([input_grad, attend_outs[0], attend_outs[3]])
        finish()

    row = ((z.seg, z.model), BF16)
    scratch = back_scratch(z)
    del scratch[1]
    results = kernel_call(
        "forward_backward", body, [], fetched, [row, row, *fed, *back_feed, *back_attend],
        [
            pltpu.VMEM((z.recent, z.model), BF16),
            pltpu.VMEM((z.stack, z.cols), F32),
            pltpu.VMEM((z.stack, z.cols), F32),
        ]
        + vmem(kept)
        + vmem(kept_feed)
        + [pltpu.VMEM((z.rows, z.model), F32), pltpu.VMEM((z.rows, z.model), BF16)]
        + scratch,
        1, tally(z, 2),
    )
    return (
        results[0], results[1], Fed(*results[2:5]), BackFeed(*results[5:9]),
        BackAttend(*results[9:13]),
    )


@partial(jax.jit, static_argnums=(0, 4))
def feed_back_call(z, weights, grad_in, kept, slot):
    back_feed = layouts(z)[3]
    fetched = [(weights.lines, None)]
    fetched += [(a, slot) for a in (kept.second_normed, kept.second_inverse)]
    fetched += [(weights.outer, None), (kept.slope, slot), (weights.inner, None)]
    fetched += [(a, slot) for a in (kept.first_normed, kept.first_inverse)]

    def body(ins, items, outs, top):
        lines, second_normed, second_inverse, outer, slope, inner, first_normed, first_inverse = items
        w = Weights(*[None] * 4, inner, outer, lines)
        held = KeptFeed(first_normed, first_inverse, second_normed, second_inverse, slope)
        feed_back_body(z, w, ins[0], held, refs_of(BackFeed, outs[1:]), outs[0].ref, top)
        send_all(outs)

    results = kernel_call(
        "feed_backward", body, [segment(grad_in, 0)], fetched,
        [((z.rows, z.model), F32), *back_feed], [pltpu.VMEM((z.rows, z.model), BF16)],
        1, tally(z, 0.3),
    )
    return results[0], BackFeed(*results[1:])


@partial(jax.jit, static_argnums=(0, 5))
def attend_back_call(z, weights, back_first, back_attend, kept, slot):
    fetched = [(back_first, 0), (back_attend, 0), (weights.output, None)]
    fetched += [(array, slot) for array in kept]
    fetched += [(a, None) for a in (weights.rel, weights.query, weights.key_value)]

    def body(ins, items, outs, *scratch):
        first, attend, output = items[:3]
        rel, query, key_value = items[9:]
        w = Weights(query, key_value, output, rel, *[None] * 3)
        send, finish = attend_sender(outs[1:])
        attend_back_body(
            z, w, Kept(*items[3:9]), first(), attend(), refs_of(BackAttend, outs[1:]), send,
            outs[0].ref, *scratch,
        )
        send_all([outs[0], outs[1], outs[4]])
        finish()

    results = kernel_call(
        "attend_backward", body, [], fetched, [((z.seg, z.model), BF16), *layouts(z)[4]],
        back_scratch(z), 1, tally(z, 0.7),
    )
    return results[0], BackAttend(*results[1:])


class Part:
    def __init__(self, z, widths, extra, devices):
        self.rows = round_up(z.model, UNIT)
        self.per_tile = self.rows // UNIT
        self.first, at = [], 0
        for width in widths:
            self.first.append(at)
            at += round_up(width, LANES) // LANES
        self.extra_at = at * self.per_tile
        self.used = self.extra_at + extra
        bits = devices.bit_length() - 1
        assert devices == 1 << bits and bits >= 3
        order = list(range(1, bits))
        self.orders = (order, [order[1], order[0]] + order[2:])
        self.pieces = devices // 2
        per_piece = -(-self.used // devices)
        self.sizes = (-(-per_piece // 2), per_piece // 2)
        self.starts = (0, self.pieces * self.sizes[0])
        self.half = self.pieces * per_piece
        self.units = 2 * self.half

    def paths(self):
        return list(zip(self.orders, self.sizes, self.starts))

    def ports(self):
        return [self.pieces // 2 * size for size in self.sizes for _ in range(2)]


def rearranged(index, order):
    total = 0
    for place, bit in enumerate(reversed(order)):
        total = total + (((index >> bit) & 1) << place)
    return total


def exchanged(array, bit):
    count = lax.axis_size("dp")
    return lax.ppermute(array, "dp", [(i, i ^ (1 << bit)) for i in range(count)])


class Chain:
    def __init__(self, order, mine, came):
        self.order, self.reduced, self.spread = order, 1, len(order) - 1
        self.keep = mine[0] + came[0]
        self.flying = exchanged(mine[1] + came[1], order[0])

    def order_after(self, other):
        self.flying, other.keep = lax.optimization_barrier((self.flying, other.keep))

    def advance(self):
        came, keep = self.flying, self.keep
        if self.reduced < len(self.order):
            half = keep.shape[0] // 2
            self.keep = keep[:half] + came[:half]
            self.flying = exchanged(keep[half:] + came[half:], self.order[self.reduced])
            self.reduced += 1
            return
        if self.spread == len(self.order) - 1:
            self.keep = keep + came
        else:
            self.keep = jnp.concatenate([keep, came], axis=0)
        self.flying = exchanged(self.keep, self.order[self.spread])
        self.spread -= 1


def swapped_cores(arrays):
    return [exchanged(array, 0) for array in arrays]


def chains_of(part, mine, came):
    return [
        Chain(order, mine[2 * k : 2 * k + 2], came[2 * k : 2 * k + 2])
        for k, order in enumerate(part.orders)
    ]


def step_all(chains, last):
    for chain in chains:
        chain.order_after(last)
        chain.advance()
        last = chain
    return last


def finished(chains):
    own = sum([[chain.keep, chain.flying] for chain in chains], [])
    return own + swapped_cores(own)


def piece_places(part, device, core):
    places = []
    for rel_core in range(2):
        base = (core ^ rel_core) * part.half
        for k, (order, size, start) in enumerate(part.paths()):
            own = rearranged(device, order)
            for piece in range(part.pieces):
                number = rel_core * 2 * len(part.orders) + 2 * k + piece // (part.pieces // 2)
                within = piece % (part.pieces // 2) * size
                places.append((number, within, base + start + (piece ^ own) * size, size))
    return places


def put_block(part, packed, number, value, tile=0):
    for t in range(value.shape[1] // LANES):
        block = value[:, LANES * t : LANES * (t + 1)]
        if block.shape[0] < part.rows:
            fill = jnp.zeros((part.rows - block.shape[0], LANES), block.dtype)
            block = jnp.concatenate([block, fill], axis=0)
        at = (part.first[number] + tile + t) * part.per_tile
        packed[at : at + part.per_tile] = block.astype(BF16).reshape(part.per_tile, UNIT, LANES)


def packed_call(
    name, z, part, section, device, choices, direct, body, scratch, flops, lists=(), grouped=0,
    per_group=1,
):
    count, ports = len(choices), len(part.ports())
    buffers, place_of = [], []
    for k, ((array, _), _) in enumerate(choices + sum(lists, [])):
        shape = array.shape[1:]
        member = k % per_group
        if k < grouped and member:
            place_of.append((len(buffers) - 1, member))
            continue
        place_of.append((len(buffers), 0 if k < grouped else None))
        rows = shape[0] * (per_group if k < grouped else 1)
        buffers.append(pltpu.VMEM((rows,) + shape[1:], array.dtype))
    choices = choices + sum(lists, [])

    def kernel(place, *refs):
        ins, refs = refs[: len(direct)], refs[len(direct) :]
        sources, refs = refs[: 2 * len(choices)], refs[2 * len(choices) :]
        halves, refs = (refs[:ports], refs[ports : 2 * ports]), refs[2 * ports :]
        joined, refs = refs[: len(lists)], refs[len(lists) :]
        landed, refs = refs[: len(buffers)], refs[len(buffers) :]
        packed, in_sems, out_sems, joined_sems = refs[:4]
        items = []
        for k, pair in enumerate(choices):
            copies, target = [], landed[place_of[k][0]]
            if place_of[k][1] is not None:
                rows = pair[0][0].shape[1]
                target = target.at[pl.ds(place_of[k][1] * rows, rows)]
            for side, (_, slot) in enumerate(pair):
                copy = pltpu.make_async_copy(
                    sources[2 * k + side].at[slot], target, in_sems.at[k]
                )
                pl.when(place[0] == side)(copy.start)
                copies.append(copy)
            items.append(Item(landed[place_of[k][0]], copies[0], lambda act: act()))
        body(items[:count], ins, packed, *refs[4:])
        if part.units > part.used:
            packed[part.used :] = jnp.zeros((part.units - part.used, UNIT, LANES), BF16)
        copies = []
        core = place[1] & 1
        side = part.pieces // 2
        for rel_core, targets in enumerate(halves):
            base = (core ^ rel_core) * part.half
            for k, (order, size, start) in enumerate(part.paths()):
                own = rearranged(place[1], order)
                for piece in range(part.pieces):
                    copies.append(
                        pltpu.make_async_copy(
                            packed.at[pl.ds(base + start + (piece ^ own) * size, size)],
                            targets[2 * k + piece // side].at[pl.ds(piece % side * size, size)],
                            out_sems.at[len(copies)],
                        )
                    )
                    copies[-1].start()
        at = count
        for k, members in enumerate(lists):
            for i in range(len(members)):
                copies.append(
                    pltpu.make_async_copy(items[at](), joined[k].at[i], joined_sems.at[at - count])
                )
                copies[-1].start()
                at += 1
        for copy in copies:
            copy.wait()

    number = 2 * part.pieces * len(part.orders)
    shapes = [jax.ShapeDtypeStruct((units, UNIT, LANES), BF16) for units in part.ports()]
    anywhere = pl.BlockSpec(memory_space=pl.ANY)
    results = pl.pallas_call(
        kernel,
        in_specs=[pl.BlockSpec(memory_space=pltpu.SMEM)]
        + [pl.BlockSpec(memory_space=pltpu.VMEM)] * len(direct)
        + [anywhere] * (2 * len(choices)),
        out_specs=[anywhere] * (2 * ports + len(lists)),
        out_shape=shapes * 2
        + [
            jax.ShapeDtypeStruct((len(members),) + members[0][0][0].shape[1:], BF16)
            for members in lists
        ],
        scratch_shapes=buffers
        + [
            pltpu.VMEM((part.units, UNIT, LANES), BF16),
            pltpu.SemaphoreType.DMA((len(choices),)),
            pltpu.SemaphoreType.DMA((number,)),
            pltpu.SemaphoreType.DMA((max(len(choices) - count, 1),)),
        ]
        + scratch,
        compiler_params=pltpu.CompilerParams(vmem_limit_bytes=VMEM_BYTES),
        cost_estimate=pl.CostEstimate(flops=flops, bytes_accessed=1 << 23, transcendentals=0),
        name=name,
    )(
        jnp.stack([section, device]).astype(jnp.int32),
        *direct,
        *[array for pair in choices for array, _ in pair],
    )
    return results[:ports], results[ports : 2 * ports], *results[2 * ports :]


def feed_gradients(z, part, section, device, fed, back):
    count = len(fed[0])

    def both_sides(groups, field):
        return [
            tuple((getattr(groups[side][i][0], field), groups[side][i][1]) for side in range(2))
            for i in range(count)
        ]

    fields = (
        both_sides(fed, Fed._fields[1]), both_sides(back, BackFeed._fields[0]),
        both_sides(back, BackFeed._fields[1]), both_sides(fed, Fed._fields[2]),
    )

    def body(items, ins, packed):
        def rows_of(k):
            return [item() for item in items[k * count : (k + 1) * count]][0][...]

        def hidden_columns(number, left, right):
            left = jnp.transpose(left)
            for at in range(0, z.hidden, 512):
                stop = min(at + 512, z.hidden)
                value = dot(left, right[:, at:stop]).astype(BF16)
                short = round_up(stop - at, LANES) - (stop - at)
                if short:
                    fill = jnp.zeros((value.shape[0], short), BF16)
                    value = jnp.concatenate([value, fill], axis=1)
                put_block(part, packed, number, value, at // LANES)

        pre = rows_of(1)
        hidden_columns(0, rows_of(0), pre)
        hidden_columns(1, rows_of(2), rows_of(3))
        wide = round_up(z.hidden, LANES)
        line = jnp.sum(pre.astype(F32), axis=0, keepdims=True)
        line = jnp.concatenate([line, jnp.zeros((1, wide - z.hidden), F32)], axis=1)
        lines = [line[:, LANES * t : LANES * (t + 1)] for t in range(wide // LANES)]
        lines.append(jnp.zeros((UNIT - len(lines), LANES), F32))
        packed[part.extra_at] = jnp.concatenate(lines, axis=0).astype(BF16)

    return packed_call(
        "feed_gradients", z, part, section, device, sum(fields, []), [], body, [], tally(z, 0.4),
        (), 4 * count, count,
    )


def attend_gradients(
    z, part, section, device, table, memory, sources, fed, back_feed, back, lists
):
    count = len(fed[0])

    def both_sides(groups, field):
        return [
            tuple((getattr(groups[side][i][0], field), groups[side][i][1]) for side in range(2))
            for i in range(count)
        ]

    fields = (
        [tuple(sources[side][i] for side in range(2)) for i in range(count)],
        both_sides(back, BackAttend._fields[0]),
        both_sides(back_feed, BackFeed._fields[2]),
        both_sides(fed, Fed._fields[0]),
        [((memory, i), (memory, i)) for i in range(count)],
        both_sides(back, BackAttend._fields[1]),
        both_sides(back, BackAttend._fields[2]),
        both_sides(back, BackAttend._fields[3]),
        both_sides(back_feed, BackFeed._fields[3]),
    )

    def body(items, ins, packed, inputs):
        def refs(k):
            return [item() for item in items[k * count : (k + 1) * count]]

        inputs[...] = jnp.zeros(inputs.shape, BF16)
        for i, ref in enumerate(refs(0)):
            inputs[i, : z.seg, :] = ref[...]
        turned = [jnp.transpose(inputs[i]) for i in range(count)]
        rows_in = jnp.concatenate([inputs[i, : z.rows, :] for i in range(count)], axis=0)
        rows_in = jnp.transpose(rows_in)
        per_half = z.width // LANES
        query, mixed = refs(1), refs(3)
        attend = jnp.transpose(jnp.concatenate([ref[...] for ref in refs(2)], axis=0))
        for half in range(HALVES):
            value = dot(rows_in, jnp.concatenate([ref[half] for ref in query], axis=0))
            put_block(part, packed, 0, value, half * per_half)
            value = dot(attend, jnp.concatenate([ref[half] for ref in mixed], axis=0))
            put_block(part, packed, 3, value, half * per_half)
        memories, key_value = refs(4), refs(5)
        value = None
        for i in range(count):
            made = key_value[i][...].reshape(2 * HALVES * z.width, z.cols)
            grad = dot_nt(memories[i][...], made[:, : z.mem])
            grad = grad + dot_nt(turned[i], made[:, z.mem :])
            value = grad if value is None else value + grad
        put_block(part, packed, 1, value)
        rel = refs(6)
        for half in range(HALVES):
            total = rel[0][half].astype(F32)
            for ref in rel[1:]:
                total = total + ref[half].astype(F32)
            value = dot_nt(ins[0][...], total.astype(BF16))
            put_block(part, packed, 2, value, half * per_half)
        biases, feed = refs(7), refs(8)
        rows = []
        for half in range(HALVES):
            total = biases[0][half]
            for ref in biases[1:]:
                total = total + ref[half]
            rows += [total[:, LANES * t : LANES * (t + 1)] for t in range(per_half)]
        packed[part.extra_at] = jnp.concatenate(
            rows + [jnp.zeros((UNIT - 8 * len(rows), LANES), F32)] * (8 * len(rows) < UNIT), axis=0
        ).astype(BF16)
        total = feed[0][...]
        for ref in feed[1:]:
            total = total + ref[...]
        short = round_up(z.model, LANES) - z.model
        total = jnp.concatenate([total, jnp.zeros((8, short), F32)], axis=1)
        rows = [total[:, LANES * t : LANES * (t + 1)] for t in range(total.shape[1] // LANES)]
        packed[part.extra_at + 1] = jnp.concatenate(
            rows + [jnp.zeros((UNIT - 8 * len(rows), LANES), F32)] * (8 * len(rows) < UNIT), axis=0
        ).astype(BF16)

    return packed_call(
        "attend_gradients", z, part, section, device, sum(fields, []), [table], body,
        [pltpu.VMEM((count, z.recent, z.model), BF16)], tally(z, 0.4), lists,
    )


def half_selection(z, turned=False):
    shape = (HALVES * z.width, z.proj) if turned else (z.proj, HALVES * z.width)
    dense, split = iota(shape, int(turned)), iota(shape, int(not turned))
    within = split % z.width
    same = (split // z.width) * z.used + within == dense
    return jnp.where((within < z.used) & same, 1.0, 0.0).astype(BF16)


def unpack_call(name, z, part, device, arrays, shapes, body):
    number = len(arrays)
    places = 2 * part.pieces * len(part.orders)

    def kernel(place, *refs):
        sources, outs = refs[:number], refs[number:-2]
        buffer, sems = refs[-2:]
        copies = []
        for source, within, at, size in piece_places(part, place[0], place[0] & 1):
            copy = pltpu.make_async_copy(
                sources[source].at[pl.ds(within, size)], buffer.at[pl.ds(at, size)],
                sems.at[len(copies)],
            )
            copy.start()
            copies.append(copy)

        def block(matrix, tile, count):
            tiles = []
            for t in range(part.first[matrix] + tile, part.first[matrix] + tile + count):
                at = t * part.per_tile
                tiles.append(buffer[at : at + part.per_tile].reshape(part.rows, LANES))
            return jnp.concatenate(tiles, axis=1) if count > 1 else tiles[0]

        for copy in copies:
            copy.wait()
        body(block, buffer, *outs)

    return pl.pallas_call(
        kernel,
        in_specs=[pl.BlockSpec(memory_space=pltpu.SMEM)]
        + [pl.BlockSpec(memory_space=pl.ANY)] * number,
        out_shape=[jax.ShapeDtypeStruct(shape, F32) for shape in shapes],
        scratch_shapes=[
            pltpu.VMEM((part.units, UNIT, LANES), BF16), pltpu.SemaphoreType.DMA((places,))
        ],
        compiler_params=pltpu.CompilerParams(vmem_limit_bytes=VMEM_BYTES),
        cost_estimate=pl.CostEstimate(flops=tally(z, 0.2), bytes_accessed=1 << 23, transcendentals=0),
        name=name,
    )(device.reshape(1).astype(jnp.int32), *arrays)


def unpack_feed(z, part, device, arrays):
    def body(block, buffer, inner, outer, inner_bias):
        for number, out in ((0, inner), (1, outer)):
            for at in range(0, z.hidden, 512):
                stop = min(at + 512, z.hidden)
                value = block(number, at // LANES, -(-(stop - at) // LANES)).astype(F32)
                out[:, 0, at:stop] = value[: z.model, : stop - at]
        stacked = buffer[part.extra_at].astype(F32)
        tiles = round_up(z.hidden, LANES) // LANES
        line = jnp.concatenate([stacked[t : t + 1] for t in range(tiles)], axis=1)
        inner_bias[...] = line[:, : z.hidden]

    wide = (z.model, 1, z.hidden)
    inner, outer, inner_bias = unpack_call(
        "unpack_feed", z, part, device, arrays, (wide, wide, (1, z.hidden)), body
    )
    return jnp.transpose(inner, (1, 0, 2)), jnp.transpose(outer, (1, 2, 0)), inner_bias


def unpack_attend(z, part, device, arrays):
    def body(block, buffer, query, key_value, position, output, content_bias, position_bias, *rows):
        spread = half_selection(z)
        wide = HALVES * z.width // LANES
        query[:, 0, :] = dot_nt(block(0, 0, wide), spread)[: z.model]
        position[:, 0, :] = dot_nt(block(2, 0, wide), spread)[: z.model]
        output[:, 0, :] = dot_nt(spread, block(3, 0, wide))[:, : z.model]
        for side in range(2):
            value = dot_nt(block(1, side * wide, wide), spread)[: z.model]
            key_value[:, 0, side * z.proj : (side + 1) * z.proj] = value
        stacked = buffer[part.extra_at].astype(F32)
        sums = jnp.concatenate([stacked[8 * t : 8 * (t + 1)] for t in range(wide)], axis=1)
        sums = dot_nt(sums.astype(BF16), spread)
        content_bias[...] = sums[0:1]
        position_bias[...] = sums[1:2]
        stacked = buffer[part.extra_at + 1].astype(F32)
        tiles = round_up(z.model, LANES) // LANES
        sums = jnp.concatenate([stacked[8 * t : 8 * (t + 1)] for t in range(tiles)], axis=1)
        for k, out in enumerate(rows):
            out[...] = sums[k : k + 1, : z.model]

    square, row = (z.model, 1, z.proj), (1, z.model)
    shapes = (
        square, (z.model, 1, 2 * z.proj), square, (z.proj, 1, z.model), (1, z.proj), (1, z.proj),
        row, row, row, row, row,
    )
    results = unpack_call("unpack_attend", z, part, device, arrays, shapes, body)
    return [jnp.transpose(r, (1, 0, 2)) if r.ndim == 3 else r for r in results]


def frequencies(z):
    exponent = np.arange(0, z.model, 2).astype(np.float32) / np.float32(z.model)
    return np.power(np.float32(10000.0), -exponent).astype(np.float32)[:, None]


def prepare_call(z, query, key_value, position, output, biases, rows):
    farthest = z.keys - 1 + z.shift - z.seg + 1
    number = len(biases)

    def body(ins, items, outs):
        key_value, query, position, output = items[:4]
        vectors = items[4:]
        query_out, key_value_out, output_out, rel_out, table, lines = [out.ref for out in outs]
        lines[...] = jnp.zeros(lines.shape, F32)
        rate = ins[0]
        rest = iota((z.model // 2, LANES), 1).astype(F32)
        near = rate[...] * rest
        far = rate[...] * (farthest - LANES * rest)
        near_sin, near_cos = jnp.sin(near), jnp.cos(near)
        far_sin, far_cos = jnp.sin(far), jnp.cos(far)
        sines, cosines = [], []
        for t in range(z.tiles):
            a, b = far_sin[:, t : t + 1], far_cos[:, t : t + 1]
            sines.append(a * near_cos - b * near_sin)
            cosines.append(b * near_cos + a * near_sin)
        values = [jnp.concatenate(tiles, axis=1) for tiles in (sines, cosines)]
        table[...] = jnp.concatenate(values, axis=0).astype(BF16)
        outs[4].send()
        spread, gather = half_selection(z), half_selection(z, True)
        parts = [slice(half * z.width, (half + 1) * z.width) for half in range(HALVES)]
        for half, lanes in enumerate(parts):
            for side in range(2):
                own = key_value()[:, side * z.proj : (side + 1) * z.proj]
                key_value_out[side * HALVES + half] = dot_nt(gather[lanes, :], own).astype(BF16)
        outs[1].send()
        for half, lanes in enumerate(parts):
            query_out[half] = dot(query()[...], spread[:, lanes]).astype(BF16)
        outs[0].send()
        for half, lanes in enumerate(parts):
            wide = dot_nt(gather[lanes, :], position()[...]).astype(BF16)
            rel_out[half] = dot(wide, table[...]).astype(BF16)
        outs[3].send()
        for half, lanes in enumerate(parts):
            output_out[half] = dot(gather[lanes, :], output()[...]).astype(BF16)
        outs[2].send()
        for half, lanes in enumerate(parts):
            for k, source in enumerate(vectors[:number]):
                at = k * HALVES + half
                lines[at : at + 1, : z.width] = dot(source()[...], spread[:, lanes])
        for k, source in enumerate(vectors[number:]):
            at = number * HALVES + k
            lines[at : at + 1, : source().shape[1]] = source()[...].astype(F32)
        outs[5].send()

    shapes = [
        ((HALVES, z.model, z.width), BF16), ((2 * HALVES, z.width, z.model), BF16),
        ((HALVES, z.width, z.model), BF16), ((HALVES, z.width, z.cols), BF16),
        ((z.model, z.cols), BF16), ((Line.count, z.hidden), F32),
    ]
    arrays = [key_value, query, position, output, *biases, *rows]
    results = kernel_call(
        "prepare", body, [whole(jnp.asarray(frequencies(z)))], [(array, None) for array in arrays],
        shapes, [],
    )
    return [array[0] for array in results]


def unwritten(shapes):
    leaves, tree = jax.tree.flatten(shapes)
    if leaves:
        leaves = pl.pallas_call(
            lambda *refs: None,
            out_shape=leaves,
            out_specs=[pl.BlockSpec(memory_space=pl.ANY)] * len(leaves),
            name="unwritten",
        )()
    return jax.tree.unflatten(tree, leaves)


def moved_along(value, pairs):
    return lax.ppermute(value, "section", pairs)


def shards(
    stream_in, memories, cotangent, query_weight, key_value_matrix, position_weight,
    output_weight, bias_content, bias_position, attend_gain, attend_bias, inner_weight,
    inner_bias, outer_weight, outer_bias, feed_gain, feed_bias,
):
    count, seg_len, model = stream_in.shape
    z = Sizes(seg_len, memories.shape[2], model, query_weight.shape[2], inner_weight.shape[2])
    devices = lax.axis_size("dp")
    section, device = lax.axis_index("section"), lax.axis_index("dp")
    first = section == 0
    memory = jnp.transpose(memories[0], (0, 2, 1))
    made = prepare_call(
        z, query_weight[0], key_value_matrix[0], position_weight[0], output_weight[0],
        [bias_content, bias_position],
        [attend_gain, attend_bias, inner_bias, outer_bias, feed_gain, feed_bias],
    )
    table = made[4]
    weights = Weights(
        made[0], made[1], made[2], made[3], inner_weight[0], jnp.transpose(outer_weight[0]), made[5],
    )

    def shape_of(value):
        return jax.tree.map(lambda a: jax.ShapeDtypeStruct(a.shape, a.dtype), value)

    def pick(first_act, second_act, second_ahead=False):
        made = [jax.eval_shape(act) for act in (first_act, second_act)]

        def blank(side):
            return unwritten(shape_of(made[side][1]))

        def run_first():
            message, rest = first_act()
            if message is None:
                message = unwritten(shape_of(made[1][0]))
            return message, rest, blank(1)

        def run_second():
            message, rest = second_act()
            return message, blank(0), rest

        if second_ahead:
            return lax.cond(first, run_first, run_second)
        return lax.cond(jnp.logical_not(first), run_second, run_first)

    def forwarded(number):
        return (forward_zero, 0) if number == 0 else (forward_rest, number - 1)

    def feed_back(number):
        stored, slot = forwarded(number)
        return feed_back_call(z, weights, grads[number], stored[2], slot)

    def attend_back(number):
        back_first, feed = feeds[number]
        stored, slot = forwarded(number)
        return attend_back_call(z, weights, back_first, feed.attend, stored[1], slot)

    def both(number):
        made = both_call(z, weights, sent[number], 0, memory, cotangent, number)
        return made[1], (made[0],) + made[2:]

    forward_zero, forward_rest = forward_call(z, weights, stream_in, memory, 0, 1), None
    feeds, attends, both_made, grads = [], [], [], []
    sent = [moved_along(forward_zero[0], [(0, 1)])]
    for tick in range(1, count + 1):

        def first_act(tick=tick):
            if tick == 1:
                made = forward_call(z, weights, stream_in, memory, 1, count - 1)
                return made[0][:1], made
            message = forward_rest[0][tick - 1 : tick] if tick < count else None
            feeds.append(feed_back(tick - 2))
            made = feeds[-1], attend_back(tick - 2)
            feeds.pop()
            return message, made

        message, made, second = pick(first_act, lambda tick=tick: both(tick - 1))
        if tick == 1:
            forward_rest = made
        else:
            feeds.append(made[0])
            attends.append(made[1])
        both_made.append((second[0], message) + second[1:])
        came = moved_along(message, [(0, 1), (1, 0)] if tick < count else [(1, 0)])
        sent.append(came)
        grads.append(came)

    feed_part = Part(z, (z.hidden, z.hidden), 1, devices)
    wide = HALVES * z.width
    attend_part = Part(z, (wide, 2 * wide, wide, wide), 2, devices)
    fed = (
        [(stored[3], slot) for stored, slot in map(forwarded, range(count))],
        [(member[2], 0) for member in both_made],
    )
    def attend_back_there(number):
        return pick(lambda: ((), attend_back(number)), lambda: ((), ()))[1]

    final = count - 1
    feeds.append(pick(lambda: ((), feed_back(final)), lambda: ((), ()))[1])
    back_feed = (
        [(feed, 0) for _, feed in feeds], [(member[3], 0) for member in both_made]
    )
    feed_mine, feed_theirs = feed_gradients(z, feed_part, section, device, fed, back_feed)
    feed_chains = chains_of(feed_part, feed_mine, swapped_cores(feed_theirs))
    last = feed_chains[1]
    back_first, last.keep = lax.optimization_barrier((feeds[final][0], last.keep))
    feeds[final] = (back_first, feeds[final][1])
    attend = attend_back_there(final)
    last_grad, feed_chains[0].flying = lax.optimization_barrier(
        (attend[0], feed_chains[0].flying)
    )
    attends.append((last_grad, attend[1]))
    sources = (
        [(stream_in, i) for i in range(count)],
        [(sent[i], 0) for i in range(count)],
    )
    passes = [forwarded(i) for i in range(count)]
    layer_out = [((passes[i][0][0], passes[i][1]), (both_made[i][0], 0)) for i in range(count)]
    input_grad = [((attends[i][0], 0), (both_made[i][1], 0)) for i in range(count)]
    mine, theirs, outputs, input_grads = attend_gradients(
        z, attend_part, section, device, table, memory, sources, fed, back_feed,
        ([(member[1], 0) for member in attends], [(member[4], 0) for member in both_made]),
        (layer_out, input_grad),
    )
    came = swapped_cores(theirs)
    last = step_all(feed_chains, last)
    came[0], last.keep = lax.optimization_barrier((came[0], last.keep))
    attend_chains = chains_of(attend_part, mine, came)
    last = attend_chains[1]
    while feed_chains[0].spread >= 0:
        for pair in zip(feed_chains, attend_chains):
            last = step_all(pair, last)
    feed_arrays = finished(feed_chains)
    inner, outer, inner_bias_grad = unpack_feed(z, feed_part, device, feed_arrays)
    chain = attend_chains[0]
    chain.flying, inner_bias_grad = lax.optimization_barrier((chain.flying, inner_bias_grad))
    while chain.spread >= 0:
        last = step_all(attend_chains, last)
    attend_arrays = finished(attend_chains)
    (
        query, key_value, position, output, bias_c, bias_p, gain_a, bias_a, bias_o, gain_f, bias_f,
    ) = unpack_attend(z, attend_part, device, attend_arrays)
    return (
        outputs[None], input_grads[None], query, key_value, position, output, bias_c, bias_p,
        gain_a, bias_a, inner, inner_bias_grad, outer, bias_o, gain_f, bias_f,
    )


def solution(mesh):
    stacked, dp = P("section"), P("dp")
    both = P("section", "dp")
    return jax.shard_map(
        shards,
        mesh=mesh,
        in_specs=(dp, both, dp) + (stacked,) * 14,
        out_specs=(both, both) + (stacked,) * 14,
        check_vma=False,
    )
```
